128 devices in a mesh: seq: 16 (over y, z_hi, core), chan: 8 (over x, z_lo).
Axes of the slice: x: 4, y: 4, z: 4 (z_hi: 2, z_lo: 2; z = z_hi * 2 + z_lo), core: 2. Of those that a mesh axis runs over, the one named last changes fastest.
Arguments:
- activations: bfloat16 [16384, 8192], P('seq', 'chan'), may hold values from -6 to 6
- proj_weight: bfloat16 [8192, 3, 1024], P('chan'), may hold values from -0.0625 to 0.0625
- filter_taps: float32 [16384, 1024], P('seq', 'chan'), may hold values from -0.046875 to 0.046875
Outputs:
- mixed: float32 [16384, 1024], P('seq', 'chan')
The draws below stay inside these ranges and needn't reach their ends.
All inputs are finite; a program needn't handle non-finite values.
Results may differ from the reference program's by a relative error of at most 0.0003.
Values sent between devices are 32-bit elements; how exact they have to be, the bound alone decides.
No kernel may reach another device: no remote copies, remote signals or barrier semaphores. Data moves between devices by JAX's collectives and lax.ppermute only.
A program may use at most 128 MiB of HBM per device.

```python
import jax
import jax.numpy as jnp

D = 8192
LENGTH = 16384
CHANNELS = 1024


def steps_of(rng, extent, cuts, low, high):
    def one(position, shards_of):
        draws = jax.random.uniform(jax.random.fold_in(jax.random.fold_in(rng, 6), position), (shards_of,), jnp.float32, low / len(cuts), high / len(cuts))
        return jnp.repeat(jnp.exp(draws), extent[position] // shards_of).reshape((-1,) + (1,) * (len(extent) - position - 1))

    gain = one(*cuts[0])
    for cut in cuts[1:]:
        gain = gain * one(*cut)
    return gain


def bell_draw(stream_key, dims, scale, reach, pieces=(), kind=jnp.bfloat16):
    loudness = steps_of(stream_key, dims, pieces, -0.22, 0.18) if pieces else 1.0
    drawn = jax.random.normal(stream_key, dims, jnp.float32) * scale * loudness
    return jnp.minimum(jnp.maximum(drawn, -reach), reach).astype(kind)


def setup_inputs(seed: int = 0) -> dict:
    arg_keys = jax.random.split(jax.random.key(seed), 4)
    activations = bell_draw(arg_keys[0], (LENGTH, D), 1.0, 6.0, ((0, 16), (1, 8)))
    proj_weight = bell_draw(arg_keys[1], (D, 3, CHANNELS), D ** -0.5, 0.0625, ((0, 8),))
    filter_taps = bell_draw(arg_keys[2], (LENGTH, CHANNELS), LENGTH ** -0.5, 0.046875, ((0, 16), (1, 8)), jnp.float32)
    return {"activations": activations, "proj_weight": proj_weight, "filter_taps": filter_taps}


def reference(activations, proj_weight, filter_taps):
    flat_weight = proj_weight.reshape(D, 3 * CHANNELS)
    projected = jnp.dot(activations, flat_weight, preferred_element_type=jnp.float32).reshape(LENGTH, 3, CHANNELS)
    product_kv = projected[:, 1, :] * projected[:, 2, :]
    spectrum_kv = jnp.fft.fft(product_kv, n=2 * LENGTH, axis=0)
    spectrum_taps = jnp.fft.fft(filter_taps, n=2 * LENGTH, axis=0)
    convolved = jnp.real(jnp.fft.ifft(spectrum_kv * spectrum_taps, axis=0))[:LENGTH].astype(jnp.float32)
    return projected[:, 0, :] * convolved
```

```python
import functools

import jax
import jax.numpy as jnp
import ml_dtypes
import numpy as np
from jax import lax
from jax.experimental import pallas as pl
from jax.experimental.pallas import tpu as pltpu
from jax.sharding import PartitionSpec as P

BLOCK = 128
X_SIZE = 4
Z_FIRST_ROWS = 448
PARAMS = pltpu.CompilerParams(vmem_limit_bytes=40 * 1024 * 1024)


def shift_x(value, step):
    return lax.ppermute(value, "chan", [(i, (i + 2 * step) % 8) for i in range(8)])


def swap_z(value):
    return lax.ppermute(value, "chan", [(i, i ^ 1) for i in range(8)])


def project(activations, weight, start, width):
    columns = lax.dynamic_slice_in_dim(weight, start, width, axis=2)
    return jnp.einsum("td,djc->jtc", activations, columns, preferred_element_type=jnp.float32)


def as_halves(value):
    return value.reshape(2, -1, value.shape[-1])


def z_first(activations, weight):
    chan = lax.axis_index("chan")
    x_at, z_at = chan // 2, chan % 2

    def part(dx, dz):
        owner = (x_at + dx) % X_SIZE * 2 + (z_at + dz) % 2
        return as_halves(project(activations, weight, owner * BLOCK, BLOCK))

    far = part(2, 0) + swap_z(part(2, 1))
    from_left = shift_x(far[0], 1)
    from_right = shift_x(far[1], -1)
    right, got_right = part(1, 0), swap_z(part(1, 1))
    left, got_left = part(3, 0), swap_z(part(3, 1))
    right = jnp.stack([right[0] + got_right[0] + from_left, right[1] + got_right[1]])
    left = jnp.stack([left[0] + got_left[0], left[1] + got_left[1] + from_right])
    return part(0, 0), swap_z(part(0, 1)), shift_x(right, 1), shift_x(left, -1)


def x_first(activations, weight):
    chan = lax.axis_index("chan")
    x_at, z_at = chan // 2, chan % 2

    def part(dx):
        owner = (x_at + dx) % X_SIZE
        return as_halves(project(activations, weight, owner * 2 * BLOCK, 2 * BLOCK))

    def pick(value, dz):
        return lax.dynamic_slice_in_dim(value, (z_at + dz) % 2 * BLOCK, BLOCK, axis=-1)

    far = part(2)
    from_left = shift_x(far[0], 1)
    from_right = shift_x(far[1], -1)
    right, left, own = part(1), part(3), part(0)

    def second(dz):
        to_right, to_left = pick(right, dz), pick(left, dz)
        to_right = jnp.stack([to_right[0] + pick(from_left, dz), to_right[1]])
        to_left = jnp.stack([to_left[0], to_left[1] + pick(from_right, dz)])
        return shift_x(to_right, 1), shift_x(to_left, -1)

    a, b = second(1)
    other = swap_z(pick(own, 1) + a + b)
    c, d = second(0)
    return pick(own, 0), c, d, other


def split_bf16(table):
    high = table.astype(np.float32).astype(ml_dtypes.bfloat16)
    low = (table - high.astype(np.float64)).astype(ml_dtypes.bfloat16)
    return high, low


@functools.lru_cache(None)
def tables(length):
    rows = length // BLOCK
    period = 2 * length
    odd = np.arange(rows) + 0.5
    first = -2 * np.pi * np.outer(odd, np.arange(rows)) / (2 * rows)
    turn = -2 * np.pi * np.outer(odd, np.arange(BLOCK)) / period
    second = -2 * np.pi * (np.outer(np.arange(BLOCK), np.arange(BLOCK)) % BLOCK) / BLOCK
    c, s = np.cos(second), np.sin(second)
    scale = 1.0 / length
    return (
        split_bf16(np.concatenate([np.cos(first), np.sin(first)], axis=0)),
        (np.cos(turn).astype(np.float32), np.sin(turn).astype(np.float32)),
        split_bf16(np.block([[c, s], [-s, c]])),
        split_bf16(np.block([[c, -s], [s, c]])),
        split_bf16(np.concatenate([np.cos(first).T, np.sin(first).T], axis=1) * scale),
    )


def split_value(value):
    high = value.astype(jnp.bfloat16)
    return high, (value - high.astype(jnp.float32)).astype(jnp.bfloat16)


def dot3(left, right):
    dot = functools.partial(jnp.dot, preferred_element_type=jnp.float32)
    return dot(left[0], right[0]) + (dot(left[0], right[1]) + dot(left[1], right[0]))


def forward(signal_ref, first, turn, second):
    seqs, channels = signal_ref.shape[:2]
    rows = seqs * signal_ref.shape[2]
    signal = jnp.concatenate(
        [signal_ref[:, c].reshape(rows, BLOCK) for c in range(channels)], axis=1
    )
    part = dot3(first, split_value(signal))
    turned = []
    for c in range(channels):
        real = part[:rows, c * BLOCK : (c + 1) * BLOCK]
        imag = part[rows:, c * BLOCK : (c + 1) * BLOCK]
        turned.append(
            jnp.concatenate(
                [real * turn[0] - imag * turn[1], real * turn[1] + imag * turn[0]], axis=1
            )
        )
    return dot3(split_value(jnp.concatenate(turned, axis=0)), second)


def taps_kernel(taps_ref, f_hi, f_lo, t_re, t_im, s_hi, s_lo, out_ref):
    out_ref[...] = forward(
        taps_ref, (f_hi[...], f_lo[...]), (t_re[...], t_im[...]), (s_hi[...], s_lo[...])
    )


def conv_kernel(
    kv_ref, spec_ref, f_hi, f_lo, t_re, t_im, s_hi, s_lo, b_hi, b_lo, i_hi, i_lo, out_ref
):
    seqs, channels, blocks, _ = kv_ref.shape
    rows = seqs * blocks
    turn = (t_re[...], t_im[...])
    spectrum = forward(kv_ref, (f_hi[...], f_lo[...]), turn, (s_hi[...], s_lo[...]))
    real, imag = spectrum[:, :BLOCK], spectrum[:, BLOCK:]
    taps_real, taps_imag = spec_ref[:, :BLOCK], spec_ref[:, BLOCK:]
    product = jnp.concatenate(
        [real * taps_real - imag * taps_imag, real * taps_imag + imag * taps_real], axis=1
    )
    back = dot3(split_value(product), (b_hi[...], b_lo[...]))
    columns = []
    for c in range(channels):
        real = back[c * rows : (c + 1) * rows, :BLOCK]
        imag = back[c * rows : (c + 1) * rows, BLOCK:]
        columns.append(
            jnp.concatenate(
                [real * turn[0] + imag * turn[1], imag * turn[0] - real * turn[1]], axis=0
            )
        )
    result = dot3((i_hi[...], i_lo[...]), split_value(jnp.concatenate(columns, axis=1)))
    for c in range(channels):
        out_ref[:, c] = result[:, c * BLOCK : (c + 1) * BLOCK].reshape(seqs, blocks, BLOCK)


def turn_blocks(value_ref, out_ref):
    for b in range(out_ref.shape[1]):
        out_ref[:, b, :] = value_ref[b * BLOCK : (b + 1) * BLOCK, :].T


def taps_turn_kernel(taps_ref, out_ref):
    turn_blocks(taps_ref, out_ref)


def kv_kernel(z0, z1, z2, z3, x0, x1, x2, x3, out_ref, kv_ref):
    rows = z0.shape[1]
    total = (z0[...] + z1[...]) + (z2[...] + z3[...])
    kv_ref[:rows] = total[0] * total[1]
    total = (x0[...] + x1[...]) + (x2[...] + x3[...])
    kv_ref[rows:] = total[0] * total[1]
    turn_blocks(kv_ref, out_ref)


def gate_kernel(conv_ref, z0, z1, z2, z3, x0, x1, x2, x3, out_ref):
    for b in range(conv_ref.shape[1]):
        out_ref[b * BLOCK : (b + 1) * BLOCK, :] = conv_ref[:, b, :].T
    rows = 2 * z0.shape[1]
    total = (z0[...] + z1[...]) + (z2[...] + z3[...])
    out_ref[:rows] = out_ref[:rows] * total.reshape(rows, BLOCK)
    total = (x0[...] + x1[...]) + (x2[...] + x3[...])
    out_ref[rows:] = out_ref[rows:] * total.reshape(-1, BLOCK)


def call(kernel, out_shape, *operands, scratch=()):
    return pl.pallas_call(
        kernel,
        out_shape=jax.ShapeDtypeStruct(out_shape, jnp.float32),
        scratch_shapes=scratch,
        compiler_params=PARAMS,
    )(*operands)


def exchange(value):
    return lax.all_to_all(value, "seq", split_axis=0, concat_axis=0, tiled=True)


def on_device(activations, proj_weight, filter_taps):
    tokens, channels = filter_taps.shape
    seqs = lax.axis_size("seq")
    length = tokens * seqs
    blocks = tokens // BLOCK
    owned = channels // seqs
    turned_shape = (channels, blocks, BLOCK)
    moved_shape = (seqs, owned, blocks, BLOCK)
    first, turn, second, back, inverse = tables(length)

    low, high = activations[:Z_FIRST_ROWS], activations[Z_FIRST_ROWS:]
    kv_weight, q_weight = proj_weight[:, 1:], proj_weight[:, :1]
    kv_parts = z_first(low, kv_weight) + x_first(high, kv_weight)
    q_parts = z_first(low, q_weight) + x_first(high, q_weight)

    taps = call(taps_turn_kernel, turned_shape, filter_taps)
    taps = exchange(taps.reshape(moved_shape))
    spectrum = call(
        taps_kernel, (owned * length // BLOCK, 2 * BLOCK), taps, *first, *turn, *second
    )

    kv = call(
        kv_kernel, turned_shape, *kv_parts, scratch=[pltpu.VMEM((tokens, channels), jnp.float32)]
    )
    moved = exchange(kv.reshape(moved_shape))
    convolved = call(
        conv_kernel, moved_shape, moved, spectrum, *first, *turn, *second, *back, *inverse
    )
    home = exchange(convolved).reshape(turned_shape)
    return call(gate_kernel, (tokens, channels), home, *q_parts)


def solution(mesh):
    return jax.shard_map(
        on_device,
        mesh=mesh,
        in_specs=(P("seq", "chan"), P("chan", None, None), P("seq", "chan")),
        out_specs=P("seq", "chan"),
        check_vma=False,
    )
```

```python
import functools

import jax
import jax.numpy as jnp
import ml_dtypes
import numpy as np
from jax import lax
from jax.experimental import pallas as pl
from jax.experimental.pallas import tpu as pltpu
from jax.sharding import PartitionSpec as P

BLOCK = 128
X_SIZE = 4
Z_ROWS = 448
PARAMS = pltpu.CompilerParams(vmem_limit_bytes=40 * 1024 * 1024)


def shift_x(value, step):
    return lax.ppermute(value, "chan", [(i, (i + 2 * step) % 8) for i in range(8)])


def swap_z(value):
    return lax.ppermute(value, "chan", [(i, i ^ 1) for i in range(8)])


def parts_of(rows, weight_ref, z_at):
    product = jnp.dot(rows, weight_ref[0], preferred_element_type=jnp.float32)
    low, high = product[:, :BLOCK], product[:, BLOCK:]
    return jnp.where(z_at == 0, high, low), jnp.where(z_at == 0, low, high)


class Halves:
    def __init__(self, tokens, z_rows, columns):
        self.columns = columns
        parts = 2 // len(columns)
        self.z_rows = z_rows // parts
        self.x_rows = (tokens - z_rows) // parts
        self.z_start = [h % parts * self.z_rows for h in range(2)]
        self.x_start = [z_rows + h % parts * self.x_rows for h in range(2)]

    def x_part(self, act, weights, half, z_at):
        rows = act[self.x_start[half] : self.x_start[half] + self.x_rows]
        return parts_of(rows, weights[half % len(weights)], z_at)

    def z_part(self, act, weights, half, z_at):
        rows = act[self.z_start[half] : self.z_start[half] + self.z_rows]
        return parts_of(rows, weights[half % len(weights)], z_at)


def far_kernel(halves, place, act, weights, outs):
    send_r, send_l, z_other, z_mine = outs
    (far,) = weights
    for half, out in enumerate((send_r, send_l)):
        out[0], out[1] = halves.x_part(act, far, half, place[4])
        z_other[half], z_mine[half] = halves.z_part(act, far, half, place[4])


def near_kernel(halves, place, act, weights, outs):
    send_r, send_l, keep_r, keep_l, z_other, z_mine = outs
    right, left = weights
    send_r[0], send_r[1] = halves.x_part(act, right, 1, place[4])
    send_l[0], send_l[1] = halves.x_part(act, left, 0, place[4])
    z_other[0], z_mine[0] = halves.z_part(act, right, 0, place[4])
    z_other[1], z_mine[1] = halves.z_part(act, right, 1, place[4])
    z_other[2], z_mine[2] = halves.z_part(act, left, 0, place[4])
    keep_r[0], keep_r[1] = halves.x_part(act, right, 0, place[4])
    keep_l[0], keep_l[1] = halves.x_part(act, left, 1, place[4])


def own_kernel(halves, place, act, weights, outs):
    x_other, x_mine, z_other, z_mine = outs
    left, own = weights
    z_other[0], z_mine[0] = halves.z_part(act, left, 1, place[4])
    for half in range(2):
        z_other[1 + half], z_mine[1 + half] = halves.z_part(act, own, half, place[4])
        x_other[half], x_mine[half] = halves.x_part(act, own, half, place[4])


def project(kernel, halves, place, activations, weight, owners, outs, after=()):
    def spec(j, entry):
        return pl.BlockSpec((1, weight.shape[1], 2 * BLOCK), lambda i, at: (j, 0, at[entry]))

    def whole(shape):
        return pl.BlockSpec(shape, lambda i, at: (0,) * len(shape))

    blocks = [spec(j, entry) for entry in owners for j in halves.columns]
    per_owner = len(halves.columns)

    def body(at, act, *refs):
        weights = [
            refs[i * per_owner : (i + 1) * per_owner] for i in range(len(owners))
        ]
        kernel(halves, at, act, weights, refs[len(blocks) + len(after) :])

    return pl.pallas_call(
        body,
        grid_spec=pltpu.PrefetchScalarGridSpec(
            num_scalar_prefetch=1,
            grid=(1,),
            in_specs=[whole(activations.shape)]
            + blocks
            + [pl.BlockSpec(memory_space=pl.ANY)] * len(after),
            out_specs=[whole(shape) for shape in outs],
        ),
        out_shape=[jax.ShapeDtypeStruct(shape, jnp.float32) for shape in outs],
        compiler_params=PARAMS,
        name=kernel.__name__,
    )(place, activations, *[weight] * len(blocks), *after)


def first_sum_kernel(keep_r, got_r, keep_l, got_l, z_mine, z_got, out_r, out_l):
    rows = keep_r.shape[1]
    for half, (keep, got, out) in enumerate(((keep_r, got_r, out_r), (keep_l, got_l, out_l))):
        out[:rows] = keep[0] + got[0]
        out[rows : 2 * rows] = keep[1] + got[1]
        out[2 * rows :] = z_mine[half] + z_got[half]


def second_sum_kernel(
    z_near, z_near_got, z_own, z_own_got, x_own, dep_r, dep_l, near_r, near_l, out_r, out_l, out_x
):
    rows, x_rows = z_near.shape[1], x_own.shape[1]
    out_r[0] = z_near[0] + z_near_got[0] + dep_r[2 * x_rows : 2 * x_rows + rows]
    out_r[1] = z_near[1] + z_near_got[1]
    out_l[0] = z_near[2] + z_near_got[2]
    out_l[1] = z_own[0] + z_own_got[0] + dep_l[2 * x_rows : 2 * x_rows + rows]
    out_x[0] = x_own[0] + (dep_r[:x_rows] + near_l[0])
    out_x[1] = x_own[1] + (near_r[0] + dep_l[:x_rows])


def reduce_chunks(halves, place, activations, weight, after=(), beside=None):
    x_rows, z_rows = halves.x_rows, halves.z_rows
    x_pair, z_pair, z_three = (2, x_rows, BLOCK), (2, z_rows, BLOCK), (3, z_rows, BLOCK)
    make = functools.partial(
        project, halves=halves, place=place, activations=activations, weight=weight
    )
    far_r, far_l, z_far, z_far_mine = make(
        far_kernel, owners=[2], outs=[x_pair, x_pair, z_pair, z_pair], after=after
    )
    far_r, far_l, z_far = shift_x(far_r, 1), shift_x(far_l, -1), swap_z(z_far)
    near_r, near_l, keep_r, keep_l, z_near, z_near_mine = make(
        near_kernel,
        owners=[1, 3],
        outs=[x_pair, x_pair, x_pair, x_pair, z_three, z_three],
        after=(z_far_mine,),
    )
    near_r, near_l, z_near = shift_x(near_r, 1), shift_x(near_l, -1), swap_z(z_near)
    x_own, x_mine, z_own, z_mine = make(
        own_kernel, owners=[3, 0], outs=[x_pair, x_pair, z_three, z_three], after=(keep_r,)
    )
    dep_shape = (2 * x_rows + z_rows, BLOCK)
    dep_r, dep_l = call(
        first_sum_kernel,
        [dep_shape, dep_shape],
        keep_r,
        far_r,
        keep_l,
        far_l,
        z_far_mine,
        z_far,
        after=(near_r, near_l, z_near, x_own),
    )
    moved = (beside(dep_r),) if beside else ()
    dep_r, dep_l, z_own_got = shift_x(dep_r, 1), shift_x(dep_l, -1), swap_z(z_own)
    last_r, last_l, x_sum = call(
        second_sum_kernel,
        [z_pair, z_pair, x_pair],
        z_near_mine,
        z_near,
        z_mine,
        z_own_got,
        x_own,
        dep_r,
        dep_l,
        near_r,
        near_l,
        after=moved,
    )
    stage_three = last_r
    last_r, last_l, x_sum = shift_x(last_r, 1), shift_x(last_l, -1), swap_z(x_sum)
    parts = (z_mine, z_own_got, last_r, last_l, x_mine, dep_r, near_r, dep_l, near_l, x_sum)
    return parts, moved, stage_three


def summed(z_own, z_got, z_r, z_l, x_own, dep_r, near_r, dep_l, near_l, x_got):
    rows = x_own.shape[1]
    z_total = [(z_own[1 + h] + z_got[1 + h]) + (z_r[h] + z_l[h]) for h in range(2)]
    x_total = [
        x_own[0] + (dep_r[rows : 2 * rows] + near_l[1]) + x_got[0],
        x_own[1] + (near_r[1] + dep_l[rows : 2 * rows]) + x_got[1],
    ]
    return z_total, x_total


def split_bf16(table):
    high = table.astype(np.float32).astype(ml_dtypes.bfloat16)
    low = (table - high.astype(np.float64)).astype(ml_dtypes.bfloat16)
    return high, low


@functools.lru_cache(None)
def tables(length):
    rows = length // BLOCK
    period = 2 * length
    odd = np.arange(rows) + 0.5
    first = -2 * np.pi * np.outer(odd, np.arange(rows)) / (2 * rows)
    turn = -2 * np.pi * np.outer(odd, np.arange(BLOCK)) / period
    second = -2 * np.pi * (np.outer(np.arange(BLOCK), np.arange(BLOCK)) % BLOCK) / BLOCK
    c, s = np.cos(second), np.sin(second)
    scale = 1.0 / length
    return (
        split_bf16(np.concatenate([np.cos(first), np.sin(first)], axis=0)),
        (np.cos(turn).astype(np.float32), np.sin(turn).astype(np.float32)),
        split_bf16(np.block([[c, s], [-s, c]])),
        split_bf16(np.block([[c, -s], [s, c]])),
        split_bf16(np.concatenate([np.cos(first).T, np.sin(first).T], axis=1) * scale),
    )


def split_value(value):
    high = value.astype(jnp.bfloat16)
    return high, (value - high.astype(jnp.float32)).astype(jnp.bfloat16)


def dot3(left, right):
    dot = functools.partial(jnp.dot, preferred_element_type=jnp.float32)
    return dot(left[0], right[0]) + (dot(left[0], right[1]) + dot(left[1], right[0]))


def forward(signal_ref, first, turn, second):
    seqs, channels = signal_ref.shape[:2]
    rows = seqs * signal_ref.shape[2]
    signal = jnp.concatenate(
        [signal_ref[:, c].reshape(rows, BLOCK) for c in range(channels)], axis=1
    )
    part = dot3(first, split_value(signal))
    turned = []
    for c in range(channels):
        real = part[:rows, c * BLOCK : (c + 1) * BLOCK]
        imag = part[rows:, c * BLOCK : (c + 1) * BLOCK]
        turned.append(
            jnp.concatenate(
                [real * turn[0] - imag * turn[1], real * turn[1] + imag * turn[0]], axis=1
            )
        )
    return dot3(split_value(jnp.concatenate(turned, axis=0)), second)


def taps_kernel(taps_ref, f_hi, f_lo, t_re, t_im, s_hi, s_lo, out_ref):
    out_ref[...] = forward(
        taps_ref, (f_hi[...], f_lo[...]), (t_re[...], t_im[...]), (s_hi[...], s_lo[...])
    )


def conv_kernel(
    kv_ref, spec_ref, f_hi, f_lo, t_re, t_im, s_hi, s_lo, b_hi, b_lo, i_hi, i_lo, out_ref
):
    seqs, channels, blocks, _ = kv_ref.shape
    rows = seqs * blocks
    turn = (t_re[...], t_im[...])
    spectrum = forward(kv_ref, (f_hi[...], f_lo[...]), turn, (s_hi[...], s_lo[...]))
    real, imag = spectrum[:, :BLOCK], spectrum[:, BLOCK:]
    taps_real, taps_imag = spec_ref[:, :BLOCK], spec_ref[:, BLOCK:]
    product = jnp.concatenate(
        [real * taps_real - imag * taps_imag, real * taps_imag + imag * taps_real], axis=1
    )
    back = dot3(split_value(product), (b_hi[...], b_lo[...]))
    columns = []
    for c in range(channels):
        real = back[c * rows : (c + 1) * rows, :BLOCK]
        imag = back[c * rows : (c + 1) * rows, BLOCK:]
        columns.append(
            jnp.concatenate(
                [real * turn[0] + imag * turn[1], imag * turn[0] - real * turn[1]], axis=0
            )
        )
    result = dot3((i_hi[...], i_lo[...]), split_value(jnp.concatenate(columns, axis=1)))
    for c in range(channels):
        out_ref[:, c] = result[:, c * BLOCK : (c + 1) * BLOCK].reshape(seqs, blocks, BLOCK)


def turn_blocks(value_ref, out_ref):
    for b in range(out_ref.shape[1]):
        out_ref[:, b, :] = value_ref[b * BLOCK : (b + 1) * BLOCK, :].T


def taps_turn_kernel(taps_ref, out_ref):
    turn_blocks(taps_ref, out_ref)


def kv_kernel(*refs):
    parts, out_ref, kv_ref = refs[:-2], refs[-2], refs[-1]
    z_total, x_total = summed(*parts)
    rows = z_total[0].shape[0]
    kv_ref[:rows] = z_total[0] * z_total[1]
    kv_ref[rows:] = x_total[0] * x_total[1]
    turn_blocks(kv_ref, out_ref)


def gate_kernel(conv_ref, *refs):
    parts, out_ref = refs[:-1], refs[-1]
    for b in range(conv_ref.shape[1]):
        out_ref[b * BLOCK : (b + 1) * BLOCK, :] = conv_ref[:, b, :].T
    z_total, x_total = summed(*parts)
    start = 0
    for query in z_total + x_total:
        end = start + query.shape[0]
        out_ref[start:end] = out_ref[start:end] * query
        start = end


def call(kernel, out_shapes, *operands, after=(), scratch=()):
    single = not isinstance(out_shapes, list)
    shapes = [out_shapes] if single else out_shapes

    def body(*refs):
        kernel(*refs[: len(operands)], *refs[len(operands) + len(after) :])

    result = pl.pallas_call(
        body,
        in_specs=[pl.BlockSpec(memory_space=pltpu.VMEM)] * len(operands)
        + [pl.BlockSpec(memory_space=pl.ANY)] * len(after),
        out_shape=[jax.ShapeDtypeStruct(shape, jnp.float32) for shape in shapes],
        scratch_shapes=scratch,
        compiler_params=PARAMS,
        name=kernel.__name__,
    )(*operands, *after)
    return result[0] if single else result


def exchange(value):
    return lax.all_to_all(value, "seq", split_axis=0, concat_axis=0, tiled=True)


def on_device(activations, proj_weight, filter_taps):
    tokens, channels = filter_taps.shape
    seqs = lax.axis_size("seq")
    length = tokens * seqs
    blocks = tokens // BLOCK
    owned = channels // seqs
    turned_shape = (channels, blocks, BLOCK)
    moved_shape = (seqs, owned, blocks, BLOCK)
    first, turn, second, back, inverse = tables(length)

    chan = lax.axis_index("chan")
    x_at, z_at = chan // 2, chan % 2
    place = jnp.stack([(x_at + dx) % X_SIZE for dx in range(X_SIZE)] + [z_at]).astype(jnp.int32)
    weight = jnp.transpose(proj_weight, (1, 0, 2))
    def move_taps(ready):
        turned = call(taps_turn_kernel, turned_shape, filter_taps, after=(ready,))
        return exchange(turned.reshape(moved_shape))

    kv_parts, (taps,), kv_last = reduce_chunks(
        Halves(tokens, Z_ROWS, (1, 2)), place, activations, weight, beside=move_taps
    )
    q_parts, _, _ = reduce_chunks(
        Halves(tokens, Z_ROWS, (0,)), place, activations, weight, after=(kv_last,)
    )

    spectrum = call(
        taps_kernel, (owned * length // BLOCK, 2 * BLOCK), taps, *first, *turn, *second
    )

    kv = call(
        kv_kernel,
        turned_shape,
        *kv_parts,
        after=(spectrum,),
        scratch=[pltpu.VMEM((tokens, channels), jnp.float32)],
    )
    moved = exchange(kv.reshape(moved_shape))
    convolved = call(
        conv_kernel, moved_shape, moved, spectrum, *first, *turn, *second, *back, *inverse
    )
    home = exchange(convolved).reshape(turned_shape)
    return call(gate_kernel, (tokens, channels), home, *q_parts)


def solution(mesh):
    return jax.shard_map(
        on_device,
        mesh=mesh,
        in_specs=(P("seq", "chan"), P("chan", None, None), P("seq", "chan")),
        out_specs=P("seq", "chan"),
        check_vma=False,
    )
```

```python
import functools

import jax
import jax.numpy as jnp
import ml_dtypes
import numpy as np
from jax import lax
from jax.experimental import pallas as pl
from jax.experimental.pallas import tpu as pltpu
from jax.sharding import PartitionSpec as P

BLOCK = 128
X_SIZE = 4


def params(mebibytes):
    return pltpu.CompilerParams(vmem_limit_bytes=mebibytes * 1024 * 1024)


def in_hbm(value):
    return pltpu.with_memory_space_constraint(value, pltpu.HBM)


def shift_x(value, step):
    return lax.ppermute(value, "chan", [(i, (i + 2 * step) % 8) for i in range(8)])


def swap_z(value):
    return lax.ppermute(value, "chan", [(i, i ^ 1) for i in range(8)])


def parts_of(rows, weight_ref, z_at):
    product = jnp.dot(rows, weight_ref[0], preferred_element_type=jnp.float32)
    low, high = product[:, :BLOCK], product[:, BLOCK:]
    return jnp.where(z_at == 0, high, low), jnp.where(z_at == 0, low, high)


class Halves:
    def __init__(self, tokens, columns):
        self.columns = columns
        parts = 2 // len(columns)
        self.rows = tokens // 2 // parts
        self.z_start = [h % parts * self.rows for h in range(2)]
        self.x_start = [tokens // 2 + start for start in self.z_start]

    def x_part(self, act, weights, half, z_at):
        rows = act[self.x_start[half] : self.x_start[half] + self.rows]
        return parts_of(rows, weights[half % len(weights)], z_at)

    def z_part(self, act, weights, half, z_at):
        rows = act[self.z_start[half] : self.z_start[half] + self.rows]
        return parts_of(rows, weights[half % len(weights)], z_at)


def far_near_kernel(halves, place, act, weights, outs):
    send_r, send_l, keep_r, keep_l, z_other, z_mine = outs
    z_at = place[4]
    step = pl.program_id(0)

    @pl.when(step == 0)
    def _():
        send_r[0], send_r[1] = halves.x_part(act, weights, 0, z_at)
        send_l[0], send_l[1] = halves.x_part(act, weights, 1, z_at)
        z_other[3], z_mine[3] = halves.z_part(act, weights, 0, z_at)
        z_other[4], z_mine[4] = halves.z_part(act, weights, 1, z_at)

    @pl.when(step == 1)
    def _():
        send_r[2], send_r[3] = halves.x_part(act, weights, 1, z_at)
        z_other[0], z_mine[0] = halves.z_part(act, weights, 0, z_at)
        z_other[1], z_mine[1] = halves.z_part(act, weights, 1, z_at)
        keep_r[0], keep_r[1] = halves.x_part(act, weights, 0, z_at)

    @pl.when(step == 2)
    def _():
        send_l[2], send_l[3] = halves.x_part(act, weights, 0, z_at)
        z_other[2], z_mine[2] = halves.z_part(act, weights, 0, z_at)
        keep_l[0], keep_l[1] = halves.x_part(act, weights, 1, z_at)


def left_own_kernel(halves, place, act, weights, outs):
    x_other, x_mine, z_other, z_mine = outs
    z_at = place[4]
    step = pl.program_id(0)

    @pl.when(step == 0)
    def _():
        z_other[2], z_mine[2] = halves.z_part(act, weights, 1, z_at)

    @pl.when(step == 1)
    def _():
        for half in range(2):
            z_other[half], z_mine[half] = halves.z_part(act, weights, half, z_at)
            x_other[half], x_mine[half] = halves.x_part(act, weights, half, z_at)


def project(kernel, halves, place, activations, weight, owner, steps, outs, after=()):
    def spec(j):
        return pl.BlockSpec(
            (1, weight.shape[1], 2 * BLOCK), lambda i, at: (j, 0, at[owner + i])
        )

    count = len(halves.columns)

    def body(at, act, *refs):
        kernel(halves, at, act, refs[:count], refs[count + len(after) :])

    return pl.pallas_call(
        body,
        grid_spec=pltpu.PrefetchScalarGridSpec(
            num_scalar_prefetch=1,
            grid=(steps,),
            in_specs=[pl.BlockSpec(activations.shape, lambda i, at: (0, 0))]
            + [spec(j) for j in halves.columns]
            + [pl.BlockSpec(memory_space=pl.ANY)] * len(after),
            out_specs=[pl.BlockSpec(memory_space=pltpu.VMEM)] * len(outs),
        ),
        out_shape=[jax.ShapeDtypeStruct(shape, jnp.float32) for shape in outs],
        compiler_params=params(24),
        name=kernel.__name__,
    )(place, activations, *[weight] * count, *after)


def first_sum_kernel(keep_r, got_r, keep_l, got_l, z_mine, z_got, out_r, out_l):
    for half, (keep, got, out) in enumerate(((keep_r, got_r, out_r), (keep_l, got_l, out_l))):
        out[0] = keep[0] + got[0]
        out[1] = keep[1] + got[1]
        out[2] = z_mine[3 + half] + z_got[3 + half]


def second_sum_kernel(
    z_near, z_near_got, z_own, z_own_got, x_own, dep_r, dep_l, got_r, got_l, out_r, out_l, out_x
):
    out_r[0] = z_near[0] + z_near_got[0] + dep_r[2]
    out_r[1] = z_near[1] + z_near_got[1]
    out_l[0] = z_near[2] + z_near_got[2]
    out_l[1] = z_own[2] + z_own_got[2] + dep_l[2]
    out_x[0] = x_own[0] + (dep_r[0] + got_l[2])
    out_x[1] = x_own[1] + (got_r[2] + dep_l[0])


def reduce_chunks(halves, place, activations, weight, after=(), beside=None):
    def pieces(count):
        return (count, halves.rows, BLOCK)

    send_r, send_l, keep_r, keep_l, z_near, z_near_mine = project(
        far_near_kernel,
        halves,
        place,
        activations,
        weight,
        0,
        3,
        [pieces(4), pieces(4), pieces(2), pieces(2), pieces(5), pieces(5)],
        after=after,
    )
    got_r, got_l, z_near = shift_x(send_r, 1), shift_x(send_l, -1), swap_z(z_near)
    x_own, x_mine, z_own, z_mine = project(
        left_own_kernel,
        halves,
        place,
        activations,
        weight,
        2,
        2,
        [pieces(2), pieces(2), pieces(3), pieces(3)],
        after=(keep_r,),
    )
    dep_r, dep_l = call(
        first_sum_kernel,
        [pieces(3), pieces(3)],
        keep_r,
        got_r,
        keep_l,
        got_l,
        z_near_mine,
        z_near,
        after=(x_own,),
    )
    moved = (beside(dep_r),) if beside else ()
    dep_r, dep_l, z_own = shift_x(dep_r, 1), shift_x(dep_l, -1), swap_z(z_own)
    last_r, last_l, x_sum = call(
        second_sum_kernel,
        [pieces(2), pieces(2), pieces(2)],
        z_near_mine,
        z_near,
        z_mine,
        z_own,
        x_own,
        dep_r,
        dep_l,
        got_r,
        got_l,
        after=moved,
    )
    last = last_r
    last_r, last_l, x_sum = shift_x(last_r, 1), shift_x(last_l, -1), swap_z(x_sum)
    return (z_mine, z_own, last_r, last_l, x_mine, dep_r, got_r, dep_l, got_l, x_sum), moved, last


def summed(z_own, z_got, z_r, z_l, x_own, dep_r, got_r, dep_l, got_l, x_got):
    return [(z_own[h] + z_got[h]) + (z_r[h] + z_l[h]) for h in range(2)], [
        x_own[0] + (dep_r[1] + got_l[3]) + x_got[0],
        x_own[1] + (got_r[3] + dep_l[1]) + x_got[1],
    ]


def split_bf16(table):
    high = table.astype(np.float32).astype(ml_dtypes.bfloat16)
    low = (table - high.astype(np.float64)).astype(ml_dtypes.bfloat16)
    return high, low


@functools.lru_cache(None)
def tables(length):
    rows = length // BLOCK
    period = 2 * length
    odd = np.arange(rows) + 0.5
    first = -2 * np.pi * np.outer(odd, np.arange(rows)) / (2 * rows)
    turn = -2 * np.pi * np.outer(odd, np.arange(BLOCK)) / period
    second = -2 * np.pi * (np.outer(np.arange(BLOCK), np.arange(BLOCK)) % BLOCK) / BLOCK
    c, s = np.cos(second), np.sin(second)
    scale = 1.0 / length
    return (
        split_bf16(np.concatenate([np.cos(first), np.sin(first)], axis=0)),
        (np.cos(turn).astype(np.float32), np.sin(turn).astype(np.float32)),
        split_bf16(np.block([[c, s], [-s, c]])),
        split_bf16(np.block([[c, -s], [s, c]])),
        split_bf16(np.concatenate([np.cos(first).T, np.sin(first).T], axis=1) * scale),
    )


def split_value(value):
    high = value.astype(jnp.bfloat16)
    return high, (value - high.astype(jnp.float32)).astype(jnp.bfloat16)


def dot3(left, right):
    dot = functools.partial(jnp.dot, preferred_element_type=jnp.float32)
    return dot(left[0], right[0]) + (dot(left[0], right[1]) + dot(left[1], right[0]))


def forward(signal_ref, first, turn, second):
    seqs, channels = signal_ref.shape[:2]
    rows = seqs * signal_ref.shape[2]
    signal = jnp.concatenate(
        [signal_ref[:, c].reshape(rows, BLOCK) for c in range(channels)], axis=1
    )
    part = dot3(first, split_value(signal))
    turned = []
    for c in range(channels):
        real = part[:rows, c * BLOCK : (c + 1) * BLOCK]
        imag = part[rows:, c * BLOCK : (c + 1) * BLOCK]
        turned.append(
            jnp.concatenate(
                [real * turn[0] - imag * turn[1], real * turn[1] + imag * turn[0]], axis=1
            )
        )
    return dot3(split_value(jnp.concatenate(turned, axis=0)), second)


def taps_kernel(taps_ref, f_hi, f_lo, t_re, t_im, s_hi, s_lo, out_ref):
    out_ref[...] = forward(
        taps_ref, (f_hi[...], f_lo[...]), (t_re[...], t_im[...]), (s_hi[...], s_lo[...])
    )


def conv_kernel(
    kv_ref, spec_ref, f_hi, f_lo, t_re, t_im, s_hi, s_lo, b_hi, b_lo, i_hi, i_lo, out_ref
):
    seqs, channels, blocks, _ = kv_ref.shape
    rows = seqs * blocks
    turn = (t_re[...], t_im[...])
    spectrum = forward(kv_ref, (f_hi[...], f_lo[...]), turn, (s_hi[...], s_lo[...]))
    real, imag = spectrum[:, :BLOCK], spectrum[:, BLOCK:]
    taps_real, taps_imag = spec_ref[:, :BLOCK], spec_ref[:, BLOCK:]
    product = jnp.concatenate(
        [real * taps_real - imag * taps_imag, real * taps_imag + imag * taps_real], axis=1
    )
    back = dot3(split_value(product), (b_hi[...], b_lo[...]))
    columns = []
    for c in range(channels):
        real = back[c * rows : (c + 1) * rows, :BLOCK]
        imag = back[c * rows : (c + 1) * rows, BLOCK:]
        columns.append(
            jnp.concatenate(
                [real * turn[0] + imag * turn[1], imag * turn[0] - real * turn[1]], axis=0
            )
        )
    result = dot3((i_hi[...], i_lo[...]), split_value(jnp.concatenate(columns, axis=1)))
    for c in range(channels):
        out_ref[:, c] = result[:, c * BLOCK : (c + 1) * BLOCK].reshape(seqs, blocks, BLOCK)


def turn_blocks(value_ref, out_ref):
    for b in range(out_ref.shape[1]):
        out_ref[:, b, :] = value_ref[b * BLOCK : (b + 1) * BLOCK, :].T


def taps_turn_kernel(taps_ref, out_ref):
    turn_blocks(taps_ref, out_ref)


def kv_kernel(*refs):
    parts, out_ref, kv_ref = refs[:-2], refs[-2], refs[-1]
    z_total, x_total = summed(*parts)
    rows = z_total[0].shape[0]
    kv_ref[:rows] = z_total[0] * z_total[1]
    kv_ref[rows:] = x_total[0] * x_total[1]
    turn_blocks(kv_ref, out_ref)


def gate_kernel(conv_ref, *refs):
    parts, out_ref = refs[:-1], refs[-1]
    for b in range(conv_ref.shape[1]):
        out_ref[b * BLOCK : (b + 1) * BLOCK, :] = conv_ref[:, b, :].T
    z_total, x_total = summed(*parts)
    start = 0
    for query in z_total + x_total:
        end = start + query.shape[0]
        out_ref[start:end] = out_ref[start:end] * query
        start = end


def call(kernel, out_shapes, *operands, after=(), scratch=(), tables=()):
    single = not isinstance(out_shapes, list)
    shapes = [out_shapes] if single else out_shapes

    def body(*refs):
        count = len(operands) + len(tables)
        kernel(*refs[:count], *refs[count + len(after) :])

    def whole(shape):
        return pl.BlockSpec(shape, lambda i: (0,) * len(shape))

    result = pl.pallas_call(
        body,
        grid=(1,),
        in_specs=[pl.BlockSpec(memory_space=pltpu.VMEM)] * len(operands)
        + [whole(table.shape) for table in tables]
        + [pl.BlockSpec(memory_space=pl.ANY)] * len(after),
        out_specs=[pl.BlockSpec(memory_space=pltpu.VMEM)] * len(shapes),
        out_shape=[jax.ShapeDtypeStruct(shape, jnp.float32) for shape in shapes],
        scratch_shapes=scratch,
        compiler_params=params(24),
        name=kernel.__name__,
    )(*operands, *[in_hbm(jnp.asarray(table)) for table in tables], *after)
    return result[0] if single else result


def exchange(value):
    return lax.all_to_all(value, "seq", split_axis=0, concat_axis=0, tiled=True)


def on_device(activations, proj_weight, filter_taps):
    tokens, channels = filter_taps.shape
    seqs = lax.axis_size("seq")
    length = tokens * seqs
    blocks = tokens // BLOCK
    owned = channels // seqs
    turned_shape = (channels, blocks, BLOCK)
    moved_shape = (seqs, owned, blocks, BLOCK)
    first, turn, second, back, inverse = tables(length)

    chan = lax.axis_index("chan")
    x_at, z_at = chan // 2, chan % 2
    owners = [(x_at + dx) % X_SIZE for dx in (2, 1, 3, 0)]
    place = jnp.stack(owners + [z_at]).astype(jnp.int32)
    weight = in_hbm(jnp.transpose(proj_weight, (1, 0, 2)))
    activations = in_hbm(activations)

    def move_taps(ready):
        turned = call(taps_turn_kernel, turned_shape, filter_taps, after=(ready,))
        return exchange(turned.reshape(moved_shape))

    kv_parts, (taps,), kv_last = reduce_chunks(
        Halves(tokens, (1, 2)), place, activations, weight, beside=move_taps
    )
    q_parts, _, _ = reduce_chunks(
        Halves(tokens, (0,)), place, activations, weight, after=(kv_last,)
    )

    spectrum = call(
        taps_kernel,
        (owned * length // BLOCK, 2 * BLOCK),
        taps,
        tables=first + turn + second,
    )

    kv = call(
        kv_kernel,
        turned_shape,
        *kv_parts,
        after=(spectrum,),
        scratch=[pltpu.VMEM((tokens, channels), jnp.float32)],
    )
    moved = exchange(kv.reshape(moved_shape))
    convolved = call(
        conv_kernel,
        moved_shape,
        moved,
        spectrum,
        tables=first + turn + second + back + inverse,
    )
    home = exchange(convolved).reshape(turned_shape)
    return call(gate_kernel, (tokens, channels), home, *q_parts)


def solution(mesh):
    return jax.shard_map(
        on_device,
        mesh=mesh,
        in_specs=(P("seq", "chan"), P("chan", None, None), P("seq", "chan")),
        out_specs=P("seq", "chan"),
        check_vma=False,
    )
```

```python
import functools

import jax
import jax.numpy as jnp
import ml_dtypes
import numpy as np
from jax import lax
from jax.experimental import pallas as pl
from jax.experimental.pallas import tpu as pltpu
from jax.sharding import PartitionSpec as P

BLOCK = 128
X_SIZE = 4


def params(mebibytes):
    return pltpu.CompilerParams(vmem_limit_bytes=mebibytes * 1024 * 1024)


def in_hbm(value):
    return pltpu.with_memory_space_constraint(value, pltpu.HBM)


def shift_x(value, step):
    return lax.ppermute(value, "chan", [(i, (i + 2 * step) % 8) for i in range(8)])


def swap_z(value):
    return lax.ppermute(value, "chan", [(i, i ^ 1) for i in range(8)])


def parts_of(rows, weight_ref, z_at):
    product = jnp.dot(rows, weight_ref[0], preferred_element_type=jnp.float32)
    low, high = product[:, :BLOCK], product[:, BLOCK:]
    return jnp.where(z_at == 0, high, low), jnp.where(z_at == 0, low, high)


class Halves:
    def __init__(self, tokens, columns):
        self.columns = columns
        parts = 2 // len(columns)
        self.rows = tokens // 2 // parts
        self.z_start = [h % parts * self.rows for h in range(2)]
        self.x_start = [tokens // 2 + start for start in self.z_start]

    def fill(self, place, act, weights, wanted):
        for j in range(len(weights)):
            mine = [w for w in wanted if len(weights) == 1 or w[0] == j]
            starts = [(self.z_start if z_first else self.x_start)[h] for h, z_first, _, _ in mine]
            if not mine:
                continue
            low, high = min(starts), max(starts) + self.rows
            other, own = parts_of(act[low:high], weights[j], place[4])
            for start, (_, _, put_other, put_mine) in zip(starts, mine):
                rows = slice(start - low, start - low + self.rows)
                put_other[0][put_other[1]] = other[rows]
                if put_mine is not None:
                    put_mine[0][put_mine[1]] = own[rows]


X, Z = False, True


def first_kernel(halves, place, act, weights, outs):
    send_r, send_l, z_other, z_mine = outs
    steps = (
        [
            (0, X, (send_r, 0), (send_r, 1)),
            (1, X, (send_l, 0), (send_l, 1)),
            (0, Z, (z_other, 0), (z_mine, 0)),
            (1, Z, (z_other, 1), (z_mine, 1)),
        ],
        [
            (1, X, (send_r, 2), (send_r, 3)),
            (0, Z, (z_other, 2), (z_mine, 2)),
            (1, Z, (z_other, 3), (z_mine, 3)),
        ],
        [(0, X, (send_l, 2), (send_l, 3))],
    )
    run_steps(halves, place, act, weights, steps)


def second_kernel(halves, place, act, weights, outs):
    keep_r, keep_l, z_other, z_mine, x_other, x_mine = outs
    steps = (
        [(0, X, (keep_r, 0), (keep_r, 1))],
        [
            (1, X, (keep_l, 0), (keep_l, 1)),
            (0, Z, (z_other, 0), (z_mine, 0)),
            (1, Z, (z_other, 1), (z_mine, 1)),
        ],
        [
            (0, X, (x_other, 0), (x_mine, 0)),
            (1, X, (x_other, 1), (x_mine, 1)),
            (0, Z, (z_other, 2), (z_mine, 2)),
            (1, Z, (z_other, 3), (z_mine, 3)),
        ],
    )
    run_steps(halves, place, act, weights, steps)


def run_steps(halves, place, act, weights, steps):
    for i, wanted in enumerate(steps):
        pl.when(pl.program_id(0) == i)(
            functools.partial(halves.fill, place, act, weights, wanted)
        )


def project(kernel, halves, place, activations, weight, owner, steps, outs, after=()):
    def spec(j):
        return pl.BlockSpec(
            (1, weight.shape[1], 2 * BLOCK), lambda i, at: (j, 0, at[owner + i])
        )

    count = len(halves.columns)

    def body(at, act, *refs):
        kernel(halves, at, act, refs[:count], refs[count + len(after) :])

    return pl.pallas_call(
        body,
        grid_spec=pltpu.PrefetchScalarGridSpec(
            num_scalar_prefetch=1,
            grid=(steps,),
            in_specs=[pl.BlockSpec(activations.shape, lambda i, at: (0, 0))]
            + [spec(j) for j in halves.columns]
            + [pl.BlockSpec(memory_space=pl.ANY)] * len(after),
            out_specs=[pl.BlockSpec(memory_space=pltpu.VMEM)] * len(outs),
        ),
        out_shape=[
            jax.ShapeDtypeStruct((count, halves.rows, BLOCK), jnp.float32) for count in outs
        ],
        compiler_params=params(24),
        name=kernel.__name__,
    )(place, activations, *[weight] * count, *after)


def first_sum_kernel(keep_r, got_r, keep_l, got_l, z_mine, z_got, out_r, out_l):
    for half, (keep, got, out) in enumerate(((keep_r, got_r, out_r), (keep_l, got_l, out_l))):
        out[0] = keep[0] + got[0]
        out[1] = keep[1] + got[1]
        out[2] = z_mine[half] + z_got[half]


def beside_two_kernel(z_mine, z_got, x_other, x_mine, got_r, got_l, out_z, out_other, out_mine):
    for half in range(2):
        out_z[half] = z_mine[2 + half] + z_got[2 + half]
    for half, got in enumerate((got_l, got_r)):
        out_other[half] = x_other[half] + got[2]
        out_mine[half] = x_mine[half] + got[3]


def second_sum_kernel(z_part, z_mine, z_got, x_part, dep_r, dep_l, out_r, out_l, out_x):
    out_r[0] = z_part[0] + dep_r[2]
    out_r[1] = z_part[1]
    out_l[0] = z_mine[0] + z_got[0]
    out_l[1] = z_mine[1] + z_got[1] + dep_l[2]
    out_x[0] = x_part[0] + dep_r[0]
    out_x[1] = x_part[1] + dep_l[0]


def beside_three_kernel(z_mine, z_got, x_part, dep_r, dep_l, out_z, out_x):
    for half, dep in enumerate((dep_r, dep_l)):
        out_z[half] = z_mine[2 + half] + z_got[2 + half]
        out_x[half] = x_part[half] + dep[1]


def shapes(halves, *counts):
    return [(count, halves.rows, BLOCK) for count in counts]


def project_all(halves, place, activations, weight, after=()):
    firsts = project(
        first_kernel, halves, place, activations, weight, 0, 3, [4, 4, 4, 4], after=after
    )
    seconds = project(
        second_kernel,
        halves,
        place,
        activations,
        weight,
        1,
        3,
        [2, 2, 4, 4, 2, 2],
        after=(firsts[3],),
    )
    return firsts, seconds


def reduce_chunks(halves, sends, firsts, seconds, beside_one=None, beside_two=None):
    _, _, _, z_first_mine = firsts
    keep_r, keep_l, z_other, z_mine, x_other, x_mine = seconds
    send_r, send_l, z_send = sends
    got_r, got_l, z_first_got = shift_x(send_r, 1), shift_x(send_l, -1), swap_z(z_send)
    ready = beside_one(keep_r) if beside_one else ()
    dep_r, dep_l = call(
        first_sum_kernel,
        shapes(halves, 3, 3),
        keep_r,
        got_r,
        keep_l,
        got_l,
        z_first_mine,
        z_first_got,
        after=(x_other,) + tuple(ready),
    )
    z_part, x_part_other, x_part_mine = call(
        beside_two_kernel,
        shapes(halves, 2, 2, 2),
        z_first_mine,
        z_first_got,
        x_other,
        x_mine,
        got_r,
        got_l,
        after=(dep_r,),
    )
    ready = beside_two(dep_r) if beside_two else ()
    dep_r, dep_l, z_got = shift_x(dep_r, 1), shift_x(dep_l, -1), swap_z(z_other)
    last_r, last_l, x_sum = call(
        second_sum_kernel,
        shapes(halves, 2, 2, 2),
        z_part,
        z_mine,
        z_got,
        x_part_other,
        dep_r,
        dep_l,
        after=ready,
    )
    last = last_r
    z_part, x_part = call(
        beside_three_kernel,
        shapes(halves, 2, 2),
        z_mine,
        z_got,
        x_part_mine,
        dep_r,
        dep_l,
        after=(last,),
    )
    last_r, last_l, x_sum = shift_x(last_r, 1), shift_x(last_l, -1), swap_z(x_sum)
    return (z_part, last_r, last_l, x_part, x_sum), last


def summed(z_part, z_r, z_l, x_part, x_got):
    return [z_part[h] + (z_r[h] + z_l[h]) for h in range(2)] + [
        x_part[h] + x_got[h] for h in range(2)
    ]


def release(values, after):
    def body(*refs):
        pass

    count = len(values)
    return pl.pallas_call(
        body,
        in_specs=[pl.BlockSpec(memory_space=pl.ANY)] * (count + 1),
        out_specs=[pl.BlockSpec(memory_space=pl.ANY)] * count,
        out_shape=[jax.ShapeDtypeStruct(value.shape, value.dtype) for value in values],
        input_output_aliases={i: i for i in range(count)},
        name="release",
    )(*values, after)


def split_bf16(table):
    high = table.astype(np.float32).astype(ml_dtypes.bfloat16)
    low = (table - high.astype(np.float64)).astype(ml_dtypes.bfloat16)
    return high, low


@functools.lru_cache(None)
def tables(length):
    rows = length // BLOCK
    period = 2 * length
    odd = np.arange(rows) + 0.5
    first = -2 * np.pi * np.outer(odd, np.arange(rows)) / (2 * rows)
    turn = -2 * np.pi * np.outer(odd, np.arange(BLOCK)) / period
    second = -2 * np.pi * (np.outer(np.arange(BLOCK), np.arange(BLOCK)) % BLOCK) / BLOCK
    c, s = np.cos(second), np.sin(second)
    scale = 1.0 / length
    return (
        split_bf16(np.concatenate([np.cos(first), np.sin(first)], axis=0)),
        (np.cos(turn).astype(np.float32), np.sin(turn).astype(np.float32)),
        split_bf16(np.block([[c, s], [-s, c]])),
        split_bf16(np.block([[c, -s], [s, c]])),
        split_bf16(np.concatenate([np.cos(first).T, np.sin(first).T], axis=1) * scale),
    )


def split_value(value):
    high = value.astype(jnp.bfloat16)
    return high, (value - high.astype(jnp.float32)).astype(jnp.bfloat16)


def dot3(left, right):
    dot = functools.partial(jnp.dot, preferred_element_type=jnp.float32)
    return dot(left[0], right[0]) + (dot(left[0], right[1]) + dot(left[1], right[0]))


def forward(signal_ref, first, turn, second):
    seqs, channels = signal_ref.shape[:2]
    rows = seqs * signal_ref.shape[2]
    signal = jnp.concatenate(
        [signal_ref[:, c].reshape(rows, BLOCK) for c in range(channels)], axis=1
    )
    part = dot3(first, split_value(signal))
    turned = []
    for c in range(channels):
        real = part[:rows, c * BLOCK : (c + 1) * BLOCK]
        imag = part[rows:, c * BLOCK : (c + 1) * BLOCK]
        turned.append(
            jnp.concatenate(
                [real * turn[0] - imag * turn[1], real * turn[1] + imag * turn[0]], axis=1
            )
        )
    return dot3(split_value(jnp.concatenate(turned, axis=0)), second)


def taps_kernel(taps_ref, f_hi, f_lo, t_re, t_im, s_hi, s_lo, out_ref):
    out_ref[...] = forward(
        taps_ref, (f_hi[...], f_lo[...]), (t_re[...], t_im[...]), (s_hi[...], s_lo[...])
    )


def conv_kernel(
    kv_ref, spec_ref, f_hi, f_lo, t_re, t_im, s_hi, s_lo, b_hi, b_lo, i_hi, i_lo, out_ref
):
    seqs, channels, blocks, _ = kv_ref.shape
    rows = seqs * blocks
    turn = (t_re[...], t_im[...])
    spectrum = forward(kv_ref, (f_hi[...], f_lo[...]), turn, (s_hi[...], s_lo[...]))
    real, imag = spectrum[:, :BLOCK], spectrum[:, BLOCK:]
    taps_real, taps_imag = spec_ref[:, :BLOCK], spec_ref[:, BLOCK:]
    product = jnp.concatenate(
        [real * taps_real - imag * taps_imag, real * taps_imag + imag * taps_real], axis=1
    )
    back = dot3(split_value(product), (b_hi[...], b_lo[...]))
    columns = []
    for c in range(channels):
        real = back[c * rows : (c + 1) * rows, :BLOCK]
        imag = back[c * rows : (c + 1) * rows, BLOCK:]
        columns.append(
            jnp.concatenate(
                [real * turn[0] + imag * turn[1], imag * turn[0] - real * turn[1]], axis=0
            )
        )
    result = dot3((i_hi[...], i_lo[...]), split_value(jnp.concatenate(columns, axis=1)))
    for c in range(channels):
        out_ref[:, c] = result[:, c * BLOCK : (c + 1) * BLOCK].reshape(seqs, blocks, BLOCK)


def turn_blocks(value_ref, out_ref):
    for b in range(out_ref.shape[1]):
        out_ref[:, b, :] = value_ref[b * BLOCK : (b + 1) * BLOCK, :].T


def taps_turn_kernel(taps_ref, out_ref):
    turn_blocks(taps_ref, out_ref)


def kv_kernel(*refs):
    parts, out_ref, kv_ref = refs[:-2], refs[-2], refs[-1]
    z_key, z_value, x_key, x_value = summed(*parts)
    rows = z_key.shape[0]
    kv_ref[:rows] = z_key * z_value
    kv_ref[rows:] = x_key * x_value
    turn_blocks(kv_ref, out_ref)


def query_kernel(*refs):
    parts, out_ref = refs[:-1], refs[-1]
    for i, query in enumerate(summed(*parts)):
        rows = query.shape[0]
        out_ref[i * rows : (i + 1) * rows] = query


def gate_kernel(conv_ref, query_ref, out_ref):
    for b in range(conv_ref.shape[1]):
        rows = slice(b * BLOCK, (b + 1) * BLOCK)
        out_ref[rows] = conv_ref[:, b, :].T * query_ref[rows]


def call(kernel, out_shapes, *operands, after=(), scratch=(), tables=()):
    single = not isinstance(out_shapes, list)
    shapes = [out_shapes] if single else out_shapes

    def body(*refs):
        count = len(operands) + len(tables)
        kernel(*refs[:count], *refs[count + len(after) :])

    def whole(shape):
        return pl.BlockSpec(shape, lambda i: (0,) * len(shape))

    result = pl.pallas_call(
        body,
        grid=(1,),
        in_specs=[pl.BlockSpec(memory_space=pltpu.VMEM)] * len(operands)
        + [whole(table.shape) for table in tables]
        + [pl.BlockSpec(memory_space=pl.ANY)] * len(after),
        out_specs=[pl.BlockSpec(memory_space=pltpu.VMEM)] * len(shapes),
        out_shape=[jax.ShapeDtypeStruct(shape, jnp.float32) for shape in shapes],
        scratch_shapes=scratch,
        compiler_params=params(24),
        name=kernel.__name__,
    )(*operands, *[in_hbm(jnp.asarray(table)) for table in tables], *after)
    return result[0] if single else result


def exchange(value):
    return lax.all_to_all(value, "seq", split_axis=0, concat_axis=0, tiled=True)


def on_device(activations, proj_weight, filter_taps):
    tokens, channels = filter_taps.shape
    seqs = lax.axis_size("seq")
    length = tokens * seqs
    blocks = tokens // BLOCK
    owned = channels // seqs
    turned_shape = (channels, blocks, BLOCK)
    moved_shape = (seqs, owned, blocks, BLOCK)
    first, turn, second, back, inverse = tables(length)

    chan = lax.axis_index("chan")
    x_at, z_at = chan // 2, chan % 2
    owners = [(x_at + dx) % X_SIZE for dx in (2, 1, 3, 0)]
    place = jnp.stack(owners + [z_at]).astype(jnp.int32)
    weight = in_hbm(jnp.transpose(proj_weight, (1, 0, 2)))
    activations = in_hbm(activations)

    kv_halves, q_halves = Halves(tokens, (1, 2)), Halves(tokens, (0,))
    hold = {}

    def move_taps(ready):
        turned = call(taps_turn_kernel, turned_shape, filter_taps, after=(ready,))
        hold["taps"] = exchange(turned.reshape(moved_shape))
        return (hold["taps"],)

    def prepare(ready):
        hold["spectrum"] = call(
            taps_kernel,
            (owned * length // BLOCK, 2 * BLOCK),
            hold["taps"],
            tables=first + turn + second,
        )
        hold["query"] = project_all(q_halves, place, activations, weight, after=(ready,))
        return hold["spectrum"], hold["query"][1][0]

    kv_firsts, kv_seconds = project_all(kv_halves, place, activations, weight)
    kv_parts, kv_last = reduce_chunks(
        kv_halves, kv_firsts[:3], kv_firsts, kv_seconds, move_taps, prepare
    )
    spectrum, (q_firsts, q_seconds) = hold["spectrum"], hold["query"]

    kv = call(
        kv_kernel,
        turned_shape,
        *kv_parts,
        scratch=[pltpu.VMEM((tokens, channels), jnp.float32)],
    )
    moved = exchange(kv.reshape(moved_shape))
    q_sends = release(q_firsts[:3], kv_last)
    q_parts, _ = reduce_chunks(q_halves, q_sends, q_firsts, q_seconds)
    query = call(query_kernel, (tokens, channels), *q_parts)
    convolved = call(
        conv_kernel,
        moved_shape,
        moved,
        spectrum,
        tables=first + turn + second + back + inverse,
    )
    home = exchange(convolved).reshape(turned_shape)
    return call(gate_kernel, (tokens, channels), home, query)


def solution(mesh):
    return jax.shard_map(
        on_device,
        mesh=mesh,
        in_specs=(P("seq", "chan"), P("chan", None, None), P("seq", "chan")),
        out_specs=P("seq", "chan"),
        check_vma=False,
    )
```

```python
import functools

import jax
import jax.numpy as jnp
import ml_dtypes
import numpy as np
from jax import lax
from jax.experimental import pallas as pl
from jax.experimental.pallas import tpu as pltpu
from jax.sharding import PartitionSpec as P

BLOCK = 128
X_SIZE = 4
CHUNK = 256


def params(mebibytes):
    return pltpu.CompilerParams(vmem_limit_bytes=mebibytes * 1024 * 1024)


def in_hbm(value):
    return pltpu.with_memory_space_constraint(value, pltpu.HBM)


def shift_x(value, step):
    return lax.ppermute(value, "chan", [(i, (i + 2 * step) % 8) for i in range(8)])


def swap_z(value):
    return lax.ppermute(value, "chan", [(i, i ^ 1) for i in range(8)])


def parts_of(rows, weight, z_at):
    product = jnp.dot(rows, weight, preferred_element_type=jnp.float32)
    low, high = product[:, :BLOCK], product[:, BLOCK:]
    return jnp.where(z_at == 0, high, low), jnp.where(z_at == 0, low, high)


class Halves:
    def __init__(self, tokens, columns):
        self.columns = columns
        parts = 2 // len(columns)
        self.rows = tokens // 2 // parts
        self.z_start = [h % parts * self.rows for h in range(2)]
        self.x_start = [tokens // 2 + start for start in self.z_start]

    def shape(self, count):
        return (count, self.rows, BLOCK)

    def fill(self, place, act, weight, half, x_outs, z_outs):
        for begin, outs in ((self.x_start[half], x_outs), (self.z_start[half], z_outs)):
            for start in range(0, self.rows, CHUNK):
                rows = act[begin + start : begin + start + CHUNK]
                for (ref, piece), part in zip(outs, parts_of(rows, weight[0], place[4])):
                    ref[piece, start : start + CHUNK] = part


def first_kernel(halves, place, act, weight, outs):
    send_r, send_l, z_other, z_mine = outs
    for half, send in enumerate((send_r, send_l)):
        pl.when(pl.program_id(0) == half)(
            functools.partial(
                halves.fill,
                place,
                act,
                weight,
                half,
                ((send, 0), (send, 1)),
                ((z_other, half), (z_mine, half)),
            )
        )


def second_kernel(halves, place, act, weight, outs):
    dep_r, dep_l, z_send, z_late, z_mine, x_other, x_mine = outs
    x_outs = (
        ((dep_r, 2), (dep_r, 3)),
        ((dep_r, 0), (dep_r, 1)),
        ((dep_l, 0), (dep_l, 1)),
        ((dep_l, 2), (dep_l, 3)),
        ((x_other, 0), (x_mine, 0)),
        ((x_other, 0), (x_mine, 0)),
    )
    for i, outs in enumerate(x_outs):
        z_other = (z_send, i) if i < 5 else (z_late, 0)
        pl.when(pl.program_id(0) == i)(
            functools.partial(
                halves.fill, place, act, weight, i % 2, outs, (z_other, (z_mine, 0))
            )
        )


def project(kernel, halves, place, activations, weight, owner, steps, outs, after=()):
    first, last = halves.columns[0], halves.columns[-1]

    def weight_block(i, at):
        return (first + (last - first) * (i % 2), 0, at[owner + i // 2])

    def body(at, act, weight_ref, *refs):
        kernel(halves, at, act, weight_ref, refs[len(after) :])

    specs, results = [], []
    for count, where in outs:
        if where == "vmem":
            specs.append(pl.BlockSpec(memory_space=pltpu.VMEM))
            results.append(jax.ShapeDtypeStruct(halves.shape(count), jnp.float32))
            continue
        results.append(pltpu.HBM(halves.shape(count), jnp.float32))
        if where == "hbm":
            specs.append(pl.BlockSpec(halves.shape(count), lambda i, at: (0, 0, 0)))
        else:
            specs.append(
                pl.BlockSpec(
                    halves.shape(1),
                    lambda i, at, start=where, end=count - 1: (
                        jnp.clip(i - start, 0, end),
                        0,
                        0,
                    ),
                )
            )
    return pl.pallas_call(
        body,
        grid_spec=pltpu.PrefetchScalarGridSpec(
            num_scalar_prefetch=1,
            grid=(steps,),
            in_specs=[
                pl.BlockSpec(activations.shape, lambda i, at: (0, 0)),
                pl.BlockSpec((1, weight.shape[1], 2 * BLOCK), weight_block),
            ]
            + [pl.BlockSpec(memory_space=pl.ANY)] * len(after),
            out_specs=specs,
        ),
        out_shape=results,
        compiler_params=params(24),
        name=kernel.__name__,
    )(place, activations, weight, *after)


def sum_call(kernel, halves, counts, near, far, after=()):
    tile = min(BLOCK, halves.rows)

    def body(*refs):
        rows = pl.ds(pl.multiple_of(pl.program_id(0) * tile, tile), tile)
        ins = [ref.at[:, rows] for ref in refs[: len(near)]]
        ins += refs[len(near) : len(near) + len(far)]
        kernel(*ins, *[ref.at[:, rows] for ref in refs[len(near) + len(far) + len(after) :]])

    return pl.pallas_call(
        body,
        grid=(halves.rows // tile,),
        in_specs=[pl.BlockSpec(memory_space=pltpu.VMEM)] * len(near)
        + [pl.BlockSpec((value.shape[0], tile, BLOCK), lambda i: (0, i, 0)) for value in far]
        + [pl.BlockSpec(memory_space=pl.ANY)] * len(after),
        out_specs=[pl.BlockSpec(memory_space=pltpu.VMEM)] * len(counts),
        out_shape=[jax.ShapeDtypeStruct(halves.shape(count), jnp.float32) for count in counts],
        compiler_params=params(16),
        name=kernel.__name__,
    )(*near, *[in_hbm(value) for value in far], *after)


def kv_first_sum_kernel(dep_r, dep_l, got_r, got_l, z_mine, z_got, out_r, out_l):
    for half, (dep, got, out) in enumerate(((dep_r, got_r, out_r), (dep_l, got_l, out_l))):
        out[0] = dep[0]
        out[1] = dep[1]
        out[2] = dep[2] + got[0]
        out[3] = dep[3] + got[1]
        out[4] = z_mine[half] + z_got[half]


def kv_second_sum_kernel(dep_r, dep_l, z_got, z_mine, x_other, z_late, out_r, out_l, out_xz):
    out_r[0] = z_mine[0] + z_got[0] + dep_r[4]
    out_r[1] = z_mine[1] + z_got[1]
    out_l[0] = z_mine[2] + z_got[2]
    out_l[1] = z_mine[3] + z_got[3] + dep_l[4]
    out_xz[0] = x_other[0] + (dep_r[2] + dep_l[0])
    out_xz[1] = x_other[1] + (dep_r[0] + dep_l[2])
    out_xz[2] = z_late[0]


def kv_beside_kernel(dep_r, dep_l, z_got, z_mine, x_mine, out_z, out_x):
    out_z[0] = z_mine[4] + z_got[4]
    out_z[1] = z_mine[5]
    out_x[0] = x_mine[0] + (dep_r[3] + dep_l[1])
    out_x[1] = x_mine[1] + (dep_r[1] + dep_l[3])


def release(values, after):
    def body(*refs):
        pass

    count = len(values)
    return pl.pallas_call(
        body,
        in_specs=[pl.BlockSpec(memory_space=pl.ANY)] * (count + 1),
        out_specs=[pl.BlockSpec(memory_space=pl.ANY)] * count,
        out_shape=[pltpu.HBM(value.shape, value.dtype) for value in values],
        input_output_aliases={i: i for i in range(count)},
        name="release",
    )(*values, after)


def query_project_kernel(halves, place, act, weight, outs):
    send_r, send_l, keep_r, keep_l, z_send, z_late, z_mine, x_other, x_mine = outs
    x_outs = (
        ((send_r, 0), (send_r, 1)),
        ((send_l, 0), (send_l, 1)),
        ((keep_r, 0), (keep_r, 1)),
        ((send_r, 2), (send_r, 3)),
        ((send_l, 2), (send_l, 3)),
        ((keep_l, 0), (keep_l, 1)),
        ((x_other, 0), (x_mine, 0)),
        ((x_other, 0), (x_mine, 0)),
    )
    for i, outs in enumerate(x_outs):
        z_other = z_send if i < 6 else z_late
        pl.when(pl.program_id(0) == i)(
            functools.partial(
                halves.fill, place, act, weight, i % 2, outs, ((z_other, 0), (z_mine, 0))
            )
        )


def query_first_sum_kernel(got_r, got_l, z_got, keep_r, keep_l, z_mine, out_r, out_l):
    for half, (keep, got, out) in enumerate(((keep_r, got_r, out_r), (keep_l, got_l, out_l))):
        out[0] = keep[0] + got[0]
        out[1] = keep[1] + got[1]
        out[2] = z_mine[half] + z_got[half]


def query_second_sum_kernel(
    dep_r, dep_l, got_r, got_l, z_got, z_mine, x_other, out_r, out_l, out_x
):
    out_r[0] = z_mine[2] + z_got[2] + dep_r[2]
    out_r[1] = z_mine[3] + z_got[3]
    out_l[0] = z_mine[4] + z_got[4]
    out_l[1] = z_mine[5] + z_got[5] + dep_l[2]
    out_x[0] = x_other[0] + (dep_r[0] + got_l[2])
    out_x[1] = x_other[1] + (got_r[2] + dep_l[0])


def query_beside_kernel(dep_r, dep_l, got_r, got_l, z_got, z_mine, x_mine, out_z, out_x):
    out_z[0] = z_mine[6] + z_got[0]
    out_z[1] = z_mine[7] + z_got[1]
    out_x[0] = x_mine[0] + (dep_r[1] + got_l[3])
    out_x[1] = x_mine[1] + (got_r[3] + dep_l[1])


def reduce_kv(halves, place, activations, weight, beside):
    send_r, send_l, z_send, z_mine = project(
        first_kernel, halves, place, activations, weight, 0, 2, [(2, "vmem")] * 4
    )
    got_r, got_l, z_got = shift_x(send_r, 1), shift_x(send_l, -1), swap_z(z_send)
    dep_r, dep_l, z_send, z_late, z_six, x_other, x_mine = project(
        second_kernel,
        halves,
        place,
        activations,
        weight,
        1,
        6,
        [(5, "vmem")] * 3 + [(1, 0), (6, 0), (2, 4), (2, 4)],
        after=(z_mine,),
    )
    dep_r, dep_l = sum_call(
        kv_first_sum_kernel,
        halves,
        [5, 5],
        [dep_r, dep_l, got_r, got_l, z_mine, z_got],
        [],
    )
    ready = beside(dep_r)
    dep_r, dep_l, z_got = shift_x(dep_r, 1), shift_x(dep_l, -1), swap_z(z_send)
    last_r, last_l, last_xz = sum_call(
        kv_second_sum_kernel,
        halves,
        [2, 2, 3],
        [dep_r, dep_l, z_got],
        [z_six, x_other, z_late],
        after=ready,
    )
    last = last_r
    z_part, x_part = sum_call(
        kv_beside_kernel, halves, [2, 2], [dep_r, dep_l, z_got], [z_six, x_mine], after=(last,)
    )
    last_r, last_l, last_xz = shift_x(last_r, 1), shift_x(last_l, -1), swap_z(last_xz)
    return (z_part, last_r, last_l, x_part, last_xz), last


def project_query(halves, place, activations, weight, after):
    return project(
        query_project_kernel,
        halves,
        place,
        activations,
        weight,
        0,
        8,
        [(4, "hbm")] * 2 + [(2, "hbm")] * 2 + [(6, 0), (2, 6), (8, 0), (2, 6), (2, 6)],
        after=after,
    )


def reduce_query(halves, projected, x_after, z_after):
    send_r, send_l, keep_r, keep_l, z_send, z_late, z_mine, x_other, x_mine = projected
    send_r, send_l = release((send_r, send_l), x_after)
    got_r, got_l = shift_x(send_r, 1), shift_x(send_l, -1)
    (z_send,) = release((z_send,), z_after)
    z_got = swap_z(z_send)
    dep_r, dep_l = sum_call(
        query_first_sum_kernel,
        halves,
        [3, 3],
        [got_r, got_l, z_got],
        [keep_r, keep_l, z_mine],
    )
    (z_late,) = release((z_late,), dep_r)
    dep_r, dep_l, late_got = shift_x(dep_r, 1), shift_x(dep_l, -1), swap_z(z_late)
    last_r, last_l, x_sum = sum_call(
        query_second_sum_kernel,
        halves,
        [2, 2, 2],
        [dep_r, dep_l, got_r, got_l, z_got],
        [z_mine, x_other],
    )
    z_part, x_part = sum_call(
        query_beside_kernel,
        halves,
        [2, 2],
        [dep_r, dep_l, got_r, got_l, late_got],
        [z_mine, x_mine],
        after=(last_r,),
    )
    last_r, last_l, x_sum = shift_x(last_r, 1), shift_x(last_l, -1), swap_z(x_sum)
    return z_part, last_r, last_l, x_part, x_sum


def summed(z_part, last_r, last_l, x_part, last_x):
    z_total = [z_part[h] + (last_r[h] + last_l[h]) for h in range(2)]
    if last_x.shape[0] == 3:
        z_total[1] = z_total[1] + last_x[2]
    return z_total + [x_part[h] + last_x[h] for h in range(2)]


def split_bf16(table):
    high = table.astype(np.float32).astype(ml_dtypes.bfloat16)
    low = (table - high.astype(np.float64)).astype(ml_dtypes.bfloat16)
    return high, low


@functools.lru_cache(None)
def tables(length):
    rows = length // BLOCK
    period = 2 * length
    odd = np.arange(rows) + 0.5
    first = -2 * np.pi * np.outer(odd, np.arange(rows)) / (2 * rows)
    turn = -2 * np.pi * np.outer(odd, np.arange(BLOCK)) / period
    second = -2 * np.pi * (np.outer(np.arange(BLOCK), np.arange(BLOCK)) % BLOCK) / BLOCK
    c, s = np.cos(second), np.sin(second)
    scale = 1.0 / length
    return (
        split_bf16(np.concatenate([np.cos(first), np.sin(first)], axis=0)),
        (np.cos(turn).astype(np.float32), np.sin(turn).astype(np.float32)),
        split_bf16(np.block([[c, s], [-s, c]])),
        split_bf16(np.block([[c, -s], [s, c]])),
        split_bf16(np.concatenate([np.cos(first).T, np.sin(first).T], axis=1) * scale),
    )


def split_value(value):
    high = value.astype(jnp.bfloat16)
    return high, (value - high.astype(jnp.float32)).astype(jnp.bfloat16)


def dot3(left, right):
    dot = functools.partial(jnp.dot, preferred_element_type=jnp.float32)
    return dot(left[0], right[0]) + (dot(left[0], right[1]) + dot(left[1], right[0]))


def forward(signal_ref, first, turn, second):
    seqs, channels = signal_ref.shape[:2]
    rows = seqs * signal_ref.shape[2]
    signal = jnp.concatenate(
        [signal_ref[:, c].reshape(rows, BLOCK) for c in range(channels)], axis=1
    )
    part = dot3(first, split_value(signal))
    turned = []
    for c in range(channels):
        real = part[:rows, c * BLOCK : (c + 1) * BLOCK]
        imag = part[rows:, c * BLOCK : (c + 1) * BLOCK]
        turned.append(
            jnp.concatenate(
                [real * turn[0] - imag * turn[1], real * turn[1] + imag * turn[0]], axis=1
            )
        )
    return dot3(split_value(jnp.concatenate(turned, axis=0)), second)


def taps_kernel(taps_ref, f_hi, f_lo, t_re, t_im, s_hi, s_lo, out_ref):
    out_ref[...] = forward(
        taps_ref, (f_hi[...], f_lo[...]), (t_re[...], t_im[...]), (s_hi[...], s_lo[...])
    )


def conv_kernel(
    kv_ref, spec_ref, f_hi, f_lo, t_re, t_im, s_hi, s_lo, b_hi, b_lo, i_hi, i_lo, out_ref
):
    seqs, channels, blocks, _ = kv_ref.shape
    rows = seqs * blocks
    turn = (t_re[...], t_im[...])
    spectrum = forward(kv_ref, (f_hi[...], f_lo[...]), turn, (s_hi[...], s_lo[...]))
    real, imag = spectrum[:, :BLOCK], spectrum[:, BLOCK:]
    taps_real, taps_imag = spec_ref[:, :BLOCK], spec_ref[:, BLOCK:]
    product = jnp.concatenate(
        [real * taps_real - imag * taps_imag, real * taps_imag + imag * taps_real], axis=1
    )
    back = dot3(split_value(product), (b_hi[...], b_lo[...]))
    columns = []
    for c in range(channels):
        real = back[c * rows : (c + 1) * rows, :BLOCK]
        imag = back[c * rows : (c + 1) * rows, BLOCK:]
        columns.append(
            jnp.concatenate(
                [real * turn[0] + imag * turn[1], imag * turn[0] - real * turn[1]], axis=0
            )
        )
    result = dot3((i_hi[...], i_lo[...]), split_value(jnp.concatenate(columns, axis=1)))
    for c in range(channels):
        out_ref[:, c] = result[:, c * BLOCK : (c + 1) * BLOCK].reshape(seqs, blocks, BLOCK)


def turn_blocks(value_ref, out_ref):
    for b in range(out_ref.shape[1]):
        out_ref[:, b, :] = value_ref[b * BLOCK : (b + 1) * BLOCK, :].T


def taps_turn_kernel(taps_ref, out_ref):
    turn_blocks(taps_ref, out_ref)


def kv_kernel(*refs):
    parts, out_ref, kv_ref = refs[:-2], refs[-2], refs[-1]
    z_key, z_value, x_key, x_value = summed(*parts)
    rows = z_key.shape[0]
    kv_ref[:rows] = z_key * z_value
    kv_ref[rows:] = x_key * x_value
    turn_blocks(kv_ref, out_ref)


def query_kernel(*refs):
    parts, out_ref = refs[:-1], refs[-1]
    for i, query in enumerate(summed(*parts)):
        rows = query.shape[0]
        out_ref[i * rows : (i + 1) * rows] = query


def gate_kernel(conv_ref, query_ref, out_ref):
    for b in range(conv_ref.shape[1]):
        rows = slice(b * BLOCK, (b + 1) * BLOCK)
        out_ref[rows] = conv_ref[:, b, :].T * query_ref[rows]


def call(kernel, out_shape, *operands, after=(), scratch=(), tables=(), to_hbm=False):
    def body(*refs):
        count = len(operands) + len(tables)
        kernel(*refs[:count], *refs[count + len(after) :])

    def whole(shape):
        return pl.BlockSpec(shape, lambda i: (0,) * len(shape))

    return pl.pallas_call(
        body,
        grid=(1,),
        in_specs=[pl.BlockSpec(memory_space=pltpu.VMEM)] * len(operands)
        + [whole(table.shape) for table in tables]
        + [pl.BlockSpec(memory_space=pl.ANY)] * len(after),
        out_specs=whole(out_shape) if to_hbm else pl.BlockSpec(memory_space=pltpu.VMEM),
        out_shape=pltpu.HBM(out_shape, jnp.float32)
        if to_hbm
        else jax.ShapeDtypeStruct(out_shape, jnp.float32),
        scratch_shapes=scratch,
        compiler_params=params(24),
        name=kernel.__name__,
    )(*operands, *[in_hbm(jnp.asarray(table)) for table in tables], *after)


def exchange(value):
    return lax.all_to_all(value, "seq", split_axis=0, concat_axis=0, tiled=True)


def on_device(activations, proj_weight, filter_taps):
    tokens, channels = filter_taps.shape
    seqs = lax.axis_size("seq")
    length = tokens * seqs
    blocks = tokens // BLOCK
    owned = channels // seqs
    turned_shape = (channels, blocks, BLOCK)
    moved_shape = (seqs, owned, blocks, BLOCK)
    first, turn, second, back, inverse = tables(length)

    chan = lax.axis_index("chan")
    x_at, z_at = chan // 2, chan % 2
    owners = [(x_at + dx) % X_SIZE for dx in (2, 1, 3, 0)]
    place = jnp.stack(owners + [z_at]).astype(jnp.int32)
    weight = in_hbm(jnp.transpose(proj_weight, (1, 0, 2)))
    activations = in_hbm(activations)

    hold = {}
    kv_halves, q_halves = Halves(tokens, (1, 2)), Halves(tokens, (0,))

    def prepare(ready):
        taps = call(taps_turn_kernel, turned_shape, filter_taps, after=(ready,), to_hbm=True)
        hold["spectrum"] = call(
            taps_kernel,
            (owned * length // BLOCK, 2 * BLOCK),
            exchange(taps.reshape(moved_shape)),
            tables=first + turn + second,
        )
        hold["query"] = project_query(q_halves, place, activations, weight, (ready,))
        return hold["spectrum"], hold["query"][0]

    kv_parts, kv_last = reduce_kv(kv_halves, place, activations, weight, prepare)
    kv = call(
        kv_kernel,
        turned_shape,
        *kv_parts,
        scratch=[pltpu.VMEM((tokens, channels), jnp.float32)],
        to_hbm=True,
    )
    q_parts = reduce_query(q_halves, hold["query"], kv_last, kv_last)
    moved = exchange(kv.reshape(moved_shape))
    convolved = call(
        conv_kernel,
        moved_shape,
        moved,
        hold["spectrum"],
        tables=first + turn + second + back + inverse,
        to_hbm=True,
    )
    query = call(query_kernel, (tokens, channels), *q_parts)
    home = exchange(convolved).reshape(turned_shape)
    return call(gate_kernel, (tokens, channels), home, query)


def solution(mesh):
    return jax.shard_map(
        on_device,
        mesh=mesh,
        in_specs=(P("seq", "chan"), P("chan", None, None), P("seq", "chan")),
        out_specs=P("seq", "chan"),
        check_vma=False,
    )
```

```python
import functools

import jax
import jax.numpy as jnp
import ml_dtypes
import numpy as np
from jax import lax
from jax.experimental import pallas as pl
from jax.experimental.pallas import tpu as pltpu
from jax.sharding import PartitionSpec as P

BLOCK = 128
X_SIZE = 4
CHUNK = 256


def params(mebibytes):
    return pltpu.CompilerParams(vmem_limit_bytes=mebibytes * 1024 * 1024)


def in_hbm(value):
    return pltpu.with_memory_space_constraint(value, pltpu.HBM)


def shift_x(value, step):
    return lax.ppermute(value, "chan", [(i, (i + 2 * step) % 8) for i in range(8)])


def swap_z(value):
    return lax.ppermute(value, "chan", [(i, i ^ 1) for i in range(8)])


def parts_of(rows, weight, z_at):
    product = jnp.dot(rows, weight, preferred_element_type=jnp.float32)
    low, high = product[:, :BLOCK], product[:, BLOCK:]
    return jnp.where(z_at == 0, high, low), jnp.where(z_at == 0, low, high)


class Halves:
    def __init__(self, tokens, columns):
        self.columns = columns
        parts = 2 // len(columns)
        self.rows = tokens // 2 // parts
        self.z_start = [h % parts * self.rows for h in range(2)]
        self.x_start = [tokens // 2 + start for start in self.z_start]

    def shape(self, count):
        return (count, self.rows, BLOCK)

    def fill(self, place, act, weight, half, x_outs, z_outs):
        for begin, outs in ((self.x_start[half], x_outs), (self.z_start[half], z_outs)):
            if outs == (None, None):
                continue
            for start in range(0, self.rows, CHUNK):
                rows = act[begin + start : begin + start + CHUNK]
                for out, part in zip(outs, parts_of(rows, weight[0], place[4])):
                    if out is not None:
                        out[0][out[1], start : start + CHUNK] = part


def first_kernel(halves, place, act, weight, outs):
    send_r, send_l, z_other, z_mine = outs
    for half, send in enumerate((send_r, send_l)):
        pl.when(pl.program_id(0) == half)(
            functools.partial(
                halves.fill,
                place,
                act,
                weight,
                half,
                ((send, 0), (send, 1)),
                ((z_other, half), (z_mine, half)),
            )
        )


def second_kernel(halves, place, act, weight, outs):
    near_r, near_l, keep_r, keep_l, z_send = outs
    x_outs = (
        ((keep_r, 0), (keep_r, 1)),
        ((near_r, 0), (near_r, 1)),
        ((near_l, 0), (near_l, 1)),
        ((keep_l, 0), (keep_l, 1)),
        (None, None),
    )
    for i, outs in enumerate(x_outs):
        pl.when(pl.program_id(0) == i)(
            functools.partial(
                halves.fill, place, act, weight, i % 2, outs, ((z_send, i), None)
            )
        )


def third_kernel(halves, place, act, weight, outs):
    z_mine, z_late, x_other, x_mine = outs
    for i in range(6):
        x_outs = (None, None) if i < 4 else ((x_other, i - 4), (x_mine, i - 4))
        z_other = (z_late, 0) if i == 5 else None
        pl.when(pl.program_id(0) == i)(
            functools.partial(
                halves.fill, place, act, weight, i % 2, x_outs, (z_other, (z_mine, i))
            )
        )


def project(kernel, halves, place, activations, weight, owner, steps, outs, after=()):
    first, last = halves.columns[0], halves.columns[-1]

    def weight_block(i, at):
        return (first + (last - first) * (i % 2), 0, at[owner + i // 2])

    def body(at, act, weight_ref, *refs):
        kernel(halves, at, act, weight_ref, refs[len(after) :])

    specs, results = [], []
    for count, where in outs:
        if where == "vmem":
            specs.append(pl.BlockSpec(memory_space=pltpu.VMEM))
            results.append(jax.ShapeDtypeStruct(halves.shape(count), jnp.float32))
            continue
        results.append(pltpu.HBM(halves.shape(count), jnp.float32))
        if where == "hbm":
            specs.append(pl.BlockSpec(halves.shape(count), lambda i, at: (0, 0, 0)))
        else:
            specs.append(
                pl.BlockSpec(
                    halves.shape(1),
                    lambda i, at, start=where, end=count - 1: (
                        jnp.clip(i - start, 0, end),
                        0,
                        0,
                    ),
                )
            )
    return pl.pallas_call(
        body,
        grid_spec=pltpu.PrefetchScalarGridSpec(
            num_scalar_prefetch=1,
            grid=(steps,),
            in_specs=[
                pl.BlockSpec(activations.shape, lambda i, at: (0, 0)),
                pl.BlockSpec((1, weight.shape[1], 2 * BLOCK), weight_block),
            ]
            + [pl.BlockSpec(memory_space=pl.ANY)] * len(after),
            out_specs=specs,
        ),
        out_shape=results,
        compiler_params=params(24),
        name=kernel.__name__,
    )(place, activations, weight, *after)


def sum_call(kernel, halves, counts, near, far, after=()):
    tile = min(BLOCK, halves.rows)

    def body(*refs):
        rows = pl.ds(pl.multiple_of(pl.program_id(0) * tile, tile), tile)
        ins = [ref.at[:, rows] for ref in refs[: len(near)]]
        ins += refs[len(near) : len(near) + len(far)]
        kernel(*ins, *[ref.at[:, rows] for ref in refs[len(near) + len(far) + len(after) :]])

    return pl.pallas_call(
        body,
        grid=(halves.rows // tile,),
        in_specs=[pl.BlockSpec(memory_space=pltpu.VMEM)] * len(near)
        + [pl.BlockSpec((value.shape[0], tile, BLOCK), lambda i: (0, i, 0)) for value in far]
        + [pl.BlockSpec(memory_space=pl.ANY)] * len(after),
        out_specs=[pl.BlockSpec(memory_space=pltpu.VMEM)] * len(counts),
        out_shape=[jax.ShapeDtypeStruct(halves.shape(count), jnp.float32) for count in counts],
        compiler_params=params(16),
        name=kernel.__name__,
    )(*near, *[in_hbm(value) for value in far], *after)


def first_sum_kernel(got_r, got_l, z_got, keep_r, keep_l, z_mine, out_r, out_l):
    for half, (keep, got, out) in enumerate(((keep_r, got_r, out_r), (keep_l, got_l, out_l))):
        out[0] = keep[0] + got[0]
        out[1] = keep[1] + got[1]
        out[2] = z_mine[half] + z_got[half]


def kv_near_kernel(near_r, near_l, x_other, x_mine, out_other, out_mine):
    for half, near in enumerate((near_l, near_r)):
        out_other[half] = x_other[half] + near[0]
        out_mine[half] = x_mine[half] + near[1]


def kv_second_sum_kernel(dep_r, dep_l, z_got, z_mine, x_part, z_late, out_r, out_l, out_xz):
    out_r[0] = z_mine[0] + z_got[0] + dep_r[2]
    out_r[1] = z_mine[1] + z_got[1]
    out_l[0] = z_mine[2] + z_got[2]
    out_l[1] = z_mine[3] + z_got[3] + dep_l[2]
    out_xz[0] = x_part[0] + dep_r[0]
    out_xz[1] = x_part[1] + dep_l[0]
    out_xz[2] = z_late[0]


def kv_beside_kernel(dep_r, dep_l, z_got, z_mine, x_part, out_z, out_x):
    out_z[0] = z_mine[4] + z_got[4]
    out_z[1] = z_mine[5]
    out_x[0] = x_part[0] + dep_r[1]
    out_x[1] = x_part[1] + dep_l[1]


def release(values, after):
    def body(*refs):
        pass

    count = len(values)
    return pl.pallas_call(
        body,
        in_specs=[pl.BlockSpec(memory_space=pl.ANY)] * (count + 1),
        out_specs=[pl.BlockSpec(memory_space=pl.ANY)] * count,
        out_shape=[pltpu.HBM(value.shape, value.dtype) for value in values],
        input_output_aliases={i: i for i in range(count)},
        name="release",
    )(*values, after)


def query_project_kernel(halves, place, act, weight, outs):
    send_r, send_l, keep_r, keep_l, z_send, z_next, z_late, z_mine, x_other, x_mine = outs
    x_outs = (
        ((send_r, 0), (send_r, 1)),
        ((send_l, 0), (send_l, 1)),
        ((keep_r, 0), (keep_r, 1)),
        ((send_r, 2), (send_r, 3)),
        ((send_l, 2), (send_l, 3)),
        ((keep_l, 0), (keep_l, 1)),
        ((x_other, 0), (x_mine, 0)),
        ((x_other, 0), (x_mine, 0)),
    )
    for i, outs in enumerate(x_outs):
        z_other = (z_send, z_next, z_late)[i // 3]
        pl.when(pl.program_id(0) == i)(
            functools.partial(
                halves.fill, place, act, weight, i % 2, outs, ((z_other, 0), (z_mine, 0))
            )
        )


def query_second_sum_kernel(
    dep_r, dep_l, got_r, got_l, z_got, z_next, z_mine, x_other, out_r, out_l, out_x
):
    out_r[0] = z_mine[2] + z_got[2] + dep_r[2]
    out_r[1] = z_mine[3] + z_next[0]
    out_l[0] = z_mine[4] + z_next[1]
    out_l[1] = z_mine[5] + z_next[2] + dep_l[2]
    out_x[0] = x_other[0] + (dep_r[0] + got_l[2])
    out_x[1] = x_other[1] + (got_r[2] + dep_l[0])


def query_beside_kernel(dep_r, dep_l, got_r, got_l, z_got, z_mine, x_mine, out_z, out_x):
    out_z[0] = z_mine[6] + z_got[0]
    out_z[1] = z_mine[7] + z_got[1]
    out_x[0] = x_mine[0] + (dep_r[1] + got_l[3])
    out_x[1] = x_mine[1] + (got_r[3] + dep_l[1])


def reduce_kv(halves, place, activations, weight, beside):
    make = functools.partial(
        project, halves=halves, place=place, activations=activations, weight=weight
    )
    send_r, send_l, z_send, z_mine = make(
        first_kernel, owner=0, steps=2, outs=[(2, "vmem")] * 4
    )
    got_r, got_l, z_got = shift_x(send_r, 1), shift_x(send_l, -1), swap_z(z_send)
    near_r, near_l, keep_r, keep_l, z_send = make(
        second_kernel,
        owner=1,
        steps=5,
        outs=[(2, "vmem")] * 4 + [(5, "vmem")],
        after=(z_mine,),
    )
    near_r, near_l, z_five = shift_x(near_r, 1), shift_x(near_l, -1), swap_z(z_send)
    dep_r, dep_l = sum_call(
        first_sum_kernel, halves, [3, 3], [got_r, got_l, z_got, keep_r, keep_l, z_mine], []
    )
    z_six, z_late, x_other, x_mine = make(
        third_kernel,
        owner=1,
        steps=6,
        outs=[(6, "vmem"), (1, "vmem"), (2, "vmem"), (2, "vmem")],
        after=(dep_r,),
    )
    x_part_other, x_part_mine = sum_call(
        kv_near_kernel, halves, [2, 2], [near_r, near_l, x_other, x_mine], []
    )
    ready = beside(dep_r, x_part_mine)
    dep_r, dep_l = shift_x(dep_r, 1), shift_x(dep_l, -1)
    last_r, last_l, last_xz = sum_call(
        kv_second_sum_kernel,
        halves,
        [2, 2, 3],
        [dep_r, dep_l, z_five, z_six, x_part_other, z_late],
        [],
        after=ready,
    )
    last = last_r
    z_part, x_part = sum_call(
        kv_beside_kernel,
        halves,
        [2, 2],
        [dep_r, dep_l, z_five, z_six, x_part_mine],
        [],
        after=(last,),
    )
    last_r, last_l, last_xz = shift_x(last_r, 1), shift_x(last_l, -1), swap_z(last_xz)
    return (z_part, last_r, last_l, x_part, last_xz), last


def project_query(halves, place, activations, weight, after):
    return project(
        query_project_kernel,
        halves,
        place,
        activations,
        weight,
        0,
        8,
        [(4, "hbm")] * 2 + [(2, "hbm")] * 2 + [(3, 0), (3, 3), (2, 6), (8, 0), (2, 6), (2, 6)],
        after=after,
    )


def reduce_query(halves, projected, after):
    send_r, send_l, keep_r, keep_l, z_send, z_next, z_late, z_mine, x_other, x_mine = projected
    got_r, got_l, z_got = shift_x(send_r, 1), shift_x(send_l, -1), swap_z(z_send)
    (z_next,) = release((z_next,), after)
    z_next = swap_z(z_next)
    dep_r, dep_l = sum_call(
        first_sum_kernel,
        halves,
        [3, 3],
        [got_r, got_l, z_got],
        [keep_r, keep_l, z_mine],
    )
    (z_late,) = release((z_late,), dep_r)
    dep_r, dep_l, late_got = shift_x(dep_r, 1), shift_x(dep_l, -1), swap_z(z_late)
    last_r, last_l, x_sum = sum_call(
        query_second_sum_kernel,
        halves,
        [2, 2, 2],
        [dep_r, dep_l, got_r, got_l, z_got, z_next],
        [z_mine, x_other],
    )
    z_part, x_part = sum_call(
        query_beside_kernel,
        halves,
        [2, 2],
        [dep_r, dep_l, got_r, got_l, late_got],
        [z_mine, x_mine],
        after=(last_r,),
    )
    last_r, last_l, x_sum = shift_x(last_r, 1), shift_x(last_l, -1), swap_z(x_sum)
    return z_part, last_r, last_l, x_part, x_sum


def summed(z_part, last_r, last_l, x_part, last_x):
    z_total = [z_part[h] + (last_r[h] + last_l[h]) for h in range(2)]
    if last_x.shape[0] == 3:
        z_total[1] = z_total[1] + last_x[2]
    return z_total + [x_part[h] + last_x[h] for h in range(2)]


def split_bf16(table):
    high = table.astype(np.float32).astype(ml_dtypes.bfloat16)
    low = (table - high.astype(np.float64)).astype(ml_dtypes.bfloat16)
    return high, low


@functools.lru_cache(None)
def tables(length):
    rows = length // BLOCK
    period = 2 * length
    odd = np.arange(rows) + 0.5
    first = -2 * np.pi * np.outer(odd, np.arange(rows)) / (2 * rows)
    turn = -2 * np.pi * np.outer(odd, np.arange(BLOCK)) / period
    second = -2 * np.pi * (np.outer(np.arange(BLOCK), np.arange(BLOCK)) % BLOCK) / BLOCK
    c, s = np.cos(second), np.sin(second)
    scale = 1.0 / length
    return (
        split_bf16(np.concatenate([np.cos(first), np.sin(first)], axis=0)),
        (np.cos(turn).astype(np.float32), np.sin(turn).astype(np.float32)),
        split_bf16(np.block([[c, s], [-s, c]])),
        split_bf16(np.block([[c, -s], [s, c]])),
        split_bf16(np.concatenate([np.cos(first).T, np.sin(first).T], axis=1) * scale),
    )


def split_value(value):
    high = value.astype(jnp.bfloat16)
    return high, (value - high.astype(jnp.float32)).astype(jnp.bfloat16)


def dot3(left, right):
    dot = functools.partial(jnp.dot, preferred_element_type=jnp.float32)
    return dot(left[0], right[0]) + (dot(left[0], right[1]) + dot(left[1], right[0]))


def forward(signal_ref, first, turn, second):
    seqs, channels = signal_ref.shape[:2]
    rows = seqs * signal_ref.shape[2]
    signal = jnp.concatenate(
        [signal_ref[:, c].reshape(rows, BLOCK) for c in range(channels)], axis=1
    )
    part = dot3(first, split_value(signal))
    turned = []
    for c in range(channels):
        real = part[:rows, c * BLOCK : (c + 1) * BLOCK]
        imag = part[rows:, c * BLOCK : (c + 1) * BLOCK]
        turned.append(
            jnp.concatenate(
                [real * turn[0] - imag * turn[1], real * turn[1] + imag * turn[0]], axis=1
            )
        )
    return dot3(split_value(jnp.concatenate(turned, axis=0)), second)


def taps_kernel(taps_ref, f_hi, f_lo, t_re, t_im, s_hi, s_lo, out_ref):
    out_ref[...] = forward(
        taps_ref, (f_hi[...], f_lo[...]), (t_re[...], t_im[...]), (s_hi[...], s_lo[...])
    )


def conv_kernel(
    kv_ref, spec_ref, f_hi, f_lo, t_re, t_im, s_hi, s_lo, b_hi, b_lo, i_hi, i_lo, out_ref
):
    seqs, channels, blocks, _ = kv_ref.shape
    rows = seqs * blocks
    turn = (t_re[...], t_im[...])
    spectrum = forward(kv_ref, (f_hi[...], f_lo[...]), turn, (s_hi[...], s_lo[...]))
    real, imag = spectrum[:, :BLOCK], spectrum[:, BLOCK:]
    taps_real, taps_imag = spec_ref[:, :BLOCK], spec_ref[:, BLOCK:]
    product = jnp.concatenate(
        [real * taps_real - imag * taps_imag, real * taps_imag + imag * taps_real], axis=1
    )
    back = dot3(split_value(product), (b_hi[...], b_lo[...]))
    columns = []
    for c in range(channels):
        real = back[c * rows : (c + 1) * rows, :BLOCK]
        imag = back[c * rows : (c + 1) * rows, BLOCK:]
        columns.append(
            jnp.concatenate(
                [real * turn[0] + imag * turn[1], imag * turn[0] - real * turn[1]], axis=0
            )
        )
    result = dot3((i_hi[...], i_lo[...]), split_value(jnp.concatenate(columns, axis=1)))
    for c in range(channels):
        out_ref[:, c] = result[:, c * BLOCK : (c + 1) * BLOCK].reshape(seqs, blocks, BLOCK)


def turn_blocks(value_ref, out_ref):
    for b in range(out_ref.shape[1]):
        out_ref[:, b, :] = value_ref[b * BLOCK : (b + 1) * BLOCK, :].T


def taps_turn_kernel(taps_ref, out_ref):
    turn_blocks(taps_ref, out_ref)


def kv_kernel(*refs):
    parts, out_ref, kv_ref = refs[:-2], refs[-2], refs[-1]
    z_key, z_value, x_key, x_value = summed(*parts)
    rows = z_key.shape[0]
    kv_ref[:rows] = z_key * z_value
    kv_ref[rows:] = x_key * x_value
    turn_blocks(kv_ref, out_ref)


def query_kernel(*refs):
    parts, out_ref = refs[:-1], refs[-1]
    for i, query in enumerate(summed(*parts)):
        rows = query.shape[0]
        out_ref[i * rows : (i + 1) * rows] = query


def gate_kernel(conv_ref, query_ref, out_ref):
    for b in range(conv_ref.shape[1]):
        rows = slice(b * BLOCK, (b + 1) * BLOCK)
        out_ref[rows] = conv_ref[:, b, :].T * query_ref[rows]


def call(kernel, out_shape, *operands, after=(), scratch=(), tables=(), to_hbm=False):
    def body(*refs):
        count = len(operands) + len(tables)
        kernel(*refs[:count], *refs[count + len(after) :])

    def whole(shape):
        return pl.BlockSpec(shape, lambda i: (0,) * len(shape))

    return pl.pallas_call(
        body,
        grid=(1,),
        in_specs=[pl.BlockSpec(memory_space=pltpu.VMEM)] * len(operands)
        + [whole(table.shape) for table in tables]
        + [pl.BlockSpec(memory_space=pl.ANY)] * len(after),
        out_specs=whole(out_shape) if to_hbm else pl.BlockSpec(memory_space=pltpu.VMEM),
        out_shape=pltpu.HBM(out_shape, jnp.float32)
        if to_hbm
        else jax.ShapeDtypeStruct(out_shape, jnp.float32),
        scratch_shapes=scratch,
        compiler_params=params(24),
        name=kernel.__name__,
    )(*operands, *[in_hbm(jnp.asarray(table)) for table in tables], *after)


def exchange(value):
    return lax.all_to_all(value, "seq", split_axis=0, concat_axis=0, tiled=True)


def on_device(activations, proj_weight, filter_taps):
    tokens, channels = filter_taps.shape
    seqs = lax.axis_size("seq")
    length = tokens * seqs
    blocks = tokens // BLOCK
    owned = channels // seqs
    turned_shape = (channels, blocks, BLOCK)
    moved_shape = (seqs, owned, blocks, BLOCK)
    first, turn, second, back, inverse = tables(length)

    chan = lax.axis_index("chan")
    x_at, z_at = chan // 2, chan % 2
    owners = [(x_at + dx) % X_SIZE for dx in (2, 1, 3, 0)]
    place = jnp.stack(owners + [z_at]).astype(jnp.int32)
    weight = in_hbm(jnp.transpose(proj_weight, (1, 0, 2)))
    activations = in_hbm(activations)

    hold = {}
    kv_halves, q_halves = Halves(tokens, (1, 2)), Halves(tokens, (0,))

    def prepare(ready, later):
        taps = call(taps_turn_kernel, turned_shape, filter_taps, after=(ready,), to_hbm=True)
        hold["taps"] = exchange(taps.reshape(moved_shape))
        hold["query"] = project_query(q_halves, place, activations, weight, (later,))
        return hold["taps"], hold["query"][0]

    kv_parts, kv_last = reduce_kv(kv_halves, place, activations, weight, prepare)
    spectrum = call(
        taps_kernel,
        (owned * length // BLOCK, 2 * BLOCK),
        hold["taps"],
        tables=first + turn + second,
        after=(kv_last,),
    )
    kv = call(
        kv_kernel,
        turned_shape,
        *kv_parts,
        after=(spectrum,),
        scratch=[pltpu.VMEM((tokens, channels), jnp.float32)],
        to_hbm=True,
    )
    q_parts = reduce_query(q_halves, hold["query"], kv_last)
    moved = exchange(kv.reshape(moved_shape))
    convolved = call(
        conv_kernel,
        moved_shape,
        moved,
        spectrum,
        tables=first + turn + second + back + inverse,
        to_hbm=True,
    )
    query = call(query_kernel, (tokens, channels), *q_parts)
    home = exchange(convolved).reshape(turned_shape)
    return call(gate_kernel, (tokens, channels), home, query)


def solution(mesh):
    return jax.shard_map(
        on_device,
        mesh=mesh,
        in_specs=(P("seq", "chan"), P("chan", None, None), P("seq", "chan")),
        out_specs=P("seq", "chan"),
        check_vma=False,
    )
```

```python
import functools

import jax
import jax.numpy as jnp
import ml_dtypes
import numpy as np
from jax import lax
from jax.experimental import pallas as pl
from jax.experimental.pallas import tpu as pltpu
from jax.sharding import PartitionSpec as P

BLOCK = 128
X_SIZE = 4
CHUNK = 256


def params(mebibytes):
    return pltpu.CompilerParams(vmem_limit_bytes=mebibytes * 1024 * 1024)


def in_hbm(value):
    return pltpu.with_memory_space_constraint(value, pltpu.HBM)


def shift_x(value, step):
    return lax.ppermute(value, "chan", [(i, (i + 2 * step) % 8) for i in range(8)])


def swap_z(value):
    return lax.ppermute(value, "chan", [(i, i ^ 1) for i in range(8)])


def parts_of(rows, weight, z_at):
    product = jnp.dot(rows, weight, preferred_element_type=jnp.float32)
    low, high = product[:, :BLOCK], product[:, BLOCK:]
    return jnp.where(z_at == 0, high, low), jnp.where(z_at == 0, low, high)


class Halves:
    def __init__(self, tokens, columns):
        self.columns = columns
        parts = 2 // len(columns)
        self.rows = tokens // 2 // parts
        self.z_start = [h % parts * self.rows for h in range(2)]
        self.x_start = [tokens // 2 + start for start in self.z_start]

    def shape(self, count):
        return (count, self.rows, BLOCK)

    def fill(self, place, act, weight, half, x_outs, z_outs):
        for begin, outs in ((self.x_start[half], x_outs), (self.z_start[half], z_outs)):
            if outs == (None, None):
                continue
            for start in range(0, self.rows, CHUNK):
                rows = act[begin + start : begin + start + CHUNK]
                for out, part in zip(outs, parts_of(rows, weight[0], place[4])):
                    if out is not None:
                        out[0][out[1], start : start + CHUNK] = part


def first_kernel(halves, place, act, weight, outs):
    send_r, send_l, z_other, z_mine = outs
    for half, send in enumerate((send_r, send_l)):
        pl.when(pl.program_id(0) == half)(
            functools.partial(
                halves.fill,
                place,
                act,
                weight,
                half,
                ((send, 0), (send, 1)),
                ((z_other, half), (z_mine, half)),
            )
        )


def second_kernel(halves, place, act, weight, outs):
    next_r, next_l, z_send = outs
    x_outs = (
        ((next_r, 2), (next_r, 3)),
        ((next_r, 0), (next_r, 1)),
        ((next_l, 0), (next_l, 1)),
        ((next_l, 2), (next_l, 3)),
        (None, None),
    )
    for i, outs in enumerate(x_outs):
        pl.when(pl.program_id(0) == i)(
            functools.partial(
                halves.fill, place, act, weight, i % 2, outs, ((z_send, i), None)
            )
        )


def third_kernel(halves, place, act, weight, outs):
    (mine,) = outs
    for i in range(6):
        x_outs = (None, None) if i < 4 else ((mine, i + 3), (mine, i + 5))
        z_other = (mine, 6) if i == 5 else None
        pl.when(pl.program_id(0) == i)(
            functools.partial(
                halves.fill, place, act, weight, i % 2, x_outs, (z_other, (mine, i))
            )
        )


def project(kernel, halves, place, activations, weight, owner, steps, outs, after=()):
    first, last = halves.columns[0], halves.columns[-1]

    def weight_block(i, at):
        return (first + (last - first) * (i % 2), 0, at[owner + i // 2])

    def body(at, act, weight_ref, *refs):
        kernel(halves, at, act, weight_ref, refs[len(after) :])

    specs, results = [], []
    for count, where in outs:
        if where == "vmem":
            specs.append(pl.BlockSpec(memory_space=pltpu.VMEM))
            results.append(jax.ShapeDtypeStruct(halves.shape(count), jnp.float32))
            continue
        results.append(pltpu.HBM(halves.shape(count), jnp.float32))
        if where == "hbm":
            specs.append(pl.BlockSpec(halves.shape(count), lambda i, at: (0, 0, 0)))
        else:
            specs.append(
                pl.BlockSpec(
                    halves.shape(1),
                    lambda i, at, start=where, end=count - 1: (
                        jnp.clip(i - start, 0, end),
                        0,
                        0,
                    ),
                )
            )
    return pl.pallas_call(
        body,
        grid_spec=pltpu.PrefetchScalarGridSpec(
            num_scalar_prefetch=1,
            grid=(steps,),
            in_specs=[
                pl.BlockSpec(activations.shape, lambda i, at: (0, 0)),
                pl.BlockSpec((1, weight.shape[1], 2 * BLOCK), weight_block),
            ]
            + [pl.BlockSpec(memory_space=pl.ANY)] * len(after),
            out_specs=specs,
        ),
        out_shape=results,
        compiler_params=params(24),
        name=kernel.__name__,
    )(place, activations, weight, *after)


def sum_call(kernel, halves, counts, near, far, after=()):
    tile = min(BLOCK, halves.rows)

    def body(*refs):
        rows = pl.ds(pl.multiple_of(pl.program_id(0) * tile, tile), tile)
        ins = [ref.at[:, rows] for ref in refs[: len(near)]]
        ins += refs[len(near) : len(near) + len(far)]
        kernel(*ins, *[ref.at[:, rows] for ref in refs[len(near) + len(far) + len(after) :]])

    return pl.pallas_call(
        body,
        grid=(halves.rows // tile,),
        in_specs=[pl.BlockSpec(memory_space=pltpu.VMEM)] * len(near)
        + [pl.BlockSpec((value.shape[0], tile, BLOCK), lambda i: (0, i, 0)) for value in far]
        + [pl.BlockSpec(memory_space=pl.ANY)] * len(after),
        out_specs=[pl.BlockSpec(memory_space=pltpu.VMEM)] * len(counts),
        out_shape=[jax.ShapeDtypeStruct(halves.shape(count), jnp.float32) for count in counts],
        compiler_params=params(8),
        name=kernel.__name__,
    )(*near, *[in_hbm(value) for value in far], *after)


def first_sum_kernel(got_r, got_l, z_got, keep_r, keep_l, z_mine, out_r, out_l):
    for half, (keep, got, out) in enumerate(((keep_r, got_r, out_r), (keep_l, got_l, out_l))):
        out[0] = keep[0] + got[0]
        out[1] = keep[1] + got[1]
        out[2] = z_mine[half] + z_got[half]


def kv_first_sum_kernel(got_r, got_l, z_got, next_r, next_l, z_mine, out_r, out_l):
    for half, (mine, got, out) in enumerate(((next_r, got_r, out_r), (next_l, got_l, out_l))):
        out[0] = mine[0]
        out[1] = mine[1]
        out[2] = mine[2] + got[0]
        out[3] = mine[3] + got[1]
        out[4] = z_mine[half] + z_got[half]


def kv_second_sum_kernel(next_r, next_l, z_got, mine, out_r, out_l, out_xz):
    out_r[0] = mine[0] + z_got[0] + next_r[4]
    out_r[1] = mine[1] + z_got[1]
    out_l[0] = mine[2] + z_got[2]
    out_l[1] = mine[3] + z_got[3] + next_l[4]
    out_xz[0] = mine[7] + (next_r[2] + next_l[0])
    out_xz[1] = mine[8] + (next_r[0] + next_l[2])
    out_xz[2] = mine[6]


def kv_beside_kernel(next_r, next_l, z_got, mine, out):
    out[0] = mine[4] + z_got[4]
    out[1] = mine[5]
    out[2] = mine[9] + (next_r[3] + next_l[1])
    out[3] = mine[10] + (next_r[1] + next_l[3])


def release(values, after):
    def body(*refs):
        pass

    count = len(values)
    return pl.pallas_call(
        body,
        in_specs=[pl.BlockSpec(memory_space=pl.ANY)] * (count + 1),
        out_specs=[pl.BlockSpec(memory_space=pl.ANY)] * count,
        out_shape=[pltpu.HBM(value.shape, value.dtype) for value in values],
        input_output_aliases={i: i for i in range(count)},
        name="release",
    )(*values, after)


def query_project_kernel(place, act, weight, *refs):
    send_r, send_l, keep_r, keep_l, z_send, z_next, z_late, z_mine, x_other, x_mine, product = refs[
        -11:
    ]
    product[...] = jnp.dot(act[...], weight[0], preferred_element_type=jnp.float32)

    def put(owner, other, mine):
        start = pl.multiple_of(place[owner] * 2 * BLOCK, 2 * BLOCK)
        columns = product[:, pl.ds(start, 2 * BLOCK)]
        low, high = columns[:, :BLOCK], columns[:, BLOCK:]
        other[0][other[1]] = jnp.where(place[4] == 0, high, low)
        mine[0][mine[1]] = jnp.where(place[4] == 0, low, high)

    def z_step(half):
        for owner in range(4):
            piece = 2 * owner + half
            put(owner, ((z_send, z_next, z_late)[piece // 3], piece % 3), (z_mine, piece))

    def x_step(half):
        far, right, left = (
            ((send_r, 0), (keep_r, 0), (send_l, 2)),
            ((send_l, 0), (send_r, 2), (keep_l, 0)),
        )[half]
        for owner, (ref, piece) in enumerate((far, right, left)):
            put(owner, (ref, piece), (ref, piece + 1))
        put(3, (x_other, half), (x_mine, half))

    for i in range(4):
        pl.when(pl.program_id(0) == i)(
            functools.partial(z_step if i < 2 else x_step, i % 2)
        )


def query_second_sum_kernel(
    dep_r, dep_l, got_r, got_l, z_got, z_next, z_mine, x_other, out_r, out_l, out_x
):
    out_r[0] = z_mine[2] + z_got[2] + dep_r[2]
    out_r[1] = z_mine[3] + z_next[0]
    out_l[0] = z_mine[4] + z_next[1]
    out_l[1] = z_mine[5] + z_next[2] + dep_l[2]
    out_x[0] = x_other[0] + (dep_r[0] + got_l[2])
    out_x[1] = x_other[1] + (got_r[2] + dep_l[0])


def query_beside_kernel(dep_r, dep_l, got_r, got_l, z_got, z_mine, x_mine, out):
    out[0] = z_mine[6] + z_got[0]
    out[1] = z_mine[7] + z_got[1]
    out[2] = x_mine[0] + (dep_r[1] + got_l[3])
    out[3] = x_mine[1] + (got_r[3] + dep_l[1])


def reduce_kv(halves, place, activations, weight, beside):
    make = functools.partial(
        project, halves=halves, place=place, activations=activations, weight=weight
    )
    send_r, send_l, z_send, z_mine = make(
        first_kernel, owner=0, steps=2, outs=[(2, "vmem")] * 4
    )
    got_r, got_l, z_got = shift_x(send_r, 1), shift_x(send_l, -1), swap_z(z_send)
    next_r, next_l, z_send = make(
        second_kernel, owner=1, steps=5, outs=[(5, "vmem")] * 3, after=(z_mine,)
    )
    next_r, next_l = sum_call(
        kv_first_sum_kernel, halves, [5, 5], [got_r, got_l, z_got, next_r, next_l, z_mine], []
    )
    ready = beside(next_r)
    (mine,) = make(
        third_kernel,
        owner=1,
        steps=6,
        outs=[(11, "vmem")],
        after=(next_r,) + ready[1:],
    )
    next_r, next_l, z_five = shift_x(next_r, 1), shift_x(next_l, -1), swap_z(z_send)
    last_r, last_l, last_xz = sum_call(
        kv_second_sum_kernel,
        halves,
        [2, 2, 3],
        [next_r, next_l, z_five, mine],
        [],
        after=ready,
    )
    last = last_r
    (part,) = sum_call(
        kv_beside_kernel,
        halves,
        [4],
        [next_r, next_l, z_five, mine],
        [],
        after=(last,),
    )
    last_r, last_l, last_xz = shift_x(last_r, 1), shift_x(last_l, -1), swap_z(last_xz)
    return (part, last_r, last_l, last_xz), part


def project_query(halves, place, activations, weight, after):
    features, columns = weight.shape[1:]
    shapes = [halves.shape(count) for count in (4, 4, 2, 2, 3, 3, 2, 8, 2, 2)]
    return pl.pallas_call(
        query_project_kernel,
        grid_spec=pltpu.PrefetchScalarGridSpec(
            num_scalar_prefetch=1,
            grid=(4,),
            in_specs=[
                pl.BlockSpec((halves.rows, features), lambda i, at: (i, 0)),
                pl.BlockSpec((1, features, columns), lambda i, at: (0, 0, 0)),
                pl.BlockSpec(memory_space=pl.ANY),
            ],
            out_specs=[pl.BlockSpec(shape, lambda i, at: (0, 0, 0)) for shape in shapes],
            scratch_shapes=[pltpu.VMEM((halves.rows, columns), jnp.float32)],
        ),
        out_shape=[pltpu.HBM(shape, jnp.float32) for shape in shapes],
        compiler_params=params(24),
        name="query_project_kernel",
    )(place, activations, weight, after)


def reduce_query(halves, projected, after):
    send_r, send_l, keep_r, keep_l, z_send, z_next, z_late, z_mine, x_other, x_mine = projected
    send_r, send_l, z_send, z_next = release((send_r, send_l, z_send, z_next), after)
    got_r, got_l, z_got = shift_x(send_r, 1), shift_x(send_l, -1), swap_z(z_send)
    z_next = swap_z(z_next)
    dep_r, dep_l = sum_call(
        first_sum_kernel,
        halves,
        [3, 3],
        [got_r, got_l, z_got],
        [keep_r, keep_l, z_mine],
    )
    (z_late,) = release((z_late,), dep_r)
    dep_r, dep_l, late_got = shift_x(dep_r, 1), shift_x(dep_l, -1), swap_z(z_late)
    last_r, last_l, x_sum = sum_call(
        query_second_sum_kernel,
        halves,
        [2, 2, 2],
        [dep_r, dep_l, got_r, got_l, z_got, z_next],
        [z_mine, x_other],
    )
    (part,) = sum_call(
        query_beside_kernel,
        halves,
        [4],
        [dep_r, dep_l, got_r, got_l, late_got],
        [z_mine, x_mine],
        after=(last_r,),
    )
    last_r, last_l, x_sum = shift_x(last_r, 1), shift_x(last_l, -1), swap_z(x_sum)
    return part, last_r, last_l, x_sum


def summed(part, last_r, last_l, last_x):
    z_total = [part[h] + (last_r[h] + last_l[h]) for h in range(2)]
    if last_x.shape[0] == 3:
        z_total[1] = z_total[1] + last_x[2]
    return z_total + [part[2 + h] + last_x[h] for h in range(2)]


def split_bf16(table):
    high = table.astype(np.float32).astype(ml_dtypes.bfloat16)
    low = (table - high.astype(np.float64)).astype(ml_dtypes.bfloat16)
    return high, low


@functools.lru_cache(None)
def tables(length):
    rows = length // BLOCK
    period = 2 * length
    odd = np.arange(rows) + 0.5
    first = -2 * np.pi * np.outer(odd, np.arange(rows)) / (2 * rows)
    turn = -2 * np.pi * np.outer(odd, np.arange(BLOCK)) / period
    second = -2 * np.pi * (np.outer(np.arange(BLOCK), np.arange(BLOCK)) % BLOCK) / BLOCK
    c, s = np.cos(second), np.sin(second)
    scale = 1.0 / length
    return (
        split_bf16(np.concatenate([np.cos(first), np.sin(first)], axis=0)),
        (np.cos(turn).astype(np.float32), np.sin(turn).astype(np.float32)),
        split_bf16(np.block([[c, s], [-s, c]])),
        split_bf16(np.block([[c, -s], [s, c]])),
        split_bf16(np.concatenate([np.cos(first).T, np.sin(first).T], axis=1) * scale),
    )


def split_value(value):
    high = value.astype(jnp.bfloat16)
    return high, (value - high.astype(jnp.float32)).astype(jnp.bfloat16)


def dot3(left, right):
    dot = functools.partial(jnp.dot, preferred_element_type=jnp.float32)
    return dot(left[0], right[0]) + (dot(left[0], right[1]) + dot(left[1], right[0]))


def forward(signal_ref, first, turn, second):
    seqs, channels = signal_ref.shape[:2]
    rows = seqs * signal_ref.shape[2]
    signal = jnp.concatenate(
        [signal_ref[:, c].reshape(rows, BLOCK) for c in range(channels)], axis=1
    )
    part = dot3(first, split_value(signal))
    turned = []
    for c in range(channels):
        real = part[:rows, c * BLOCK : (c + 1) * BLOCK]
        imag = part[rows:, c * BLOCK : (c + 1) * BLOCK]
        turned.append(
            jnp.concatenate(
                [real * turn[0] - imag * turn[1], real * turn[1] + imag * turn[0]], axis=1
            )
        )
    return dot3(split_value(jnp.concatenate(turned, axis=0)), second)


def taps_kernel(taps_ref, f_hi, f_lo, t_re, t_im, s_hi, s_lo, out_ref):
    out_ref[...] = forward(
        taps_ref, (f_hi[...], f_lo[...]), (t_re[...], t_im[...]), (s_hi[...], s_lo[...])
    )


def conv_kernel(
    kv_ref, spec_ref, f_hi, f_lo, t_re, t_im, s_hi, s_lo, b_hi, b_lo, i_hi, i_lo, out_ref
):
    seqs, channels, blocks, _ = kv_ref.shape
    rows = seqs * blocks
    turn = (t_re[...], t_im[...])
    spectrum = forward(kv_ref, (f_hi[...], f_lo[...]), turn, (s_hi[...], s_lo[...]))
    real, imag = spectrum[:, :BLOCK], spectrum[:, BLOCK:]
    taps_real, taps_imag = spec_ref[:, :BLOCK], spec_ref[:, BLOCK:]
    product = jnp.concatenate(
        [real * taps_real - imag * taps_imag, real * taps_imag + imag * taps_real], axis=1
    )
    back = dot3(split_value(product), (b_hi[...], b_lo[...]))
    columns = []
    for c in range(channels):
        real = back[c * rows : (c + 1) * rows, :BLOCK]
        imag = back[c * rows : (c + 1) * rows, BLOCK:]
        columns.append(
            jnp.concatenate(
                [real * turn[0] + imag * turn[1], imag * turn[0] - real * turn[1]], axis=0
            )
        )
    result = dot3((i_hi[...], i_lo[...]), split_value(jnp.concatenate(columns, axis=1)))
    for c in range(channels):
        out_ref[:, c] = result[:, c * BLOCK : (c + 1) * BLOCK].reshape(seqs, blocks, BLOCK)


def turn_blocks(value_ref, out_ref):
    for b in range(out_ref.shape[1]):
        out_ref[:, b, :] = value_ref[b * BLOCK : (b + 1) * BLOCK, :].T


def taps_turn_kernel(taps_ref, out_ref):
    turn_blocks(taps_ref, out_ref)


def kv_kernel(*refs):
    parts, out_ref, kv_ref = refs[:-2], refs[-2], refs[-1]
    z_key, z_value, x_key, x_value = summed(*parts)
    rows = z_key.shape[0]
    kv_ref[:rows] = z_key * z_value
    kv_ref[rows:] = x_key * x_value
    turn_blocks(kv_ref, out_ref)


def query_kernel(*refs):
    parts, out_ref = refs[:-1], refs[-1]
    for i, query in enumerate(summed(*parts)):
        rows = query.shape[0]
        out_ref[i * rows : (i + 1) * rows] = query


def gate_kernel(conv_ref, query_ref, out_ref):
    for b in range(conv_ref.shape[1]):
        rows = slice(b * BLOCK, (b + 1) * BLOCK)
        out_ref[rows] = conv_ref[:, b, :].T * query_ref[rows]


def call(kernel, out_shape, *operands, after=(), scratch=(), tables=(), to_hbm=False):
    def body(*refs):
        count = len(operands) + len(tables)
        kernel(*refs[:count], *refs[count + len(after) :])

    def whole(shape):
        return pl.BlockSpec(shape, lambda i: (0,) * len(shape))

    return pl.pallas_call(
        body,
        grid=(1,),
        in_specs=[pl.BlockSpec(memory_space=pltpu.VMEM)] * len(operands)
        + [whole(table.shape) for table in tables]
        + [pl.BlockSpec(memory_space=pl.ANY)] * len(after),
        out_specs=whole(out_shape) if to_hbm else pl.BlockSpec(memory_space=pltpu.VMEM),
        out_shape=pltpu.HBM(out_shape, jnp.float32)
        if to_hbm
        else jax.ShapeDtypeStruct(out_shape, jnp.float32),
        scratch_shapes=scratch,
        compiler_params=params(24),
        name=kernel.__name__,
    )(*operands, *[in_hbm(jnp.asarray(table)) for table in tables], *after)


def exchange(value):
    return lax.all_to_all(value, "seq", split_axis=0, concat_axis=0, tiled=True)


def on_device(activations, proj_weight, filter_taps):
    tokens, channels = filter_taps.shape
    seqs = lax.axis_size("seq")
    length = tokens * seqs
    blocks = tokens // BLOCK
    owned = channels // seqs
    turned_shape = (channels, blocks, BLOCK)
    moved_shape = (seqs, owned, blocks, BLOCK)
    first, turn, second, back, inverse = tables(length)

    chan = lax.axis_index("chan")
    x_at, z_at = chan // 2, chan % 2
    owners = [(x_at + dx) % X_SIZE for dx in (2, 1, 3, 0)]
    place = jnp.stack(owners + [z_at]).astype(jnp.int32)
    weight = in_hbm(jnp.transpose(proj_weight, (1, 0, 2)))
    activations = in_hbm(activations)

    hold = {}
    kv_halves, q_halves = Halves(tokens, (1, 2)), Halves(tokens, (0,))

    def prepare(ready):
        taps = call(taps_turn_kernel, turned_shape, filter_taps, after=(ready,), to_hbm=True)
        hold["taps"] = exchange(taps.reshape(moved_shape))
        hold["query"] = project_query(q_halves, place, activations, weight, ready)
        return hold["taps"], hold["query"][0]

    kv_parts, kv_part = reduce_kv(kv_halves, place, activations, weight, prepare)
    spectrum = call(
        taps_kernel,
        (owned * length // BLOCK, 2 * BLOCK),
        hold["taps"],
        tables=first + turn + second,
        after=(kv_part,),
        to_hbm=True,
    )
    kv = call(
        kv_kernel,
        turned_shape,
        *kv_parts,
        after=(spectrum,),
        scratch=[pltpu.VMEM((tokens, channels), jnp.float32)],
        to_hbm=True,
    )
    q_parts = reduce_query(q_halves, hold["query"], spectrum)
    moved = exchange(kv.reshape(moved_shape))
    convolved = call(
        conv_kernel,
        moved_shape,
        moved,
        tables=(spectrum,) + first + turn + second + back + inverse,
        to_hbm=True,
    )
    query = call(query_kernel, (tokens, channels), *q_parts)
    home = exchange(convolved).reshape(turned_shape)
    return call(gate_kernel, (tokens, channels), home, query)


def solution(mesh):
    return jax.shard_map(
        on_device,
        mesh=mesh,
        in_specs=(P("seq", "chan"), P("chan", None, None), P("seq", "chan")),
        out_specs=P("seq", "chan"),
        check_vma=False,
    )
```

```python
import functools

import jax
import jax.numpy as jnp
import ml_dtypes
import numpy as np
from jax import lax
from jax.experimental import pallas as pl
from jax.experimental.pallas import tpu as pltpu
from jax.sharding import PartitionSpec as P

BLOCK = 128
X_SIZE = 4
CHUNK = 512


def params(mebibytes):
    return pltpu.CompilerParams(vmem_limit_bytes=mebibytes * 1024 * 1024)


def in_hbm(value):
    return pltpu.with_memory_space_constraint(value, pltpu.HBM)


def shift_x(value, step):
    return lax.ppermute(value, "chan", [(i, (i + 2 * step) % 8) for i in range(8)])


def swap_z(value):
    return lax.ppermute(value, "chan", [(i, i ^ 1) for i in range(8)])


def parts_of(rows, weight, z_at):
    product = jnp.dot(rows, weight, preferred_element_type=jnp.float32)
    low, high = product[:, :BLOCK], product[:, BLOCK:]
    return jnp.where(z_at == 0, high, low), jnp.where(z_at == 0, low, high)


class Halves:
    def __init__(self, tokens, columns):
        self.columns = columns
        parts = 2 // len(columns)
        self.rows = tokens // 2 // parts
        self.z_start = [h % parts * self.rows for h in range(2)]
        self.x_start = [tokens // 2 + start for start in self.z_start]

    def shape(self, count):
        return (count, self.rows, BLOCK)

    def fill(self, place, act, weight, half, x_outs, z_outs):
        for begin, outs in ((self.x_start[half], x_outs), (self.z_start[half], z_outs)):
            if outs == (None, None):
                continue
            for start in range(0, self.rows, CHUNK):
                rows = act[begin + start : begin + start + CHUNK]
                for out, part in zip(outs, parts_of(rows, weight[0], place[4])):
                    if out is not None:
                        out[0][out[1], start : start + CHUNK] = part


def first_kernel(halves, place, act, weight, outs):
    send_r, send_l, z_other, z_mine = outs
    for half, send in enumerate((send_r, send_l)):
        pl.when(pl.program_id(0) == half)(
            functools.partial(
                halves.fill,
                place,
                act,
                weight,
                half,
                ((send, 0), (send, 1)),
                ((z_other, half), (z_mine, half)),
            )
        )


def second_kernel(halves, place, act, weight, outs):
    next_r, next_l, z_send = outs
    x_outs = (
        ((next_r, 2), (next_r, 3)),
        ((next_r, 0), (next_r, 1)),
        ((next_l, 0), (next_l, 1)),
        ((next_l, 2), (next_l, 3)),
        (None, None),
    )
    for i, outs in enumerate(x_outs):
        pl.when(pl.program_id(0) == i)(
            functools.partial(
                halves.fill, place, act, weight, i % 2, outs, ((z_send, i), None)
            )
        )


def third_kernel(halves, place, act, weight, outs):
    (mine,) = outs
    for i in range(6):
        x_outs = (None, None) if i < 4 else ((mine, i + 3), (mine, i + 5))
        z_other = (mine, 6) if i == 5 else None
        pl.when(pl.program_id(0) == i)(
            functools.partial(
                halves.fill, place, act, weight, i % 2, x_outs, (z_other, (mine, i))
            )
        )


def project(kernel, halves, place, activations, weight, owner, steps, outs, after=()):
    first, last = halves.columns[0], halves.columns[-1]

    def weight_block(i, at):
        return (first + (last - first) * (i % 2), 0, at[owner + i // 2])

    def body(at, act, weight_ref, *refs):
        kernel(halves, at, act, weight_ref, refs[len(after) :])

    specs, results = [], []
    for count, where in outs:
        if where == "vmem":
            specs.append(pl.BlockSpec(memory_space=pltpu.VMEM))
            results.append(jax.ShapeDtypeStruct(halves.shape(count), jnp.float32))
            continue
        results.append(pltpu.HBM(halves.shape(count), jnp.float32))
        if where == "hbm":
            specs.append(pl.BlockSpec(halves.shape(count), lambda i, at: (0, 0, 0)))
        else:
            specs.append(
                pl.BlockSpec(
                    halves.shape(1),
                    lambda i, at, start=where, end=count - 1: (
                        jnp.clip(i - start, 0, end),
                        0,
                        0,
                    ),
                )
            )
    return pl.pallas_call(
        body,
        grid_spec=pltpu.PrefetchScalarGridSpec(
            num_scalar_prefetch=1,
            grid=(steps,),
            in_specs=[
                pl.BlockSpec(activations.shape, lambda i, at: (0, 0)),
                pl.BlockSpec((1, weight.shape[1], 2 * BLOCK), weight_block),
            ]
            + [pl.BlockSpec(memory_space=pl.ANY)] * len(after),
            out_specs=specs,
        ),
        out_shape=results,
        compiler_params=params(24),
        name=kernel.__name__,
    )(place, activations, weight, *after)


def sum_call(kernel, halves, counts, near, far, after=()):
    tile = min(BLOCK, halves.rows)

    def body(*refs):
        rows = pl.ds(pl.multiple_of(pl.program_id(0) * tile, tile), tile)
        ins = [ref.at[:, rows] for ref in refs[: len(near)]]
        ins += refs[len(near) : len(near) + len(far)]
        kernel(*ins, *[ref.at[:, rows] for ref in refs[len(near) + len(far) + len(after) :]])

    return pl.pallas_call(
        body,
        grid=(halves.rows // tile,),
        in_specs=[pl.BlockSpec(memory_space=pltpu.VMEM)] * len(near)
        + [pl.BlockSpec((value.shape[0], tile, BLOCK), lambda i: (0, i, 0)) for value in far]
        + [pl.BlockSpec(memory_space=pl.ANY)] * len(after),
        out_specs=[pl.BlockSpec(memory_space=pltpu.VMEM)] * len(counts),
        out_shape=[jax.ShapeDtypeStruct(halves.shape(count), jnp.float32) for count in counts],
        compiler_params=params(8),
        name=kernel.__name__,
    )(*near, *[in_hbm(value) for value in far], *after)


def first_sum_kernel(got_r, got_l, z_got, keep_r, keep_l, z_mine, out_r, out_l):
    for half, (keep, got, out) in enumerate(((keep_r, got_r, out_r), (keep_l, got_l, out_l))):
        out[0] = keep[0] + got[0]
        out[1] = keep[1] + got[1]
        out[2] = z_mine[half] + z_got[half]


def kv_first_sum_kernel(got_r, got_l, z_got, next_r, next_l, z_mine, out_r, out_l):
    for half, (mine, got, out) in enumerate(((next_r, got_r, out_r), (next_l, got_l, out_l))):
        out[0] = mine[0]
        out[1] = mine[1]
        out[2] = mine[2] + got[0]
        out[3] = mine[3] + got[1]
        out[4] = z_mine[half] + z_got[half]


def kv_second_sum_kernel(next_r, next_l, z_got, mine, out_r, out_l, out_xz):
    out_r[0] = mine[0] + z_got[0] + next_r[4]
    out_r[1] = mine[1] + z_got[1]
    out_l[0] = mine[2] + z_got[2]
    out_l[1] = mine[3] + z_got[3] + next_l[4]
    out_xz[0] = mine[7] + (next_r[2] + next_l[0])
    out_xz[1] = mine[8] + (next_r[0] + next_l[2])
    out_xz[2] = mine[6]


def kv_beside_kernel(next_r, next_l, z_got, mine, out):
    out[0] = mine[4] + z_got[4]
    out[1] = mine[5]
    out[2] = mine[9] + (next_r[3] + next_l[1])
    out[3] = mine[10] + (next_r[1] + next_l[3])


def release(values, after):
    def body(*refs):
        pass

    count = len(values)
    return pl.pallas_call(
        body,
        in_specs=[pl.BlockSpec(memory_space=pl.ANY)] * (count + 1),
        out_specs=[pl.BlockSpec(memory_space=pl.ANY)] * count,
        out_shape=[pltpu.HBM(value.shape, value.dtype) for value in values],
        input_output_aliases={i: i for i in range(count)},
        name="release",
    )(*values, after)


def query_project_kernel(place, act, weight, *refs):
    send_r, send_l, keep_r, keep_l, z_send, z_next, z_mine, x_other, x_mine, product = refs[-10:]
    product[...] = jnp.dot(act[...], weight[0], preferred_element_type=jnp.float32)

    def put(owner, other, mine):
        start = pl.multiple_of(place[owner] * 2 * BLOCK, 2 * BLOCK)
        columns = product[:, pl.ds(start, 2 * BLOCK)]
        low, high = columns[:, :BLOCK], columns[:, BLOCK:]
        other[0][other[1]] = jnp.where(place[4] == 0, high, low)
        mine[0][mine[1]] = jnp.where(place[4] == 0, low, high)

    def z_step(half):
        for owner in range(4):
            piece = 2 * owner + half
            other = (z_send, piece) if piece < 3 else (z_next, piece - 3)
            put(owner, other, (z_mine, piece))

    def x_step(half):
        far, right, left = (
            ((send_r, 0), (keep_r, 0), (send_l, 2)),
            ((send_l, 0), (send_r, 2), (keep_l, 0)),
        )[half]
        for owner, (ref, piece) in enumerate((far, right, left)):
            put(owner, (ref, piece), (ref, piece + 1))
        put(3, (x_other, half), (x_mine, half))

    for i in range(4):
        pl.when(pl.program_id(0) == i)(
            functools.partial(z_step if i < 2 else x_step, i % 2)
        )


def query_second_sum_kernel(
    dep_r, dep_l, got_r, got_l, z_got, z_next, z_mine, x_other, out_r, out_l, out_x
):
    out_r[0] = z_mine[2] + z_got[2] + dep_r[2]
    out_r[1] = z_mine[3] + z_next[0]
    out_l[0] = z_mine[4] + z_next[1]
    out_l[1] = z_mine[5] + z_next[2] + dep_l[2]
    out_x[0] = x_other[0] + (dep_r[0] + got_l[2])
    out_x[1] = x_other[1] + (got_r[2] + dep_l[0])


def query_beside_kernel(dep_r, dep_l, got_r, got_l, z_next, z_mine, x_mine, out):
    out[0] = z_mine[6] + z_next[3]
    out[1] = z_mine[7] + z_next[4]
    out[2] = x_mine[0] + (dep_r[1] + got_l[3])
    out[3] = x_mine[1] + (got_r[3] + dep_l[1])


def reduce_kv(halves, place, activations, weight, beside):
    make = functools.partial(
        project, halves=halves, place=place, activations=activations, weight=weight
    )
    send_r, send_l, z_send, z_mine = make(
        first_kernel, owner=0, steps=2, outs=[(2, "vmem")] * 4
    )
    got_r, got_l, z_got = shift_x(send_r, 1), shift_x(send_l, -1), swap_z(z_send)
    next_r, next_l, z_send = make(
        second_kernel, owner=1, steps=5, outs=[(5, "vmem")] * 3, after=(z_mine,)
    )
    next_r, next_l = sum_call(
        kv_first_sum_kernel, halves, [5, 5], [got_r, got_l, z_got, next_r, next_l, z_mine], []
    )
    ready = beside(next_r)
    (mine,) = make(
        third_kernel,
        owner=1,
        steps=6,
        outs=[(11, "vmem")],
        after=(next_r,) + ready[1:],
    )
    next_r, next_l, z_five = shift_x(next_r, 1), shift_x(next_l, -1), swap_z(z_send)
    last_r, last_l, last_xz = sum_call(
        kv_second_sum_kernel,
        halves,
        [2, 2, 3],
        [next_r, next_l, z_five, mine],
        [],
        after=ready,
    )
    last = last_r
    (part,) = sum_call(
        kv_beside_kernel,
        halves,
        [4],
        [next_r, next_l, z_five, mine],
        [],
        after=(last,),
    )
    last_r, last_l, last_xz = shift_x(last_r, 1), shift_x(last_l, -1), swap_z(last_xz)
    return (part, last_r, last_l, last_xz), part


def project_query(halves, place, activations, weight, after):
    features, columns = weight.shape[1:]
    shapes = [halves.shape(count) for count in (4, 4, 2, 2, 3, 5, 8, 2, 2)]
    return pl.pallas_call(
        query_project_kernel,
        grid_spec=pltpu.PrefetchScalarGridSpec(
            num_scalar_prefetch=1,
            grid=(4,),
            in_specs=[
                pl.BlockSpec((halves.rows, features), lambda i, at: (i, 0)),
                pl.BlockSpec((1, features, columns), lambda i, at: (0, 0, 0)),
                pl.BlockSpec(memory_space=pl.ANY),
            ],
            out_specs=[pl.BlockSpec(shape, lambda i, at: (0, 0, 0)) for shape in shapes],
            scratch_shapes=[pltpu.VMEM((halves.rows, columns), jnp.float32)],
        ),
        out_shape=[pltpu.HBM(shape, jnp.float32) for shape in shapes],
        compiler_params=params(24),
        name="query_project_kernel",
    )(place, activations, weight, after)


def reduce_query(halves, projected, after):
    send_r, send_l, keep_r, keep_l, z_send, z_next, z_mine, x_other, x_mine = projected
    send_r, send_l, z_send, z_next = release((send_r, send_l, z_send, z_next), after)
    got_r, got_l, z_got = shift_x(send_r, 1), shift_x(send_l, -1), swap_z(z_send)
    z_next = swap_z(z_next)
    dep_r, dep_l = sum_call(
        first_sum_kernel,
        halves,
        [3, 3],
        [got_r, got_l, z_got],
        [keep_r, keep_l, z_mine],
    )
    dep_r, dep_l = shift_x(dep_r, 1), shift_x(dep_l, -1)
    last_r, last_l, x_sum = sum_call(
        query_second_sum_kernel,
        halves,
        [2, 2, 2],
        [dep_r, dep_l, got_r, got_l, z_got, z_next],
        [z_mine, x_other],
    )
    (part,) = sum_call(
        query_beside_kernel,
        halves,
        [4],
        [dep_r, dep_l, got_r, got_l, z_next],
        [z_mine, x_mine],
        after=(last_r,),
    )
    last_r, last_l, x_sum = shift_x(last_r, 1), shift_x(last_l, -1), swap_z(x_sum)
    return part, last_r, last_l, x_sum


def summed(part, last_r, last_l, last_x):
    z_total = [part[h] + (last_r[h] + last_l[h]) for h in range(2)]
    if last_x.shape[0] == 3:
        z_total[1] = z_total[1] + last_x[2]
    return z_total + [part[2 + h] + last_x[h] for h in range(2)]


def split_bf16(table):
    high = table.astype(np.float32).astype(ml_dtypes.bfloat16)
    low = (table - high.astype(np.float64)).astype(ml_dtypes.bfloat16)
    return high, low


@functools.lru_cache(None)
def tables(length):
    rows = length // BLOCK
    period = 2 * length
    odd = np.arange(rows) + 0.5
    first = -2 * np.pi * np.outer(odd, np.arange(rows)) / (2 * rows)
    turn = -2 * np.pi * np.outer(odd, np.arange(BLOCK)) / period
    second = -2 * np.pi * (np.outer(np.arange(BLOCK), np.arange(BLOCK)) % BLOCK) / BLOCK
    c, s = np.cos(second), np.sin(second)
    scale = 1.0 / length
    return (
        split_bf16(np.concatenate([np.cos(first), np.sin(first)], axis=0)),
        (np.cos(turn).astype(np.float32), np.sin(turn).astype(np.float32)),
        split_bf16(np.block([[c, s], [-s, c]])),
        split_bf16(np.block([[c, -s], [s, c]])),
        split_bf16(np.concatenate([np.cos(first).T, np.sin(first).T], axis=1) * scale),
    )


def split_value(value):
    high = value.astype(jnp.bfloat16)
    return high, (value - high.astype(jnp.float32)).astype(jnp.bfloat16)


def dot3(left, right):
    dot = functools.partial(jnp.dot, preferred_element_type=jnp.float32)
    return dot(left[0], right[0]) + (dot(left[0], right[1]) + dot(left[1], right[0]))


def forward(signal_ref, first, turn, second):
    seqs, channels = signal_ref.shape[:2]
    rows = seqs * signal_ref.shape[2]
    signal = jnp.concatenate(
        [signal_ref[:, c].reshape(rows, BLOCK) for c in range(channels)], axis=1
    )
    part = dot3(first, split_value(signal))
    turned = []
    for c in range(channels):
        real = part[:rows, c * BLOCK : (c + 1) * BLOCK]
        imag = part[rows:, c * BLOCK : (c + 1) * BLOCK]
        turned.append(
            jnp.concatenate(
                [real * turn[0] - imag * turn[1], real * turn[1] + imag * turn[0]], axis=1
            )
        )
    return dot3(split_value(jnp.concatenate(turned, axis=0)), second)


def taps_kernel(taps_ref, f_hi, f_lo, t_re, t_im, s_hi, s_lo, out_ref):
    out_ref[...] = forward(
        taps_ref, (f_hi[...], f_lo[...]), (t_re[...], t_im[...]), (s_hi[...], s_lo[...])
    )


def conv_kernel(
    kv_ref, spec_ref, f_hi, f_lo, t_re, t_im, s_hi, s_lo, b_hi, b_lo, i_hi, i_lo, out_ref
):
    seqs, channels, blocks, _ = kv_ref.shape
    rows = seqs * blocks
    turn = (t_re[...], t_im[...])
    spectrum = forward(kv_ref, (f_hi[...], f_lo[...]), turn, (s_hi[...], s_lo[...]))
    real, imag = spectrum[:, :BLOCK], spectrum[:, BLOCK:]
    taps_real, taps_imag = spec_ref[:, :BLOCK], spec_ref[:, BLOCK:]
    product = jnp.concatenate(
        [real * taps_real - imag * taps_imag, real * taps_imag + imag * taps_real], axis=1
    )
    back = dot3(split_value(product), (b_hi[...], b_lo[...]))
    columns = []
    for c in range(channels):
        real = back[c * rows : (c + 1) * rows, :BLOCK]
        imag = back[c * rows : (c + 1) * rows, BLOCK:]
        columns.append(
            jnp.concatenate(
                [real * turn[0] + imag * turn[1], imag * turn[0] - real * turn[1]], axis=0
            )
        )
    result = dot3((i_hi[...], i_lo[...]), split_value(jnp.concatenate(columns, axis=1)))
    for c in range(channels):
        out_ref[:, c] = result[:, c * BLOCK : (c + 1) * BLOCK].reshape(seqs, blocks, BLOCK)


def turn_blocks(value_ref, out_ref):
    for b in range(out_ref.shape[1]):
        out_ref[:, b, :] = value_ref[b * BLOCK : (b + 1) * BLOCK, :].T


def taps_turn_kernel(taps_ref, out_ref):
    turn_blocks(taps_ref, out_ref)


def kv_kernel(*refs):
    parts, out_ref, kv_ref = refs[:-2], refs[-2], refs[-1]
    z_key, z_value, x_key, x_value = summed(*parts)
    rows = z_key.shape[0]
    kv_ref[:rows] = z_key * z_value
    kv_ref[rows:] = x_key * x_value
    turn_blocks(kv_ref, out_ref)


def query_kernel(*refs):
    parts, out_ref = refs[:-1], refs[-1]
    for i, query in enumerate(summed(*parts)):
        rows = query.shape[0]
        out_ref[i * rows : (i + 1) * rows] = query


def gate_kernel(conv_ref, query_ref, out_ref):
    for b in range(conv_ref.shape[1]):
        rows = slice(b * BLOCK, (b + 1) * BLOCK)
        out_ref[rows] = conv_ref[:, b, :].T * query_ref[rows]


def call(kernel, out_shape, *operands, after=(), scratch=(), tables=(), to_hbm=False):
    def body(*refs):
        count = len(operands) + len(tables)
        kernel(*refs[:count], *refs[count + len(after) :])

    def whole(shape):
        return pl.BlockSpec(shape, lambda i: (0,) * len(shape))

    return pl.pallas_call(
        body,
        grid=(1,),
        in_specs=[pl.BlockSpec(memory_space=pltpu.VMEM)] * len(operands)
        + [whole(table.shape) for table in tables]
        + [pl.BlockSpec(memory_space=pl.ANY)] * len(after),
        out_specs=whole(out_shape) if to_hbm else pl.BlockSpec(memory_space=pltpu.VMEM),
        out_shape=pltpu.HBM(out_shape, jnp.float32)
        if to_hbm
        else jax.ShapeDtypeStruct(out_shape, jnp.float32),
        scratch_shapes=scratch,
        compiler_params=params(24),
        name=kernel.__name__,
    )(*operands, *[in_hbm(jnp.asarray(table)) for table in tables], *after)


def exchange(value):
    return lax.all_to_all(value, "seq", split_axis=0, concat_axis=0, tiled=True)


def on_device(activations, proj_weight, filter_taps):
    tokens, channels = filter_taps.shape
    seqs = lax.axis_size("seq")
    length = tokens * seqs
    blocks = tokens // BLOCK
    owned = channels // seqs
    turned_shape = (channels, blocks, BLOCK)
    moved_shape = (seqs, owned, blocks, BLOCK)
    first, turn, second, back, inverse = tables(length)

    chan = lax.axis_index("chan")
    x_at, z_at = chan // 2, chan % 2
    owners = [(x_at + dx) % X_SIZE for dx in (2, 1, 3, 0)]
    place = jnp.stack(owners + [z_at]).astype(jnp.int32)
    weight = in_hbm(jnp.transpose(proj_weight, (1, 0, 2)))
    activations = in_hbm(activations)

    hold = {}
    kv_halves, q_halves = Halves(tokens, (1, 2)), Halves(tokens, (0,))

    def prepare(ready):
        taps = call(taps_turn_kernel, turned_shape, filter_taps, after=(ready,), to_hbm=True)
        hold["taps"] = exchange(taps.reshape(moved_shape))
        hold["query"] = project_query(q_halves, place, activations, weight, ready)
        return hold["taps"], hold["query"][0]

    kv_parts, kv_part = reduce_kv(kv_halves, place, activations, weight, prepare)
    spectrum = call(
        taps_kernel,
        (owned * length // BLOCK, 2 * BLOCK),
        hold["taps"],
        tables=first + turn + second,
        after=(kv_part,),
        to_hbm=True,
    )
    kv = call(
        kv_kernel,
        turned_shape,
        *kv_parts,
        after=(spectrum,),
        scratch=[pltpu.VMEM((tokens, channels), jnp.float32)],
        to_hbm=True,
    )
    q_parts = reduce_query(q_halves, hold["query"], spectrum)
    moved = exchange(kv.reshape(moved_shape))
    convolved = call(
        conv_kernel,
        moved_shape,
        moved,
        tables=(spectrum,) + first + turn + second + back + inverse,
        to_hbm=True,
    )
    query = call(query_kernel, (tokens, channels), *q_parts)
    home = exchange(convolved).reshape(turned_shape)
    return call(gate_kernel, (tokens, channels), home, query)


def solution(mesh):
    return jax.shard_map(
        on_device,
        mesh=mesh,
        in_specs=(P("seq", "chan"), P("chan", None, None), P("seq", "chan")),
        out_specs=P("seq", "chan"),
        check_vma=False,
    )
```

```python
import functools

import jax
import jax.numpy as jnp
import ml_dtypes
import numpy as np
from jax import lax
from jax.experimental import pallas as pl
from jax.experimental.pallas import tpu as pltpu
from jax.sharding import PartitionSpec as P

BLOCK = 128
X_SIZE = 4
CHUNK = 512


def params(mebibytes):
    return pltpu.CompilerParams(vmem_limit_bytes=mebibytes * 1024 * 1024)


def in_hbm(value):
    return pltpu.with_memory_space_constraint(value, pltpu.HBM)


def shift_x(value, step):
    return lax.ppermute(value, "chan", [(i, (i + 2 * step) % 8) for i in range(8)])


def swap_z(value):
    return lax.ppermute(value, "chan", [(i, i ^ 1) for i in range(8)])


def parts_of(rows, weight, z_at):
    product = jnp.dot(rows, weight, preferred_element_type=jnp.float32)
    low, high = product[:, :BLOCK], product[:, BLOCK:]
    return jnp.where(z_at == 0, high, low), jnp.where(z_at == 0, low, high)


class Halves:
    def __init__(self, tokens, columns):
        self.columns = columns
        parts = 2 // len(columns)
        self.rows = tokens // 2 // parts
        self.z_start = [h % parts * self.rows for h in range(2)]
        self.x_start = [tokens // 2 + start for start in self.z_start]

    def shape(self, count):
        return (count, self.rows, BLOCK)

    def fill(self, place, act, weight, half, x_outs, z_outs):
        for begin, outs in ((self.x_start[half], x_outs), (self.z_start[half], z_outs)):
            if outs == (None, None):
                continue
            for start in range(0, self.rows, CHUNK):
                rows = act[begin + start : begin + start + CHUNK]
                for out, part in zip(outs, parts_of(rows, weight[0], place[4])):
                    if out is not None:
                        out[0][out[1], start : start + CHUNK] = part


def first_kernel(halves, place, act, weight, outs):
    send_r, send_l, z_other, z_mine = outs
    for half, send in enumerate((send_r, send_l)):
        pl.when(pl.program_id(0) == half)(
            functools.partial(
                halves.fill,
                place,
                act,
                weight,
                half,
                ((send, 0), (send, 1)),
                ((z_other, half), (z_mine, half)),
            )
        )


def second_kernel(halves, place, act, weight, outs):
    next_r, next_l, z_send = outs
    x_outs = (
        ((next_r, 2), (next_r, 3)),
        ((next_r, 0), (next_r, 1)),
        ((next_l, 0), (next_l, 1)),
        ((next_l, 2), (next_l, 3)),
        (None, None),
    )
    for i, outs in enumerate(x_outs):
        pl.when(pl.program_id(0) == i)(
            functools.partial(
                halves.fill, place, act, weight, i % 2, outs, ((z_send, i), None)
            )
        )


def third_kernel(halves, place, act, weight, outs):
    (mine,) = outs
    for i in range(6):
        x_outs = (None, None) if i < 4 else ((mine, i + 3), (mine, i + 5))
        z_other = (mine, 6) if i == 5 else None
        pl.when(pl.program_id(0) == i)(
            functools.partial(
                halves.fill, place, act, weight, i % 2, x_outs, (z_other, (mine, i))
            )
        )


def project(kernel, halves, place, activations, weight, owner, steps, outs, after=()):
    first, last = halves.columns[0], halves.columns[-1]

    def weight_block(i, at):
        return (first + (last - first) * (i % 2), 0, at[owner + i // 2])

    def body(at, act, weight_ref, *refs):
        kernel(halves, at, act, weight_ref, refs[len(after) :])

    specs, results = [], []
    for count, where in outs:
        if where == "vmem":
            specs.append(pl.BlockSpec(memory_space=pltpu.VMEM))
            results.append(jax.ShapeDtypeStruct(halves.shape(count), jnp.float32))
            continue
        results.append(pltpu.HBM(halves.shape(count), jnp.float32))
        if where == "hbm":
            specs.append(pl.BlockSpec(halves.shape(count), lambda i, at: (0, 0, 0)))
        else:
            specs.append(
                pl.BlockSpec(
                    halves.shape(1),
                    lambda i, at, start=where, end=count - 1: (
                        jnp.clip(i - start, 0, end),
                        0,
                        0,
                    ),
                )
            )
    return pl.pallas_call(
        body,
        grid_spec=pltpu.PrefetchScalarGridSpec(
            num_scalar_prefetch=1,
            grid=(steps,),
            in_specs=[
                pl.BlockSpec(activations.shape, lambda i, at: (0, 0)),
                pl.BlockSpec((1, weight.shape[1], 2 * BLOCK), weight_block),
            ]
            + [pl.BlockSpec(memory_space=pl.ANY)] * len(after),
            out_specs=specs,
        ),
        out_shape=results,
        compiler_params=params(24),
        name=kernel.__name__,
    )(place, activations, weight, *after)


def sum_call(kernel, halves, counts, near, far, after=()):
    tile = min(BLOCK, halves.rows)

    def body(*refs):
        rows = pl.ds(pl.multiple_of(pl.program_id(0) * tile, tile), tile)
        ins = [ref.at[:, rows] for ref in refs[: len(near)]]
        ins += refs[len(near) : len(near) + len(far)]
        kernel(*ins, *[ref.at[:, rows] for ref in refs[len(near) + len(far) + len(after) :]])

    return pl.pallas_call(
        body,
        grid=(halves.rows // tile,),
        in_specs=[pl.BlockSpec(memory_space=pltpu.VMEM)] * len(near)
        + [pl.BlockSpec((value.shape[0], tile, BLOCK), lambda i: (0, i, 0)) for value in far]
        + [pl.BlockSpec(memory_space=pl.ANY)] * len(after),
        out_specs=[pl.BlockSpec(memory_space=pltpu.VMEM)] * len(counts),
        out_shape=[jax.ShapeDtypeStruct(halves.shape(count), jnp.float32) for count in counts],
        compiler_params=params(8),
        name=kernel.__name__,
    )(*near, *[in_hbm(value) for value in far], *after)


def first_sum_kernel(got_r, got_l, z_got, keep_r, keep_l, z_mine, out_r, out_l):
    for half, (keep, got, out) in enumerate(((keep_r, got_r, out_r), (keep_l, got_l, out_l))):
        out[0] = keep[0] + got[0]
        out[1] = keep[1] + got[1]
        out[2] = z_mine[half] + z_got[half]


def kv_first_sum_kernel(got_r, got_l, z_got, next_r, next_l, z_mine, out_r, out_l):
    for half, (mine, got, out) in enumerate(((next_r, got_r, out_r), (next_l, got_l, out_l))):
        out[0] = mine[0]
        out[1] = mine[1]
        out[2] = mine[2] + got[0]
        out[3] = mine[3] + got[1]
        out[4] = z_mine[half] + z_got[half]


def piece_call(kernel, halves, counts, pieces, after=()):
    tile = min(2 * BLOCK, halves.rows)

    def body(*refs):
        kernel(*refs[: len(pieces)], *refs[len(pieces) + len(after) :])

    def spec(index):
        return pl.BlockSpec((1, tile, BLOCK), lambda i: (index, i, 0))

    return pl.pallas_call(
        body,
        grid=(halves.rows // tile,),
        in_specs=[spec(index) for _, index in pieces]
        + [pl.BlockSpec(memory_space=pl.ANY)] * len(after),
        out_specs=[pl.BlockSpec((n, tile, BLOCK), lambda i: (0, i, 0)) for n in counts],
        out_shape=[jax.ShapeDtypeStruct(halves.shape(count), jnp.float32) for count in counts],
        compiler_params=params(12),
        name=kernel.__name__,
    )(*[value for value, _ in pieces], *after)


def kv_other_kernel(own_k, own_v, r_k, r_v, l_k, l_v, late, out):
    out[0:1] = own_k[...] + (r_k[...] + l_k[...])
    out[1:2] = own_v[...] + (r_v[...] + l_v[...])
    out[2:3] = late[...]


def kv_last_kernel(m0, m1, m2, m3, g0, g1, g2, g3, next_r, next_l, out_r, out_l):
    out_r[0:1] = m0[...] + g0[...] + next_r[...]
    out_r[1:2] = m1[...] + g1[...]
    out_l[0:1] = m2[...] + g2[...]
    out_l[1:2] = m3[...] + g3[...] + next_l[...]


def kv_beside_kernel(m4, m5, g4, own_k, own_v, r_k, r_v, l_k, l_v, out):
    out[0:1] = m4[...] + g4[...]
    out[1:2] = m5[...]
    out[2:3] = own_k[...] + (r_k[...] + l_k[...])
    out[3:4] = own_v[...] + (r_v[...] + l_v[...])


def release(values, after):
    def body(*refs):
        pass

    count = len(values)
    return pl.pallas_call(
        body,
        in_specs=[pl.BlockSpec(memory_space=pl.ANY)] * (count + 1),
        out_specs=[pl.BlockSpec(memory_space=pl.ANY)] * count,
        out_shape=[pltpu.HBM(value.shape, value.dtype) for value in values],
        input_output_aliases={i: i for i in range(count)},
        name="release",
    )(*values, after)


def query_project_kernel(place, act, weight, *refs):
    send_r, send_l, keep_r, keep_l, z_send, z_next, z_mine, x_other, x_mine, product = refs[-10:]
    product[...] = jnp.dot(act[...], weight[0], preferred_element_type=jnp.float32)

    def put(owner, other, mine):
        start = pl.multiple_of(place[owner] * 2 * BLOCK, 2 * BLOCK)
        columns = product[:, pl.ds(start, 2 * BLOCK)]
        low, high = columns[:, :BLOCK], columns[:, BLOCK:]
        other[0][other[1]] = jnp.where(place[4] == 0, high, low)
        mine[0][mine[1]] = jnp.where(place[4] == 0, low, high)

    def z_step(half):
        for owner in range(4):
            piece = 2 * owner + half
            other = (z_send, piece) if piece < 3 else (z_next, piece - 3)
            put(owner, other, (z_mine, piece))

    def x_step(half):
        far, right, left = (
            ((send_r, 0), (keep_r, 0), (send_l, 2)),
            ((send_l, 0), (send_r, 2), (keep_l, 0)),
        )[half]
        for owner, (ref, piece) in enumerate((far, right, left)):
            put(owner, (ref, piece), (ref, piece + 1))
        put(3, (x_other, half), (x_mine, half))

    for i in range(4):
        pl.when(pl.program_id(0) == i)(
            functools.partial(z_step if i < 2 else x_step, i % 2)
        )


def query_second_sum_kernel(
    dep_r, dep_l, got_r, got_l, z_got, z_next, z_mine, x_other, out_r, out_l, out_x
):
    out_r[0] = z_mine[2] + z_got[2] + dep_r[2]
    out_r[1] = z_mine[3] + z_next[0]
    out_l[0] = z_mine[4] + z_next[1]
    out_l[1] = z_mine[5] + z_next[2] + dep_l[2]
    out_x[0] = x_other[0] + (dep_r[0] + got_l[2])
    out_x[1] = x_other[1] + (got_r[2] + dep_l[0])


def query_beside_kernel(dep_r, dep_l, got_r, got_l, z_next, z_mine, x_mine, out):
    out[0] = z_mine[6] + z_next[3]
    out[1] = z_mine[7] + z_next[4]
    out[2] = x_mine[0] + (dep_r[1] + got_l[3])
    out[3] = x_mine[1] + (got_r[3] + dep_l[1])


def reduce_kv(halves, place, activations, weight, beside):
    make = functools.partial(
        project, halves=halves, place=place, activations=activations, weight=weight
    )
    send_r, send_l, z_send, z_mine = make(
        first_kernel, owner=0, steps=2, outs=[(2, "vmem")] * 4
    )
    got_r, got_l, z_got = shift_x(send_r, 1), shift_x(send_l, -1), swap_z(z_send)
    next_r, next_l, z_send = make(
        second_kernel, owner=1, steps=5, outs=[(5, "vmem")] * 3, after=(z_mine,)
    )
    next_r, next_l = sum_call(
        kv_first_sum_kernel, halves, [5, 5], [got_r, got_l, z_got, next_r, next_l, z_mine], []
    )
    ready = beside(next_r)
    (mine,) = make(
        third_kernel,
        owner=1,
        steps=6,
        outs=[(11, "vmem")],
        after=(next_r,) + ready[1:],
    )
    next_r, next_l, z_five = shift_x(next_r, 1), shift_x(next_l, -1), swap_z(z_send)
    (last_xz,) = piece_call(
        kv_other_kernel,
        halves,
        [3],
        [(mine, 7), (mine, 8), (next_r, 2), (next_r, 0), (next_l, 0), (next_l, 2), (mine, 6)],
    )
    last_r, last_l = piece_call(
        kv_last_kernel,
        halves,
        [2, 2],
        [(mine, i) for i in range(4)]
        + [(z_five, i) for i in range(4)]
        + [(next_r, 4), (next_l, 4)],
        after=(last_xz,) + ready,
    )
    (part,) = piece_call(
        kv_beside_kernel,
        halves,
        [4],
        [(mine, 4), (mine, 5), (z_five, 4), (mine, 9), (mine, 10)]
        + [(next_r, 3), (next_r, 1), (next_l, 1), (next_l, 3)],
        after=(last_r,),
    )
    last_r, last_l, last_xz = shift_x(last_r, 1), shift_x(last_l, -1), swap_z(last_xz)
    return (part, last_r, last_l, last_xz), part


def project_query(halves, place, activations, weight, after):
    features, columns = weight.shape[1:]
    shapes = [halves.shape(count) for count in (4, 4, 2, 2, 3, 5, 8, 2, 2)]
    return pl.pallas_call(
        query_project_kernel,
        grid_spec=pltpu.PrefetchScalarGridSpec(
            num_scalar_prefetch=1,
            grid=(4,),
            in_specs=[
                pl.BlockSpec((halves.rows, features), lambda i, at: (i, 0)),
                pl.BlockSpec((1, features, columns), lambda i, at: (0, 0, 0)),
                pl.BlockSpec(memory_space=pl.ANY),
            ],
            out_specs=[pl.BlockSpec(shape, lambda i, at: (0, 0, 0)) for shape in shapes],
            scratch_shapes=[pltpu.VMEM((halves.rows, columns), jnp.float32)],
        ),
        out_shape=[pltpu.HBM(shape, jnp.float32) for shape in shapes],
        compiler_params=params(24),
        name="query_project_kernel",
    )(place, activations, weight, after)


def reduce_query(halves, projected, after):
    send_r, send_l, keep_r, keep_l, z_send, z_next, z_mine, x_other, x_mine = projected
    send_r, send_l, z_send, z_next = release((send_r, send_l, z_send, z_next), after)
    got_r, got_l, z_got = shift_x(send_r, 1), shift_x(send_l, -1), swap_z(z_send)
    z_next = swap_z(z_next)
    dep_r, dep_l = sum_call(
        first_sum_kernel,
        halves,
        [3, 3],
        [got_r, got_l, z_got],
        [keep_r, keep_l, z_mine],
    )
    dep_r, dep_l = shift_x(dep_r, 1), shift_x(dep_l, -1)
    last_r, last_l, x_sum = sum_call(
        query_second_sum_kernel,
        halves,
        [2, 2, 2],
        [dep_r, dep_l, got_r, got_l, z_got, z_next],
        [z_mine, x_other],
    )
    (part,) = sum_call(
        query_beside_kernel,
        halves,
        [4],
        [dep_r, dep_l, got_r, got_l, z_next],
        [z_mine, x_mine],
        after=(last_r,),
    )
    last_r, last_l, x_sum = shift_x(last_r, 1), shift_x(last_l, -1), swap_z(x_sum)
    return part, last_r, last_l, x_sum


def summed(part, last_r, last_l, last_x):
    z_total = [part[h] + (last_r[h] + last_l[h]) for h in range(2)]
    if last_x.shape[0] == 3:
        z_total[1] = z_total[1] + last_x[2]
    return z_total + [part[2 + h] + last_x[h] for h in range(2)]


def split_bf16(table):
    high = table.astype(np.float32).astype(ml_dtypes.bfloat16)
    low = (table - high.astype(np.float64)).astype(ml_dtypes.bfloat16)
    return high, low


@functools.lru_cache(None)
def tables(length):
    rows = length // BLOCK
    period = 2 * length
    odd = np.arange(rows) + 0.5
    first = -2 * np.pi * np.outer(odd, np.arange(rows)) / (2 * rows)
    turn = -2 * np.pi * np.outer(odd, np.arange(BLOCK)) / period
    second = -2 * np.pi * (np.outer(np.arange(BLOCK), np.arange(BLOCK)) % BLOCK) / BLOCK
    c, s = np.cos(second), np.sin(second)
    scale = 1.0 / length
    return (
        split_bf16(np.concatenate([np.cos(first), np.sin(first)], axis=0)),
        (np.cos(turn).astype(np.float32), np.sin(turn).astype(np.float32)),
        split_bf16(np.block([[c, s], [-s, c]])),
        split_bf16(np.block([[c, -s], [s, c]])),
        split_bf16(np.concatenate([np.cos(first).T, np.sin(first).T], axis=1) * scale),
    )


def split_value(value):
    high = value.astype(jnp.bfloat16)
    return high, (value - high.astype(jnp.float32)).astype(jnp.bfloat16)


def dot3(left, right):
    dot = functools.partial(jnp.dot, preferred_element_type=jnp.float32)
    return dot(left[0], right[0]) + (dot(left[0], right[1]) + dot(left[1], right[0]))


def forward(signal_ref, first, turn, second):
    seqs, channels = signal_ref.shape[:2]
    rows = seqs * signal_ref.shape[2]
    signal = jnp.concatenate(
        [signal_ref[:, c].reshape(rows, BLOCK) for c in range(channels)], axis=1
    )
    part = dot3(first, split_value(signal))
    turned = []
    for c in range(channels):
        real = part[:rows, c * BLOCK : (c + 1) * BLOCK]
        imag = part[rows:, c * BLOCK : (c + 1) * BLOCK]
        turned.append(
            jnp.concatenate(
                [real * turn[0] - imag * turn[1], real * turn[1] + imag * turn[0]], axis=1
            )
        )
    return dot3(split_value(jnp.concatenate(turned, axis=0)), second)


def taps_kernel(taps_ref, f_hi, f_lo, t_re, t_im, s_hi, s_lo, out_ref):
    out_ref[...] = forward(
        taps_ref, (f_hi[...], f_lo[...]), (t_re[...], t_im[...]), (s_hi[...], s_lo[...])
    )


def conv_kernel(
    kv_ref, spec_ref, f_hi, f_lo, t_re, t_im, s_hi, s_lo, b_hi, b_lo, i_hi, i_lo, out_ref
):
    seqs, channels, blocks, _ = kv_ref.shape
    rows = seqs * blocks
    turn = (t_re[...], t_im[...])
    spectrum = forward(kv_ref, (f_hi[...], f_lo[...]), turn, (s_hi[...], s_lo[...]))
    real, imag = spectrum[:, :BLOCK], spectrum[:, BLOCK:]
    taps_real, taps_imag = spec_ref[:, :BLOCK], spec_ref[:, BLOCK:]
    product = jnp.concatenate(
        [real * taps_real - imag * taps_imag, real * taps_imag + imag * taps_real], axis=1
    )
    back = dot3(split_value(product), (b_hi[...], b_lo[...]))
    columns = []
    for c in range(channels):
        real = back[c * rows : (c + 1) * rows, :BLOCK]
        imag = back[c * rows : (c + 1) * rows, BLOCK:]
        columns.append(
            jnp.concatenate(
                [real * turn[0] + imag * turn[1], imag * turn[0] - real * turn[1]], axis=0
            )
        )
    result = dot3((i_hi[...], i_lo[...]), split_value(jnp.concatenate(columns, axis=1)))
    for c in range(channels):
        out_ref[:, c] = result[:, c * BLOCK : (c + 1) * BLOCK].reshape(seqs, blocks, BLOCK)


def turn_blocks(value_ref, out_ref):
    for b in range(out_ref.shape[1]):
        out_ref[:, b, :] = value_ref[b * BLOCK : (b + 1) * BLOCK, :].T


def taps_turn_kernel(taps_ref, out_ref):
    turn_blocks(taps_ref, out_ref)


def kv_kernel(*refs):
    parts, out_ref, kv_ref = refs[:-2], refs[-2], refs[-1]
    z_key, z_value, x_key, x_value = summed(*parts)
    rows = z_key.shape[0]
    kv_ref[:rows] = z_key * z_value
    kv_ref[rows:] = x_key * x_value
    turn_blocks(kv_ref, out_ref)


def query_kernel(*refs):
    parts, out_ref = refs[:-1], refs[-1]
    for i, query in enumerate(summed(*parts)):
        rows = query.shape[0]
        out_ref[i * rows : (i + 1) * rows] = query


def gate_kernel(conv_ref, query_ref, out_ref):
    for b in range(conv_ref.shape[1]):
        rows = slice(b * BLOCK, (b + 1) * BLOCK)
        out_ref[rows] = conv_ref[:, b, :].T * query_ref[rows]


def call(kernel, out_shape, *operands, after=(), scratch=(), tables=(), to_hbm=False):
    def body(*refs):
        count = len(operands) + len(tables)
        kernel(*refs[:count], *refs[count + len(after) :])

    def whole(shape):
        return pl.BlockSpec(shape, lambda i: (0,) * len(shape))

    return pl.pallas_call(
        body,
        grid=(1,),
        in_specs=[pl.BlockSpec(memory_space=pltpu.VMEM)] * len(operands)
        + [whole(table.shape) for table in tables]
        + [pl.BlockSpec(memory_space=pl.ANY)] * len(after),
        out_specs=whole(out_shape) if to_hbm else pl.BlockSpec(memory_space=pltpu.VMEM),
        out_shape=pltpu.HBM(out_shape, jnp.float32)
        if to_hbm
        else jax.ShapeDtypeStruct(out_shape, jnp.float32),
        scratch_shapes=scratch,
        compiler_params=params(24),
        name=kernel.__name__,
    )(*operands, *[in_hbm(jnp.asarray(table)) for table in tables], *after)


def exchange(value):
    return lax.all_to_all(value, "seq", split_axis=0, concat_axis=0, tiled=True)


def on_device(activations, proj_weight, filter_taps):
    tokens, channels = filter_taps.shape
    seqs = lax.axis_size("seq")
    length = tokens * seqs
    blocks = tokens // BLOCK
    owned = channels // seqs
    turned_shape = (channels, blocks, BLOCK)
    moved_shape = (seqs, owned, blocks, BLOCK)
    first, turn, second, back, inverse = tables(length)

    chan = lax.axis_index("chan")
    x_at, z_at = chan // 2, chan % 2
    owners = [(x_at + dx) % X_SIZE for dx in (2, 1, 3, 0)]
    place = jnp.stack(owners + [z_at]).astype(jnp.int32)
    weight = in_hbm(jnp.transpose(proj_weight, (1, 0, 2)))
    activations = in_hbm(activations)

    hold = {}
    kv_halves, q_halves = Halves(tokens, (1, 2)), Halves(tokens, (0,))

    def prepare(ready):
        taps = call(taps_turn_kernel, turned_shape, filter_taps, after=(ready,), to_hbm=True)
        hold["taps"] = exchange(taps.reshape(moved_shape))
        hold["query"] = project_query(q_halves, place, activations, weight, ready)
        return hold["taps"], hold["query"][0]

    kv_parts, kv_part = reduce_kv(kv_halves, place, activations, weight, prepare)
    spectrum = call(
        taps_kernel,
        (owned * length // BLOCK, 2 * BLOCK),
        hold["taps"],
        tables=first + turn + second,
        after=(kv_part,),
        to_hbm=True,
    )
    kv = call(
        kv_kernel,
        turned_shape,
        *kv_parts,
        after=(spectrum,),
        scratch=[pltpu.VMEM((tokens, channels), jnp.float32)],
        to_hbm=True,
    )
    q_parts = reduce_query(q_halves, hold["query"], spectrum)
    moved = exchange(kv.reshape(moved_shape))
    convolved = call(
        conv_kernel,
        moved_shape,
        moved,
        tables=(spectrum,) + first + turn + second + back + inverse,
        to_hbm=True,
    )
    query = call(query_kernel, (tokens, channels), *q_parts)
    home = exchange(convolved).reshape(turned_shape)
    return call(gate_kernel, (tokens, channels), home, query)


def solution(mesh):
    return jax.shard_map(
        on_device,
        mesh=mesh,
        in_specs=(P("seq", "chan"), P("chan", None, None), P("seq", "chan")),
        out_specs=P("seq", "chan"),
        check_vma=False,
    )
```

```python
import functools

import jax
import jax.numpy as jnp
import ml_dtypes
import numpy as np
from jax import lax
from jax.experimental import pallas as pl
from jax.experimental.pallas import tpu as pltpu
from jax.sharding import PartitionSpec as P

BLOCK = 128
X_SIZE = 4
CHUNK = 512


def params(mebibytes):
    return pltpu.CompilerParams(vmem_limit_bytes=mebibytes * 1024 * 1024)


def in_hbm(value):
    return pltpu.with_memory_space_constraint(value, pltpu.HBM)


def shift_x(value, step):
    return lax.ppermute(value, "chan", [(i, (i + 2 * step) % 8) for i in range(8)])


def swap_z(value):
    return lax.ppermute(value, "chan", [(i, i ^ 1) for i in range(8)])


def parts_of(rows, weight, z_at):
    product = jnp.dot(rows, weight, preferred_element_type=jnp.float32)
    low, high = product[:, :BLOCK], product[:, BLOCK:]
    return jnp.where(z_at == 0, high, low), jnp.where(z_at == 0, low, high)


class Halves:
    def __init__(self, tokens, columns):
        self.columns = columns
        parts = 2 // len(columns)
        self.rows = tokens // 2 // parts
        self.z_start = [h % parts * self.rows for h in range(2)]
        self.x_start = [tokens // 2 + start for start in self.z_start]

    def shape(self, count):
        return (count, self.rows, BLOCK)

    def fill(self, place, act, weight, half, x_outs, z_outs):
        for begin, outs in ((self.x_start[half], x_outs), (self.z_start[half], z_outs)):
            if outs == (None, None):
                continue
            for start in range(0, self.rows, CHUNK):
                rows = act[begin + start : begin + start + CHUNK]
                for out, part in zip(outs, parts_of(rows, weight[0], place[4])):
                    if out is not None:
                        out[0][out[1], start : start + CHUNK] = part


def first_kernel(halves, place, act, weight, outs):
    send_r, send_l, z_other, z_mine = outs
    for half, send in enumerate((send_r, send_l)):
        pl.when(pl.program_id(0) == half)(
            functools.partial(
                halves.fill,
                place,
                act,
                weight,
                half,
                ((send, 0), (send, 1)),
                ((z_other, half), (z_mine, half)),
            )
        )


def second_kernel(halves, place, act, weight, outs):
    next_r, next_l, z_send = outs
    x_outs = (
        ((next_r, 2), (next_r, 3)),
        ((next_r, 0), (next_r, 1)),
        ((next_l, 0), (next_l, 1)),
        ((next_l, 2), (next_l, 3)),
        (None, None),
        (None, None),
    )
    for i, outs in enumerate(x_outs):
        pl.when(pl.program_id(0) == i)(
            functools.partial(
                halves.fill, place, act, weight, i % 2, outs, ((z_send, i), None)
            )
        )


def third_kernel(halves, place, act, weight, outs):
    (mine,) = outs
    for i in range(6):
        x_outs = (None, None) if i < 4 else ((mine, i + 2), (mine, i + 4))
        pl.when(pl.program_id(0) == i)(
            functools.partial(halves.fill, place, act, weight, i % 2, x_outs, (None, (mine, i)))
        )


def project(kernel, halves, place, activations, weight, owner, steps, outs, after=()):
    first, last = halves.columns[0], halves.columns[-1]

    def weight_block(i, at):
        return (first + (last - first) * (i % 2), 0, at[owner + i // 2])

    def body(at, act, weight_ref, *refs):
        kernel(halves, at, act, weight_ref, refs[len(after) :])

    specs, results = [], []
    for count, where in outs:
        if where == "vmem":
            specs.append(pl.BlockSpec(memory_space=pltpu.VMEM))
            results.append(jax.ShapeDtypeStruct(halves.shape(count), jnp.float32))
            continue
        results.append(pltpu.HBM(halves.shape(count), jnp.float32))
        if where == "hbm":
            specs.append(pl.BlockSpec(halves.shape(count), lambda i, at: (0, 0, 0)))
        else:
            specs.append(
                pl.BlockSpec(
                    halves.shape(1),
                    lambda i, at, start=where, end=count - 1: (
                        jnp.clip(i - start, 0, end),
                        0,
                        0,
                    ),
                )
            )
    return pl.pallas_call(
        body,
        grid_spec=pltpu.PrefetchScalarGridSpec(
            num_scalar_prefetch=1,
            grid=(steps,),
            in_specs=[
                pl.BlockSpec(activations.shape, lambda i, at: (0, 0)),
                pl.BlockSpec((1, weight.shape[1], 2 * BLOCK), weight_block),
            ]
            + [pl.BlockSpec(memory_space=pl.ANY)] * len(after),
            out_specs=specs,
        ),
        out_shape=results,
        compiler_params=params(24),
        name=kernel.__name__,
    )(place, activations, weight, *after)


def sum_call(kernel, halves, counts, near, far, after=()):
    tile = min(BLOCK, halves.rows)

    def body(*refs):
        rows = pl.ds(pl.multiple_of(pl.program_id(0) * tile, tile), tile)
        ins = [ref.at[:, rows] for ref in refs[: len(near)]]
        ins += refs[len(near) : len(near) + len(far)]
        kernel(*ins, *[ref.at[:, rows] for ref in refs[len(near) + len(far) + len(after) :]])

    return pl.pallas_call(
        body,
        grid=(halves.rows // tile,),
        in_specs=[pl.BlockSpec(memory_space=pltpu.VMEM)] * len(near)
        + [pl.BlockSpec((value.shape[0], tile, BLOCK), lambda i: (0, i, 0)) for value in far]
        + [pl.BlockSpec(memory_space=pl.ANY)] * len(after),
        out_specs=[pl.BlockSpec(memory_space=pltpu.VMEM)] * len(counts),
        out_shape=[jax.ShapeDtypeStruct(halves.shape(count), jnp.float32) for count in counts],
        compiler_params=params(8),
        name=kernel.__name__,
    )(*near, *[in_hbm(value) for value in far], *after)


def first_sum_kernel(got_r, got_l, z_got, keep_r, keep_l, z_mine, out_r, out_l):
    for half, (keep, got, out) in enumerate(((keep_r, got_r, out_r), (keep_l, got_l, out_l))):
        out[0] = keep[0] + got[0]
        out[1] = keep[1] + got[1]
        out[2] = z_mine[half] + z_got[half]


def kv_first_sum_kernel(got_r, got_l, z_got, next_r, next_l, z_mine, out_r, out_l):
    for half, (mine, got, out) in enumerate(((next_r, got_r, out_r), (next_l, got_l, out_l))):
        out[0] = mine[0]
        out[1] = mine[1]
        out[2] = mine[2] + got[0]
        out[3] = mine[3] + got[1]
        out[4] = z_mine[half] + z_got[half]


def piece_call(kernel, halves, counts, pieces, after=()):
    tile = min(2 * BLOCK, halves.rows)

    def body(*refs):
        kernel(*refs[: len(pieces)], *refs[len(pieces) + len(after) :])

    def spec(index):
        return pl.BlockSpec((1, tile, BLOCK), lambda i: (index, i, 0))

    return pl.pallas_call(
        body,
        grid=(halves.rows // tile,),
        in_specs=[spec(index) for _, index in pieces]
        + [pl.BlockSpec(memory_space=pl.ANY)] * len(after),
        out_specs=[pl.BlockSpec((n, tile, BLOCK), lambda i: (0, i, 0)) for n in counts],
        out_shape=[jax.ShapeDtypeStruct(halves.shape(count), jnp.float32) for count in counts],
        compiler_params=params(12),
        name=kernel.__name__,
    )(*[value for value, _ in pieces], *after)


def kv_second_sum_kernel(*refs):
    m0, m1, m2, m3, g0, g1, g2, g3, z_r, z_l = refs[:10]
    own_k, own_v, r_k, r_v, l_k, l_v, out_r, out_l, out_x = refs[10:]
    out_r[0:1] = m0[...] + g0[...] + z_r[...]
    out_r[1:2] = m1[...] + g1[...]
    out_l[0:1] = m2[...] + g2[...]
    out_l[1:2] = m3[...] + g3[...] + z_l[...]
    out_x[0:1] = own_k[...] + (r_k[...] + l_k[...])
    out_x[1:2] = own_v[...] + (r_v[...] + l_v[...])


def kv_beside_kernel(m4, m5, g4, g5, own_k, own_v, r_k, r_v, l_k, l_v, out):
    out[0:1] = m4[...] + g4[...]
    out[1:2] = m5[...] + g5[...]
    out[2:3] = own_k[...] + (r_k[...] + l_k[...])
    out[3:4] = own_v[...] + (r_v[...] + l_v[...])


def release(values, after):
    def body(*refs):
        pass

    count = len(values)
    return pl.pallas_call(
        body,
        in_specs=[pl.BlockSpec(memory_space=pl.ANY)] * (count + 1),
        out_specs=[pl.BlockSpec(memory_space=pl.ANY)] * count,
        out_shape=[pltpu.HBM(value.shape, value.dtype) for value in values],
        input_output_aliases={i: i for i in range(count)},
        name="release",
    )(*values, after)


def query_project_kernel(place, act, weight, *refs):
    send_r, send_l, keep_r, keep_l, z_send, z_next, z_mine, x_other, x_mine, product = refs[-10:]
    product[...] = jnp.dot(act[...], weight[0], preferred_element_type=jnp.float32)

    def put(owner, other, mine):
        start = pl.multiple_of(place[owner] * 2 * BLOCK, 2 * BLOCK)
        columns = product[:, pl.ds(start, 2 * BLOCK)]
        low, high = columns[:, :BLOCK], columns[:, BLOCK:]
        other[0][other[1]] = jnp.where(place[4] == 0, high, low)
        mine[0][mine[1]] = jnp.where(place[4] == 0, low, high)

    def z_step(half):
        for owner in range(4):
            piece = 2 * owner + half
            other = (z_send, piece) if piece < 3 else (z_next, piece - 3)
            put(owner, other, (z_mine, piece))

    def x_step(half):
        far, right, left = (
            ((send_r, 0), (keep_r, 0), (send_l, 2)),
            ((send_l, 0), (send_r, 2), (keep_l, 0)),
        )[half]
        for owner, (ref, piece) in enumerate((far, right, left)):
            put(owner, (ref, piece), (ref, piece + 1))
        put(3, (x_other, half), (x_mine, half))

    for i in range(4):
        pl.when(pl.program_id(0) == i)(
            functools.partial(z_step if i < 2 else x_step, i % 2)
        )


def query_second_sum_kernel(
    dep_r, dep_l, got_r, got_l, z_got, z_next, z_mine, x_other, out_r, out_l, out_x
):
    out_r[0] = z_mine[2] + z_got[2] + dep_r[2]
    out_r[1] = z_mine[3] + z_next[0]
    out_l[0] = z_mine[4] + z_next[1]
    out_l[1] = z_mine[5] + z_next[2] + dep_l[2]
    out_x[0] = x_other[0] + (dep_r[0] + got_l[2])
    out_x[1] = x_other[1] + (got_r[2] + dep_l[0])


def query_beside_kernel(dep_r, dep_l, got_r, got_l, z_next, z_mine, x_mine, out):
    out[0] = z_mine[6] + z_next[3]
    out[1] = z_mine[7] + z_next[4]
    out[2] = x_mine[0] + (dep_r[1] + got_l[3])
    out[3] = x_mine[1] + (got_r[3] + dep_l[1])


def reduce_kv(halves, place, activations, weight, beside):
    make = functools.partial(
        project, halves=halves, place=place, activations=activations, weight=weight
    )
    send_r, send_l, z_send, z_mine = make(
        first_kernel, owner=0, steps=2, outs=[(2, "vmem")] * 4
    )
    got_r, got_l, z_got = shift_x(send_r, 1), shift_x(send_l, -1), swap_z(z_send)
    next_r, next_l, z_send = make(
        second_kernel, owner=1, steps=6, outs=[(5, "vmem")] * 2 + [(6, "vmem")], after=(z_mine,)
    )
    next_r, next_l = sum_call(
        kv_first_sum_kernel, halves, [5, 5], [got_r, got_l, z_got, next_r, next_l, z_mine], []
    )
    ready = beside(next_r)
    (mine,) = make(
        third_kernel,
        owner=1,
        steps=6,
        outs=[(10, "vmem")],
        after=(next_r,) + ready[1:],
    )
    next_r, next_l, z_six = shift_x(next_r, 1), shift_x(next_l, -1), swap_z(z_send)
    last_r, last_l, last_x = piece_call(
        kv_second_sum_kernel,
        halves,
        [2, 2, 2],
        [(mine, i) for i in range(4)]
        + [(z_six, i) for i in range(4)]
        + [(next_r, 4), (next_l, 4), (mine, 6), (mine, 7)]
        + [(next_r, 2), (next_r, 0), (next_l, 0), (next_l, 2)],
        after=ready,
    )
    (part,) = piece_call(
        kv_beside_kernel,
        halves,
        [4],
        [(mine, 4), (mine, 5), (z_six, 4), (z_six, 5), (mine, 8), (mine, 9)]
        + [(next_r, 3), (next_r, 1), (next_l, 1), (next_l, 3)],
        after=(last_r,),
    )
    last_r, last_l, last_x = shift_x(last_r, 1), shift_x(last_l, -1), swap_z(last_x)
    return (part, last_r, last_l, last_x), part


def project_query(halves, place, activations, weight, after):
    features, columns = weight.shape[1:]
    shapes = [halves.shape(count) for count in (4, 4, 2, 2, 3, 5, 8, 2, 2)]
    return pl.pallas_call(
        query_project_kernel,
        grid_spec=pltpu.PrefetchScalarGridSpec(
            num_scalar_prefetch=1,
            grid=(4,),
            in_specs=[
                pl.BlockSpec((halves.rows, features), lambda i, at: (i, 0)),
                pl.BlockSpec((1, features, columns), lambda i, at: (0, 0, 0)),
                pl.BlockSpec(memory_space=pl.ANY),
            ],
            out_specs=[pl.BlockSpec(shape, lambda i, at: (0, 0, 0)) for shape in shapes],
            scratch_shapes=[pltpu.VMEM((halves.rows, columns), jnp.float32)],
        ),
        out_shape=[pltpu.HBM(shape, jnp.float32) for shape in shapes],
        compiler_params=params(24),
        name="query_project_kernel",
    )(place, activations, weight, after)


def reduce_query(halves, projected, after):
    send_r, send_l, keep_r, keep_l, z_send, z_next, z_mine, x_other, x_mine = projected
    send_r, send_l, z_send, z_next = release((send_r, send_l, z_send, z_next), after)
    got_r, got_l, z_got = shift_x(send_r, 1), shift_x(send_l, -1), swap_z(z_send)
    z_next = swap_z(z_next)
    dep_r, dep_l = sum_call(
        first_sum_kernel,
        halves,
        [3, 3],
        [got_r, got_l, z_got],
        [keep_r, keep_l, z_mine],
    )
    dep_r, dep_l = shift_x(dep_r, 1), shift_x(dep_l, -1)
    last_r, last_l, x_sum = sum_call(
        query_second_sum_kernel,
        halves,
        [2, 2, 2],
        [dep_r, dep_l, got_r, got_l, z_got, z_next],
        [z_mine, x_other],
    )
    (part,) = sum_call(
        query_beside_kernel,
        halves,
        [4],
        [dep_r, dep_l, got_r, got_l, z_next],
        [z_mine, x_mine],
        after=(last_r,),
    )
    last_r, last_l, x_sum = shift_x(last_r, 1), shift_x(last_l, -1), swap_z(x_sum)
    return part, last_r, last_l, x_sum


def summed(part, last_r, last_l, last_x):
    return [part[h] + (last_r[h] + last_l[h]) for h in range(2)] + [
        part[2 + h] + last_x[h] for h in range(2)
    ]


def split_bf16(table):
    high = table.astype(np.float32).astype(ml_dtypes.bfloat16)
    low = (table - high.astype(np.float64)).astype(ml_dtypes.bfloat16)
    return high, low


@functools.lru_cache(None)
def tables(length):
    rows = length // BLOCK
    period = 2 * length
    odd = np.arange(rows) + 0.5
    first = -2 * np.pi * np.outer(odd, np.arange(rows)) / (2 * rows)
    turn = -2 * np.pi * np.outer(odd, np.arange(BLOCK)) / period
    second = -2 * np.pi * (np.outer(np.arange(BLOCK), np.arange(BLOCK)) % BLOCK) / BLOCK
    c, s = np.cos(second), np.sin(second)
    scale = 1.0 / length
    return (
        split_bf16(np.concatenate([np.cos(first), np.sin(first)], axis=0)),
        (np.cos(turn).astype(np.float32), np.sin(turn).astype(np.float32)),
        split_bf16(np.block([[c, s], [-s, c]])),
        split_bf16(np.block([[c, -s], [s, c]])),
        split_bf16(np.concatenate([np.cos(first).T, np.sin(first).T], axis=1) * scale),
    )


def split_value(value):
    high = value.astype(jnp.bfloat16)
    return high, (value - high.astype(jnp.float32)).astype(jnp.bfloat16)


def dot3(left, right):
    dot = functools.partial(jnp.dot, preferred_element_type=jnp.float32)
    return dot(left[0], right[0]) + (dot(left[0], right[1]) + dot(left[1], right[0]))


def forward(signal_ref, first, turn, second):
    seqs, channels = signal_ref.shape[:2]
    rows = seqs * signal_ref.shape[2]
    signal = jnp.concatenate(
        [signal_ref[:, c].reshape(rows, BLOCK) for c in range(channels)], axis=1
    )
    part = dot3(first, split_value(signal))
    turned = []
    for c in range(channels):
        real = part[:rows, c * BLOCK : (c + 1) * BLOCK]
        imag = part[rows:, c * BLOCK : (c + 1) * BLOCK]
        turned.append(
            jnp.concatenate(
                [real * turn[0] - imag * turn[1], real * turn[1] + imag * turn[0]], axis=1
            )
        )
    return dot3(split_value(jnp.concatenate(turned, axis=0)), second)


def taps_kernel(taps_ref, f_hi, f_lo, t_re, t_im, s_hi, s_lo, out_ref):
    out_ref[...] = forward(
        taps_ref, (f_hi[...], f_lo[...]), (t_re[...], t_im[...]), (s_hi[...], s_lo[...])
    )


def conv_kernel(
    kv_ref, spec_ref, f_hi, f_lo, t_re, t_im, s_hi, s_lo, b_hi, b_lo, i_hi, i_lo, out_ref
):
    seqs, channels, blocks, _ = kv_ref.shape
    rows = seqs * blocks
    turn = (t_re[...], t_im[...])
    spectrum = forward(kv_ref, (f_hi[...], f_lo[...]), turn, (s_hi[...], s_lo[...]))
    real, imag = spectrum[:, :BLOCK], spectrum[:, BLOCK:]
    taps_real, taps_imag = spec_ref[:, :BLOCK], spec_ref[:, BLOCK:]
    product = jnp.concatenate(
        [real * taps_real - imag * taps_imag, real * taps_imag + imag * taps_real], axis=1
    )
    back = dot3(split_value(product), (b_hi[...], b_lo[...]))
    columns = []
    for c in range(channels):
        real = back[c * rows : (c + 1) * rows, :BLOCK]
        imag = back[c * rows : (c + 1) * rows, BLOCK:]
        columns.append(
            jnp.concatenate(
                [real * turn[0] + imag * turn[1], imag * turn[0] - real * turn[1]], axis=0
            )
        )
    result = dot3((i_hi[...], i_lo[...]), split_value(jnp.concatenate(columns, axis=1)))
    for c in range(channels):
        out_ref[:, c] = result[:, c * BLOCK : (c + 1) * BLOCK].reshape(seqs, blocks, BLOCK)


def turn_blocks(value_ref, out_ref):
    for b in range(out_ref.shape[1]):
        out_ref[:, b, :] = value_ref[b * BLOCK : (b + 1) * BLOCK, :].T


def taps_turn_kernel(taps_ref, out_ref):
    turn_blocks(taps_ref, out_ref)


def kv_kernel(*refs):
    parts, out_ref, kv_ref = refs[:-2], refs[-2], refs[-1]
    z_key, z_value, x_key, x_value = summed(*parts)
    rows = z_key.shape[0]
    kv_ref[:rows] = z_key * z_value
    kv_ref[rows:] = x_key * x_value
    turn_blocks(kv_ref, out_ref)


def query_kernel(*refs):
    parts, out_ref = refs[:-1], refs[-1]
    for i, query in enumerate(summed(*parts)):
        rows = query.shape[0]
        out_ref[i * rows : (i + 1) * rows] = query


def gate_kernel(conv_ref, query_ref, out_ref):
    for b in range(conv_ref.shape[1]):
        rows = slice(b * BLOCK, (b + 1) * BLOCK)
        out_ref[rows] = conv_ref[:, b, :].T * query_ref[rows]


def call(kernel, out_shape, *operands, after=(), scratch=(), tables=(), to_hbm=False):
    def body(*refs):
        count = len(operands) + len(tables)
        kernel(*refs[:count], *refs[count + len(after) :])

    def whole(shape):
        return pl.BlockSpec(shape, lambda i: (0,) * len(shape))

    return pl.pallas_call(
        body,
        grid=(1,),
        in_specs=[pl.BlockSpec(memory_space=pltpu.VMEM)] * len(operands)
        + [whole(table.shape) for table in tables]
        + [pl.BlockSpec(memory_space=pl.ANY)] * len(after),
        out_specs=whole(out_shape) if to_hbm else pl.BlockSpec(memory_space=pltpu.VMEM),
        out_shape=pltpu.HBM(out_shape, jnp.float32)
        if to_hbm
        else jax.ShapeDtypeStruct(out_shape, jnp.float32),
        scratch_shapes=scratch,
        compiler_params=params(24),
        name=kernel.__name__,
    )(*operands, *[in_hbm(jnp.asarray(table)) for table in tables], *after)


def exchange(value):
    return lax.all_to_all(value, "seq", split_axis=0, concat_axis=0, tiled=True)


def on_device(activations, proj_weight, filter_taps):
    tokens, channels = filter_taps.shape
    seqs = lax.axis_size("seq")
    length = tokens * seqs
    blocks = tokens // BLOCK
    owned = channels // seqs
    turned_shape = (channels, blocks, BLOCK)
    moved_shape = (seqs, owned, blocks, BLOCK)
    first, turn, second, back, inverse = tables(length)

    chan = lax.axis_index("chan")
    x_at, z_at = chan // 2, chan % 2
    owners = [(x_at + dx) % X_SIZE for dx in (2, 1, 3, 0)]
    place = jnp.stack(owners + [z_at]).astype(jnp.int32)
    weight = in_hbm(jnp.transpose(proj_weight, (1, 0, 2)))
    activations = in_hbm(activations)

    hold = {}
    kv_halves, q_halves = Halves(tokens, (1, 2)), Halves(tokens, (0,))

    def prepare(ready):
        taps = call(taps_turn_kernel, turned_shape, filter_taps, after=(ready,), to_hbm=True)
        hold["taps"] = exchange(taps.reshape(moved_shape))
        hold["query"] = project_query(q_halves, place, activations, weight, ready)
        return hold["taps"], hold["query"][0]

    kv_parts, kv_part = reduce_kv(kv_halves, place, activations, weight, prepare)
    spectrum = call(
        taps_kernel,
        (owned * length // BLOCK, 2 * BLOCK),
        hold["taps"],
        tables=first + turn + second,
        after=(kv_part,),
        to_hbm=True,
    )
    kv = call(
        kv_kernel,
        turned_shape,
        *kv_parts,
        after=(spectrum,),
        scratch=[pltpu.VMEM((tokens, channels), jnp.float32)],
        to_hbm=True,
    )
    q_parts = reduce_query(q_halves, hold["query"], spectrum)
    moved = exchange(kv.reshape(moved_shape))
    convolved = call(
        conv_kernel,
        moved_shape,
        moved,
        tables=(spectrum,) + first + turn + second + back + inverse,
        to_hbm=True,
    )
    query = call(query_kernel, (tokens, channels), *q_parts)
    home = exchange(convolved).reshape(turned_shape)
    return call(gate_kernel, (tokens, channels), home, query)


def solution(mesh):
    return jax.shard_map(
        on_device,
        mesh=mesh,
        in_specs=(P("seq", "chan"), P("chan", None, None), P("seq", "chan")),
        out_specs=P("seq", "chan"),
        check_vma=False,
    )
```

```python
import functools

import jax
import jax.numpy as jnp
import ml_dtypes
import numpy as np
from jax import lax
from jax.experimental import pallas as pl
from jax.experimental.pallas import tpu as pltpu
from jax.sharding import PartitionSpec as P

BLOCK = 128
X_SIZE = 4
CHUNK = 512


def params(mebibytes):
    return pltpu.CompilerParams(vmem_limit_bytes=mebibytes * 1024 * 1024)


def in_hbm(value):
    return pltpu.with_memory_space_constraint(value, pltpu.HBM)


def shift_x(value, step):
    return lax.ppermute(value, "chan", [(i, (i + 2 * step) % 8) for i in range(8)])


def swap_z(value):
    return lax.ppermute(value, "chan", [(i, i ^ 1) for i in range(8)])


def parts_of(rows, weight, z_at):
    product = jnp.dot(rows, weight, preferred_element_type=jnp.float32)
    low, high = product[:, :BLOCK], product[:, BLOCK:]
    return jnp.where(z_at == 0, high, low), jnp.where(z_at == 0, low, high)


class Halves:
    def __init__(self, tokens, columns):
        self.columns = columns
        parts = 2 // len(columns)
        self.rows = tokens // 2 // parts
        self.z_start = [h % parts * self.rows for h in range(2)]
        self.x_start = [tokens // 2 + start for start in self.z_start]

    def shape(self, count):
        return (count, self.rows, BLOCK)

    def fill(self, place, act, weight, half, x_outs, z_outs):
        for begin, outs in ((self.x_start[half], x_outs), (self.z_start[half], z_outs)):
            if outs == (None, None):
                continue
            for start in range(0, self.rows, CHUNK):
                rows = act[begin + start : begin + start + CHUNK]
                for out, part in zip(outs, parts_of(rows, weight[0], place[4])):
                    if out is not None:
                        out[0][out[1], start : start + CHUNK] = part


def first_kernel(halves, place, act, weight, outs):
    send_r, send_l, z_other, z_mine = outs
    for half, send in enumerate((send_r, send_l)):
        pl.when(pl.program_id(0) == half)(
            functools.partial(
                halves.fill,
                place,
                act,
                weight,
                half,
                ((send, 0), (send, 1)),
                ((z_other, half), (z_mine, half)),
            )
        )


def second_kernel(halves, place, act, weight, outs):
    next_r, next_l, z_send = outs
    x_outs = (
        ((next_r, 2), (next_r, 3)),
        ((next_r, 0), (next_r, 1)),
        ((next_l, 0), (next_l, 1)),
        ((next_l, 2), (next_l, 3)),
        (None, None),
        (None, None),
    )
    for i, outs in enumerate(x_outs):
        pl.when(pl.program_id(0) == i)(
            functools.partial(
                halves.fill, place, act, weight, i % 2, outs, ((z_send, i), None)
            )
        )


def third_kernel(halves, place, act, weight, outs):
    (mine,) = outs
    for i in range(6):
        x_outs = (None, None) if i < 4 else ((mine, i + 2), (mine, i + 4))
        pl.when(pl.program_id(0) == i)(
            functools.partial(halves.fill, place, act, weight, i % 2, x_outs, (None, (mine, i)))
        )


def project(kernel, halves, place, activations, weight, owner, steps, outs, after=()):
    first, last = halves.columns[0], halves.columns[-1]

    def weight_block(i, at):
        return (first + (last - first) * (i % 2), 0, at[owner + i // 2])

    def body(at, act, weight_ref, *refs):
        kernel(halves, at, act, weight_ref, refs[len(after) :])

    specs, results = [], []
    for count, where in outs:
        if where == "vmem":
            specs.append(pl.BlockSpec(memory_space=pltpu.VMEM))
            results.append(jax.ShapeDtypeStruct(halves.shape(count), jnp.float32))
            continue
        results.append(pltpu.HBM(halves.shape(count), jnp.float32))
        if where == "hbm":
            specs.append(pl.BlockSpec(halves.shape(count), lambda i, at: (0, 0, 0)))
        else:
            specs.append(
                pl.BlockSpec(
                    halves.shape(1),
                    lambda i, at, start=where, end=count - 1: (
                        jnp.clip(i - start, 0, end),
                        0,
                        0,
                    ),
                )
            )
    return pl.pallas_call(
        body,
        grid_spec=pltpu.PrefetchScalarGridSpec(
            num_scalar_prefetch=1,
            grid=(steps,),
            in_specs=[
                pl.BlockSpec(activations.shape, lambda i, at: (0, 0)),
                pl.BlockSpec((1, weight.shape[1], 2 * BLOCK), weight_block),
            ]
            + [pl.BlockSpec(memory_space=pl.ANY)] * len(after),
            out_specs=specs,
        ),
        out_shape=results,
        compiler_params=params(24),
        name=kernel.__name__,
    )(place, activations, weight, *after)


def sum_call(kernel, halves, counts, near, far, after=()):
    tile = min(BLOCK, halves.rows)

    def body(*refs):
        rows = pl.ds(pl.multiple_of(pl.program_id(0) * tile, tile), tile)
        ins = [ref.at[:, rows] for ref in refs[: len(near)]]
        ins += refs[len(near) : len(near) + len(far)]
        kernel(*ins, *[ref.at[:, rows] for ref in refs[len(near) + len(far) + len(after) :]])

    return pl.pallas_call(
        body,
        grid=(halves.rows // tile,),
        in_specs=[pl.BlockSpec(memory_space=pltpu.VMEM)] * len(near)
        + [pl.BlockSpec((value.shape[0], tile, BLOCK), lambda i: (0, i, 0)) for value in far]
        + [pl.BlockSpec(memory_space=pl.ANY)] * len(after),
        out_specs=[pl.BlockSpec(memory_space=pltpu.VMEM)] * len(counts),
        out_shape=[jax.ShapeDtypeStruct(halves.shape(count), jnp.float32) for count in counts],
        compiler_params=params(8),
        name=kernel.__name__,
    )(*near, *[in_hbm(value) for value in far], *after)


def first_sum_kernel(got_r, got_l, z_got, keep_r, keep_l, z_mine, out_r, out_l):
    for half, (keep, got, out) in enumerate(((keep_r, got_r, out_r), (keep_l, got_l, out_l))):
        out[0] = keep[0] + got[0]
        out[1] = keep[1] + got[1]
        out[2] = z_mine[half] + z_got[half]


def kv_first_sum_kernel(got_r, got_l, z_got, next_r, next_l, z_mine, out_r, out_l):
    for half, (mine, got, out) in enumerate(((next_r, got_r, out_r), (next_l, got_l, out_l))):
        out[0] = mine[0]
        out[1] = mine[1]
        out[2] = mine[2] + got[0]
        out[3] = mine[3] + got[1]
        out[4] = z_mine[half] + z_got[half]


def piece_call(kernel, halves, counts, pieces, after=()):
    tile = min(2 * BLOCK, halves.rows)

    def body(*refs):
        kernel(*refs[: len(pieces)], *refs[len(pieces) + len(after) :])

    def spec(index):
        return pl.BlockSpec((1, tile, BLOCK), lambda i: (index, i, 0))

    return pl.pallas_call(
        body,
        grid=(halves.rows // tile,),
        in_specs=[spec(index) for _, index in pieces]
        + [pl.BlockSpec(memory_space=pl.ANY)] * len(after),
        out_specs=[pl.BlockSpec((n, tile, BLOCK), lambda i: (0, i, 0)) for n in counts],
        out_shape=[jax.ShapeDtypeStruct(halves.shape(count), jnp.float32) for count in counts],
        compiler_params=params(12),
        name=kernel.__name__,
    )(*[value for value, _ in pieces], *after)


def kv_second_sum_kernel(*refs):
    m0, m1, m2, m3, g0, g1, g2, g3, z_r, z_l = refs[:10]
    own_k, own_v, r_k, r_v, l_k, l_v, out_r, out_l, out_x = refs[10:]
    out_r[0:1] = m0[...] + g0[...] + z_r[...]
    out_r[1:2] = m1[...] + g1[...]
    out_l[0:1] = m2[...] + g2[...]
    out_l[1:2] = m3[...] + g3[...] + z_l[...]
    out_x[0:1] = own_k[...] + (r_k[...] + l_k[...])
    out_x[1:2] = own_v[...] + (r_v[...] + l_v[...])


def kv_beside_kernel(m4, m5, g4, g5, own_k, own_v, r_k, r_v, l_k, l_v, out):
    out[0:1] = m4[...] + g4[...]
    out[1:2] = m5[...] + g5[...]
    out[2:3] = own_k[...] + (r_k[...] + l_k[...])
    out[3:4] = own_v[...] + (r_v[...] + l_v[...])


def release(values, after):
    def body(*refs):
        pass

    count = len(values)
    return pl.pallas_call(
        body,
        in_specs=[pl.BlockSpec(memory_space=pl.ANY)] * (count + 1),
        out_specs=[pl.BlockSpec(memory_space=pl.ANY)] * count,
        out_shape=[pltpu.HBM(value.shape, value.dtype) for value in values],
        input_output_aliases={i: i for i in range(count)},
        name="release",
    )(*values, after)


def query_project_kernel(place, act, weight, *refs):
    send_r, send_l, keep_r, keep_l, z_send, z_next, z_mine, x_other, x_mine, product = refs[-10:]
    product[...] = jnp.dot(act[...], weight[0], preferred_element_type=jnp.float32)

    def put(owner, other, mine):
        start = pl.multiple_of(place[owner] * 2 * BLOCK, 2 * BLOCK)
        columns = product[:, pl.ds(start, 2 * BLOCK)]
        low, high = columns[:, :BLOCK], columns[:, BLOCK:]
        other[0][other[1]] = jnp.where(place[4] == 0, high, low)
        mine[0][mine[1]] = jnp.where(place[4] == 0, low, high)

    def z_step(half):
        for owner in range(4):
            piece = 2 * owner + half
            other = (z_send, piece) if piece < 3 else (z_next, piece - 3)
            put(owner, other, (z_mine, piece))

    def x_step(half):
        far, right, left = (
            ((send_r, 0), (keep_r, 0), (send_l, 2)),
            ((send_l, 0), (send_r, 2), (keep_l, 0)),
        )[half]
        for owner, (ref, piece) in enumerate((far, right, left)):
            put(owner, (ref, piece), (ref, piece + 1))
        put(3, (x_other, half), (x_mine, half))

    for i in range(4):
        pl.when(pl.program_id(0) == i)(
            functools.partial(z_step if i < 2 else x_step, i % 2)
        )


def query_second_sum_kernel(
    dep_r, dep_l, got_r, got_l, z_got, z_next, z_mine, x_other, out_r, out_l, out_x
):
    out_r[0] = z_mine[2] + z_got[2] + dep_r[2]
    out_r[1] = z_mine[3] + z_next[0]
    out_l[0] = z_mine[4] + z_next[1]
    out_l[1] = z_mine[5] + z_next[2] + dep_l[2]
    out_x[0] = x_other[0] + (dep_r[0] + got_l[2])
    out_x[1] = x_other[1] + (got_r[2] + dep_l[0])


def query_beside_kernel(dep_r, dep_l, got_r, got_l, z_next, z_mine, x_mine, out):
    out[0] = z_mine[6] + z_next[3]
    out[1] = z_mine[7] + z_next[4]
    out[2] = x_mine[0] + (dep_r[1] + got_l[3])
    out[3] = x_mine[1] + (got_r[3] + dep_l[1])


def reduce_kv(halves, place, activations, weight, beside):
    make = functools.partial(
        project, halves=halves, place=place, activations=activations, weight=weight
    )
    send_r, send_l, z_send, z_mine = make(
        first_kernel, owner=0, steps=2, outs=[(2, "vmem")] * 4
    )
    got_r, got_l, z_got = shift_x(send_r, 1), shift_x(send_l, -1), swap_z(z_send)
    next_r, next_l, z_send = make(
        second_kernel, owner=1, steps=6, outs=[(5, "vmem")] * 2 + [(6, "vmem")], after=(z_mine,)
    )
    next_r, next_l = sum_call(
        kv_first_sum_kernel, halves, [5, 5], [got_r, got_l, z_got, next_r, next_l, z_mine], []
    )
    ready = beside(next_r)
    (mine,) = make(
        third_kernel,
        owner=1,
        steps=6,
        outs=[(10, "vmem")],
        after=(next_r,) + ready,
    )
    next_r, next_l, z_six = shift_x(next_r, 1), shift_x(next_l, -1), swap_z(z_send)
    last_r, last_l, last_x = piece_call(
        kv_second_sum_kernel,
        halves,
        [2, 2, 2],
        [(mine, i) for i in range(4)]
        + [(z_six, i) for i in range(4)]
        + [(next_r, 4), (next_l, 4), (mine, 6), (mine, 7)]
        + [(next_r, 2), (next_r, 0), (next_l, 0), (next_l, 2)],
        after=ready,
    )
    (part,) = piece_call(
        kv_beside_kernel,
        halves,
        [4],
        [(mine, 4), (mine, 5), (z_six, 4), (z_six, 5), (mine, 8), (mine, 9)]
        + [(next_r, 3), (next_r, 1), (next_l, 1), (next_l, 3)],
        after=(last_r,),
    )
    last_r, last_l, last_x = shift_x(last_r, 1), shift_x(last_l, -1), swap_z(last_x)
    return (part, last_r, last_l, last_x), part


def project_query(halves, place, activations, weight, after):
    features, columns = weight.shape[1:]
    shapes = [halves.shape(count) for count in (4, 4, 2, 2, 3, 5, 8, 2, 2)]
    return pl.pallas_call(
        query_project_kernel,
        grid_spec=pltpu.PrefetchScalarGridSpec(
            num_scalar_prefetch=1,
            grid=(4,),
            in_specs=[
                pl.BlockSpec((halves.rows, features), lambda i, at: (i, 0)),
                pl.BlockSpec((1, features, columns), lambda i, at: (0, 0, 0)),
                pl.BlockSpec(memory_space=pl.ANY),
            ],
            out_specs=[pl.BlockSpec(shape, lambda i, at: (0, 0, 0)) for shape in shapes],
            scratch_shapes=[pltpu.VMEM((halves.rows, columns), jnp.float32)],
        ),
        out_shape=[pltpu.HBM(shape, jnp.float32) for shape in shapes],
        compiler_params=params(24),
        name="query_project_kernel",
    )(place, activations, weight, after)


def reduce_query(halves, projected, after):
    send_r, send_l, keep_r, keep_l, z_send, z_next, z_mine, x_other, x_mine = projected
    send_r, send_l, z_send, z_next = release((send_r, send_l, z_send, z_next), after)
    got_r, got_l, z_got = shift_x(send_r, 1), shift_x(send_l, -1), swap_z(z_send)
    z_next = swap_z(z_next)
    dep_r, dep_l = sum_call(
        first_sum_kernel,
        halves,
        [3, 3],
        [got_r, got_l, z_got],
        [keep_r, keep_l, z_mine],
    )
    dep_r, dep_l = shift_x(dep_r, 1), shift_x(dep_l, -1)
    last_r, last_l, x_sum = sum_call(
        query_second_sum_kernel,
        halves,
        [2, 2, 2],
        [dep_r, dep_l, got_r, got_l, z_got, z_next],
        [z_mine, x_other],
    )
    (part,) = sum_call(
        query_beside_kernel,
        halves,
        [4],
        [dep_r, dep_l, got_r, got_l, z_next],
        [z_mine, x_mine],
        after=(last_r,),
    )
    last_r, last_l, x_sum = shift_x(last_r, 1), shift_x(last_l, -1), swap_z(x_sum)
    return part, last_r, last_l, x_sum


def summed(part, last_r, last_l, last_x):
    return [part[h] + (last_r[h] + last_l[h]) for h in range(2)] + [
        part[2 + h] + last_x[h] for h in range(2)
    ]


def split_bf16(table):
    high = table.astype(np.float32).astype(ml_dtypes.bfloat16)
    low = (table - high.astype(np.float64)).astype(ml_dtypes.bfloat16)
    return high, low


@functools.lru_cache(None)
def tables(length):
    rows = length // BLOCK
    period = 2 * length
    odd = np.arange(rows) + 0.5
    first = -2 * np.pi * np.outer(odd, np.arange(rows)) / (2 * rows)
    turn = -2 * np.pi * np.outer(odd, np.arange(BLOCK)) / period
    second = -2 * np.pi * (np.outer(np.arange(BLOCK), np.arange(BLOCK)) % BLOCK) / BLOCK
    c, s = np.cos(second), np.sin(second)
    scale = 1.0 / length
    return (
        split_bf16(np.concatenate([np.cos(first), np.sin(first)], axis=0)),
        (np.cos(turn).astype(np.float32), np.sin(turn).astype(np.float32)),
        split_bf16(np.block([[c, s], [-s, c]])),
        split_bf16(np.block([[c, -s], [s, c]])),
        split_bf16(np.concatenate([np.cos(first).T, np.sin(first).T], axis=1) * scale),
    )


def split_value(value):
    high = value.astype(jnp.bfloat16)
    return high, (value - high.astype(jnp.float32)).astype(jnp.bfloat16)


def dot3(left, right):
    dot = functools.partial(jnp.dot, preferred_element_type=jnp.float32)
    return dot(left[0], right[0]) + (dot(left[0], right[1]) + dot(left[1], right[0]))


def forward(signals, first, turn, second):
    rows = signals[0].shape[0]
    part = dot3(first, split_value(jnp.concatenate(signals, axis=1)))
    turned = []
    for c in range(len(signals)):
        real = part[:rows, c * BLOCK : (c + 1) * BLOCK]
        imag = part[rows:, c * BLOCK : (c + 1) * BLOCK]
        turned.append(
            jnp.concatenate(
                [real * turn[0] - imag * turn[1], real * turn[1] + imag * turn[0]], axis=1
            )
        )
    return dot3(split_value(jnp.concatenate(turned, axis=0)), second)


def conv_kernel(
    both_ref, f_hi, f_lo, t_re, t_im, s_hi, s_lo, b_hi, b_lo, i_hi, i_lo, out_ref
):
    seqs, _, channels, blocks, _ = both_ref.shape
    rows = seqs * blocks
    turn = (t_re[...], t_im[...])
    kv_spectrum, taps_spectrum = (
        forward(
            [both_ref[:, part, c].reshape(rows, BLOCK) for c in range(channels)],
            (f_hi[...], f_lo[...]),
            turn,
            (s_hi[...], s_lo[...]),
        )
        for part in range(2)
    )
    real, imag = kv_spectrum[:, :BLOCK], kv_spectrum[:, BLOCK:]
    taps_real, taps_imag = taps_spectrum[:, :BLOCK], taps_spectrum[:, BLOCK:]
    product = jnp.concatenate(
        [real * taps_real - imag * taps_imag, real * taps_imag + imag * taps_real], axis=1
    )
    back = dot3(split_value(product), (b_hi[...], b_lo[...]))
    columns = []
    for c in range(channels):
        real = back[c * rows : (c + 1) * rows, :BLOCK]
        imag = back[c * rows : (c + 1) * rows, BLOCK:]
        columns.append(
            jnp.concatenate(
                [real * turn[0] + imag * turn[1], imag * turn[0] - real * turn[1]], axis=0
            )
        )
    result = dot3((i_hi[...], i_lo[...]), split_value(jnp.concatenate(columns, axis=1)))
    for c in range(channels):
        out_ref[:, c] = result[:, c * BLOCK : (c + 1) * BLOCK].reshape(seqs, blocks, BLOCK)


def turn_blocks(value_ref, out_ref):
    for b in range(out_ref.shape[1]):
        out_ref[:, b, :] = value_ref[b * BLOCK : (b + 1) * BLOCK, :].T


def taps_turn_kernel(taps_ref, out_ref):
    turn_blocks(taps_ref, out_ref)


def kv_kernel(part, last_r, last_l, last_x, taps, out_ref, kv_ref, turned_ref):
    key, value, x_key, x_value = summed(part, last_r, last_l, last_x)
    rows = key.shape[0]
    kv_ref[:rows] = key * value
    kv_ref[rows:] = x_key * x_value
    turn_blocks(kv_ref, turned_ref)
    shape = out_ref.shape[:1] + out_ref.shape[2:]
    out_ref[:, 0] = turned_ref[...].reshape(shape)
    out_ref[:, 1] = taps[...].reshape(shape)


def query_kernel(*refs):
    parts, out_ref = refs[:-1], refs[-1]
    for i, query in enumerate(summed(*parts)):
        rows = query.shape[0]
        out_ref[i * rows : (i + 1) * rows] = query


def gate_kernel(conv_ref, query_ref, out_ref):
    for b in range(conv_ref.shape[1]):
        rows = slice(b * BLOCK, (b + 1) * BLOCK)
        out_ref[rows] = conv_ref[:, b, :].T * query_ref[rows]


def call(kernel, out_shape, *operands, after=(), scratch=(), tables=(), to_hbm=False):
    def body(*refs):
        count = len(operands) + len(tables)
        kernel(*refs[:count], *refs[count + len(after) :])

    def whole(shape):
        return pl.BlockSpec(shape, lambda i: (0,) * len(shape))

    return pl.pallas_call(
        body,
        grid=(1,),
        in_specs=[pl.BlockSpec(memory_space=pltpu.VMEM)] * len(operands)
        + [whole(table.shape) for table in tables]
        + [pl.BlockSpec(memory_space=pl.ANY)] * len(after),
        out_specs=whole(out_shape) if to_hbm else pl.BlockSpec(memory_space=pltpu.VMEM),
        out_shape=pltpu.HBM(out_shape, jnp.float32)
        if to_hbm
        else jax.ShapeDtypeStruct(out_shape, jnp.float32),
        scratch_shapes=scratch,
        compiler_params=params(24),
        name=kernel.__name__,
    )(*operands, *[in_hbm(jnp.asarray(table)) for table in tables], *after)


def exchange(value):
    return lax.all_to_all(value, "seq", split_axis=0, concat_axis=0, tiled=True)


def on_device(activations, proj_weight, filter_taps):
    tokens, channels = filter_taps.shape
    seqs = lax.axis_size("seq")
    length = tokens * seqs
    blocks = tokens // BLOCK
    owned = channels // seqs
    turned_shape = (channels, blocks, BLOCK)
    moved_shape = (seqs, owned, blocks, BLOCK)
    first, turn, second, back, inverse = tables(length)

    chan = lax.axis_index("chan")
    x_at, z_at = chan // 2, chan % 2
    owners = [(x_at + dx) % X_SIZE for dx in (2, 1, 3, 0)]
    place = jnp.stack(owners + [z_at]).astype(jnp.int32)
    weight = in_hbm(jnp.transpose(proj_weight, (1, 0, 2)))
    activations = in_hbm(activations)

    hold = {}
    kv_halves, q_halves = Halves(tokens, (1, 2)), Halves(tokens, (0,))

    def prepare(ready):
        hold["taps"] = call(taps_turn_kernel, turned_shape, filter_taps, after=(ready,))
        hold["query"] = project_query(q_halves, place, activations, weight, ready)
        return hold["query"][0], hold["taps"]

    kv_parts, kv_part = reduce_kv(kv_halves, place, activations, weight, prepare)
    both = call(
        kv_kernel,
        (seqs, 2, owned, blocks, BLOCK),
        *kv_parts,
        hold["taps"],
        scratch=[
            pltpu.VMEM((tokens, channels), jnp.float32),
            pltpu.VMEM(turned_shape, jnp.float32),
        ],
        to_hbm=True,
    )
    q_parts = reduce_query(q_halves, hold["query"], kv_part)
    convolved = call(
        conv_kernel,
        moved_shape,
        exchange(both),
        tables=first + turn + second + back + inverse,
        to_hbm=True,
    )
    query = call(query_kernel, (tokens, channels), *q_parts)
    home = exchange(convolved).reshape(turned_shape)
    return call(gate_kernel, (tokens, channels), home, query)


def solution(mesh):
    return jax.shard_map(
        on_device,
        mesh=mesh,
        in_specs=(P("seq", "chan"), P("chan", None, None), P("seq", "chan")),
        out_specs=P("seq", "chan"),
        check_vma=False,
    )
```

```python
import functools

import jax
import jax.numpy as jnp
import ml_dtypes
import numpy as np
from jax import lax
from jax.experimental import pallas as pl
from jax.experimental.pallas import tpu as pltpu
from jax.sharding import PartitionSpec as P

BLOCK = 128
X_SIZE = 4
CHUNK = 512


def params(mebibytes):
    return pltpu.CompilerParams(vmem_limit_bytes=mebibytes * 1024 * 1024)


def in_hbm(value):
    return pltpu.with_memory_space_constraint(value, pltpu.HBM)


def shift_x(value, step):
    return lax.ppermute(value, "chan", [(i, (i + 2 * step) % 8) for i in range(8)])


def swap_z(value):
    return lax.ppermute(value, "chan", [(i, i ^ 1) for i in range(8)])


def parts_of(rows, weight, z_at):
    product = jnp.dot(rows, weight, preferred_element_type=jnp.float32)
    low, high = product[:, :BLOCK], product[:, BLOCK:]
    return jnp.where(z_at == 0, high, low), jnp.where(z_at == 0, low, high)


class Halves:
    def __init__(self, tokens, columns):
        self.columns = columns
        parts = 2 // len(columns)
        self.rows = tokens // 2 // parts
        self.z_start = [h % parts * self.rows for h in range(2)]
        self.x_start = [tokens // 2 + start for start in self.z_start]

    def shape(self, count):
        return (count, self.rows, BLOCK)

    def fill(self, place, act, weight, half, x_outs, z_outs):
        for begin, outs in ((self.x_start[half], x_outs), (self.z_start[half], z_outs)):
            if outs == (None, None):
                continue
            for start in range(0, self.rows, CHUNK):
                rows = act[begin + start : begin + start + CHUNK]
                for out, part in zip(outs, parts_of(rows, weight[0], place[4])):
                    if out is not None:
                        out[0][out[1], start : start + CHUNK] = part


def first_kernel(halves, place, act, weight, outs):
    send_r, send_l, z_other, z_mine = outs
    for half, send in enumerate((send_r, send_l)):
        pl.when(pl.program_id(0) == half)(
            functools.partial(
                halves.fill,
                place,
                act,
                weight,
                half,
                ((send, 0), (send, 1)),
                ((z_other, half), (z_mine, half)),
            )
        )


def second_kernel(halves, place, act, weight, outs):
    next_r, next_l, z_send = outs
    x_outs = (
        ((next_r, 2), (next_r, 3)),
        ((next_r, 0), (next_r, 1)),
        ((next_l, 0), (next_l, 1)),
        ((next_l, 2), (next_l, 3)),
        (None, None),
    )
    for i, outs in enumerate(x_outs):
        pl.when(pl.program_id(0) == i)(
            functools.partial(
                halves.fill, place, act, weight, i % 2, outs, ((z_send, i), None)
            )
        )


def third_kernel(halves, place, act, weight, outs):
    (mine,) = outs
    for i in range(6):
        x_outs = (None, None) if i < 4 else ((mine, i + 3), (mine, i + 5))
        z_other = (mine, 6) if i == 5 else None
        pl.when(pl.program_id(0) == i)(
            functools.partial(
                halves.fill, place, act, weight, i % 2, x_outs, (z_other, (mine, i))
            )
        )


def project(kernel, halves, place, activations, weight, owner, steps, outs, after=()):
    first, last = halves.columns[0], halves.columns[-1]

    def weight_block(i, at):
        return (first + (last - first) * (i % 2), 0, at[owner + i // 2])

    def body(at, act, weight_ref, *refs):
        kernel(halves, at, act, weight_ref, refs[len(after) :])

    specs, results = [], []
    for count, where in outs:
        if where == "vmem":
            specs.append(pl.BlockSpec(memory_space=pltpu.VMEM))
            results.append(jax.ShapeDtypeStruct(halves.shape(count), jnp.float32))
            continue
        results.append(pltpu.HBM(halves.shape(count), jnp.float32))
        if where == "hbm":
            specs.append(pl.BlockSpec(halves.shape(count), lambda i, at: (0, 0, 0)))
        else:
            specs.append(
                pl.BlockSpec(
                    halves.shape(1),
                    lambda i, at, start=where, end=count - 1: (
                        jnp.clip(i - start, 0, end),
                        0,
                        0,
                    ),
                )
            )
    return pl.pallas_call(
        body,
        grid_spec=pltpu.PrefetchScalarGridSpec(
            num_scalar_prefetch=1,
            grid=(steps,),
            in_specs=[
                pl.BlockSpec(activations.shape, lambda i, at: (0, 0)),
                pl.BlockSpec((1, weight.shape[1], 2 * BLOCK), weight_block),
            ]
            + [pl.BlockSpec(memory_space=pl.ANY)] * len(after),
            out_specs=specs,
        ),
        out_shape=results,
        compiler_params=params(24),
        name=kernel.__name__,
    )(place, activations, weight, *after)


def sum_call(kernel, halves, counts, near, far, after=()):
    tile = min(BLOCK, halves.rows)

    def body(*refs):
        rows = pl.ds(pl.multiple_of(pl.program_id(0) * tile, tile), tile)
        ins = [ref.at[:, rows] for ref in refs[: len(near)]]
        ins += refs[len(near) : len(near) + len(far)]
        kernel(*ins, *[ref.at[:, rows] for ref in refs[len(near) + len(far) + len(after) :]])

    return pl.pallas_call(
        body,
        grid=(halves.rows // tile,),
        in_specs=[pl.BlockSpec(memory_space=pltpu.VMEM)] * len(near)
        + [pl.BlockSpec((value.shape[0], tile, BLOCK), lambda i: (0, i, 0)) for value in far]
        + [pl.BlockSpec(memory_space=pl.ANY)] * len(after),
        out_specs=[pl.BlockSpec(memory_space=pltpu.VMEM)] * len(counts),
        out_shape=[jax.ShapeDtypeStruct(halves.shape(count), jnp.float32) for count in counts],
        compiler_params=params(8),
        name=kernel.__name__,
    )(*near, *[in_hbm(value) for value in far], *after)


def first_sum_kernel(got_r, got_l, z_got, keep_r, keep_l, z_mine, out_r, out_l):
    for half, (keep, got, out) in enumerate(((keep_r, got_r, out_r), (keep_l, got_l, out_l))):
        out[0] = keep[0] + got[0]
        out[1] = keep[1] + got[1]
        out[2] = z_mine[half] + z_got[half]


def kv_first_sum_kernel(got_r, got_l, z_got, next_r, next_l, z_mine, out_r, out_l):
    for half, (mine, got, out) in enumerate(((next_r, got_r, out_r), (next_l, got_l, out_l))):
        out[0] = mine[0]
        out[1] = mine[1]
        out[2] = mine[2] + got[0]
        out[3] = mine[3] + got[1]
        out[4] = z_mine[half] + z_got[half]


def piece_call(kernel, halves, counts, pieces, after=()):
    tile = min(2 * BLOCK, halves.rows)

    def body(*refs):
        kernel(*refs[: len(pieces)], *refs[len(pieces) + len(after) :])

    def spec(index):
        return pl.BlockSpec((1, tile, BLOCK), lambda i: (index, i, 0))

    return pl.pallas_call(
        body,
        grid=(halves.rows // tile,),
        in_specs=[spec(index) for _, index in pieces]
        + [pl.BlockSpec(memory_space=pl.ANY)] * len(after),
        out_specs=[pl.BlockSpec((n, tile, BLOCK), lambda i: (0, i, 0)) for n in counts],
        out_shape=[jax.ShapeDtypeStruct(halves.shape(count), jnp.float32) for count in counts],
        compiler_params=params(12),
        name=kernel.__name__,
    )(*[value for value, _ in pieces], *after)


def kv_other_kernel(own_k, own_v, r_k, r_v, l_k, l_v, late, out):
    out[0:1] = own_k[...] + (r_k[...] + l_k[...])
    out[1:2] = own_v[...] + (r_v[...] + l_v[...])
    out[2:3] = late[...]


def kv_last_kernel(m0, m1, m2, m3, g0, g1, g2, g3, next_r, next_l, out_r, out_l):
    out_r[0:1] = m0[...] + g0[...] + next_r[...]
    out_r[1:2] = m1[...] + g1[...]
    out_l[0:1] = m2[...] + g2[...]
    out_l[1:2] = m3[...] + g3[...] + next_l[...]


def kv_beside_kernel(m4, m5, g4, own_k, own_v, r_k, r_v, l_k, l_v, out):
    out[0:1] = m4[...] + g4[...]
    out[1:2] = m5[...]
    out[2:3] = own_k[...] + (r_k[...] + l_k[...])
    out[3:4] = own_v[...] + (r_v[...] + l_v[...])


def release(values, after):
    def body(*refs):
        pass

    count = len(values)
    return pl.pallas_call(
        body,
        in_specs=[pl.BlockSpec(memory_space=pl.ANY)] * (count + 1),
        out_specs=[pl.BlockSpec(memory_space=pl.ANY)] * count,
        out_shape=[pltpu.HBM(value.shape, value.dtype) for value in values],
        input_output_aliases={i: i for i in range(count)},
        name="release",
    )(*values, after)


def query_project_kernel(place, act, weight, *refs):
    send_r, send_l, keep_r, keep_l, z_send, z_next, z_mine, x_other, x_mine, product = refs[-10:]
    product[...] = jnp.dot(act[...], weight[0], preferred_element_type=jnp.float32)

    def put(owner, other, mine):
        start = pl.multiple_of(place[owner] * 2 * BLOCK, 2 * BLOCK)
        columns = product[:, pl.ds(start, 2 * BLOCK)]
        low, high = columns[:, :BLOCK], columns[:, BLOCK:]
        other[0][other[1]] = jnp.where(place[4] == 0, high, low)
        mine[0][mine[1]] = jnp.where(place[4] == 0, low, high)

    def z_step(half):
        for owner in range(4):
            piece = 2 * owner + half
            other = (z_send, piece) if piece < 3 else (z_next, piece - 3)
            put(owner, other, (z_mine, piece))

    def x_step(half):
        far, right, left = (
            ((send_r, 0), (keep_r, 0), (send_l, 2)),
            ((send_l, 0), (send_r, 2), (keep_l, 0)),
        )[half]
        for owner, (ref, piece) in enumerate((far, right, left)):
            put(owner, (ref, piece), (ref, piece + 1))
        put(3, (x_other, half), (x_mine, half))

    for i in range(4):
        pl.when(pl.program_id(0) == i)(
            functools.partial(z_step if i < 2 else x_step, i % 2)
        )


def query_second_sum_kernel(
    dep_r, dep_l, got_r, got_l, z_got, z_next, z_mine, x_other, out_r, out_l, out_x
):
    out_r[0] = z_mine[2] + z_got[2] + dep_r[2]
    out_r[1] = z_mine[3] + z_next[0]
    out_l[0] = z_mine[4] + z_next[1]
    out_l[1] = z_mine[5] + z_next[2] + dep_l[2]
    out_x[0] = x_other[0] + (dep_r[0] + got_l[2])
    out_x[1] = x_other[1] + (got_r[2] + dep_l[0])


def query_beside_kernel(dep_r, dep_l, got_r, got_l, z_next, z_mine, x_mine, out):
    out[0] = z_mine[6] + z_next[3]
    out[1] = z_mine[7] + z_next[4]
    out[2] = x_mine[0] + (dep_r[1] + got_l[3])
    out[3] = x_mine[1] + (got_r[3] + dep_l[1])


def reduce_kv(halves, place, activations, weight, beside):
    make = functools.partial(
        project, halves=halves, place=place, activations=activations, weight=weight
    )
    send_r, send_l, z_send, z_mine = make(
        first_kernel, owner=0, steps=2, outs=[(2, "vmem")] * 4
    )
    got_r, got_l, z_got = shift_x(send_r, 1), shift_x(send_l, -1), swap_z(z_send)
    next_r, next_l, z_send = make(
        second_kernel, owner=1, steps=5, outs=[(5, "vmem")] * 3, after=(z_mine,)
    )
    next_r, next_l = sum_call(
        kv_first_sum_kernel, halves, [5, 5], [got_r, got_l, z_got, next_r, next_l, z_mine], []
    )
    ready = beside(next_r)
    (mine,) = make(
        third_kernel,
        owner=1,
        steps=6,
        outs=[(11, "vmem")],
        after=(next_r,) + ready[1:],
    )
    next_r, next_l, z_five = shift_x(next_r, 1), shift_x(next_l, -1), swap_z(z_send)
    (last_xz,) = piece_call(
        kv_other_kernel,
        halves,
        [3],
        [(mine, 7), (mine, 8), (next_r, 2), (next_r, 0), (next_l, 0), (next_l, 2), (mine, 6)],
        after=(z_five,) + ready,
    )
    last_r, last_l = piece_call(
        kv_last_kernel,
        halves,
        [2, 2],
        [(mine, i) for i in range(4)]
        + [(z_five, i) for i in range(4)]
        + [(next_r, 4), (next_l, 4)],
        after=(last_xz,),
    )
    (part,) = piece_call(
        kv_beside_kernel,
        halves,
        [4],
        [(mine, 4), (mine, 5), (z_five, 4), (mine, 9), (mine, 10)]
        + [(next_r, 3), (next_r, 1), (next_l, 1), (next_l, 3)],
        after=(last_r,),
    )
    last_r, last_l, last_xz = shift_x(last_r, 1), shift_x(last_l, -1), swap_z(last_xz)
    return (part, last_r, last_l, last_xz), part


def project_query(halves, place, activations, weight, after):
    features, columns = weight.shape[1:]
    shapes = [halves.shape(count) for count in (4, 4, 2, 2, 3, 5, 8, 2, 2)]
    return pl.pallas_call(
        query_project_kernel,
        grid_spec=pltpu.PrefetchScalarGridSpec(
            num_scalar_prefetch=1,
            grid=(4,),
            in_specs=[
                pl.BlockSpec((halves.rows, features), lambda i, at: (i, 0)),
                pl.BlockSpec((1, features, columns), lambda i, at: (0, 0, 0)),
                pl.BlockSpec(memory_space=pl.ANY),
            ],
            out_specs=[pl.BlockSpec(shape, lambda i, at: (0, 0, 0)) for shape in shapes],
            scratch_shapes=[pltpu.VMEM((halves.rows, columns), jnp.float32)],
        ),
        out_shape=[pltpu.HBM(shape, jnp.float32) for shape in shapes],
        compiler_params=params(24),
        name="query_project_kernel",
    )(place, activations, weight, after)


def reduce_query(halves, projected, after):
    send_r, send_l, keep_r, keep_l, z_send, z_next, z_mine, x_other, x_mine = projected
    send_r, send_l, z_send, z_next = release((send_r, send_l, z_send, z_next), after)
    got_r, got_l, z_got = shift_x(send_r, 1), shift_x(send_l, -1), swap_z(z_send)
    z_next = swap_z(z_next)
    dep_r, dep_l = sum_call(
        first_sum_kernel,
        halves,
        [3, 3],
        [got_r, got_l, z_got],
        [keep_r, keep_l, z_mine],
    )
    dep_r, dep_l = shift_x(dep_r, 1), shift_x(dep_l, -1)
    last_r, last_l, x_sum = sum_call(
        query_second_sum_kernel,
        halves,
        [2, 2, 2],
        [dep_r, dep_l, got_r, got_l, z_got, z_next],
        [z_mine, x_other],
    )
    (part,) = sum_call(
        query_beside_kernel,
        halves,
        [4],
        [dep_r, dep_l, got_r, got_l, z_next],
        [z_mine, x_mine],
        after=(last_r,),
    )
    last_r, last_l, x_sum = shift_x(last_r, 1), shift_x(last_l, -1), swap_z(x_sum)
    return part, last_r, last_l, x_sum


def summed(part, last_r, last_l, last_x):
    z_total = [part[h] + (last_r[h] + last_l[h]) for h in range(2)]
    if last_x.shape[0] == 3:
        z_total[1] = z_total[1] + last_x[2]
    return z_total + [part[2 + h] + last_x[h] for h in range(2)]


def split_bf16(table):
    high = table.astype(np.float32).astype(ml_dtypes.bfloat16)
    low = (table - high.astype(np.float64)).astype(ml_dtypes.bfloat16)
    return high, low


@functools.lru_cache(None)
def tables(length):
    rows = length // BLOCK
    period = 2 * length
    odd = np.arange(rows) + 0.5
    first = -2 * np.pi * np.outer(odd, np.arange(rows)) / (2 * rows)
    turn = -2 * np.pi * np.outer(odd, np.arange(BLOCK)) / period
    second = -2 * np.pi * (np.outer(np.arange(BLOCK), np.arange(BLOCK)) % BLOCK) / BLOCK
    c, s = np.cos(second), np.sin(second)
    scale = 1.0 / length
    return (
        split_bf16(np.concatenate([np.cos(first), np.sin(first)], axis=0)),
        (np.cos(turn).astype(np.float32), np.sin(turn).astype(np.float32)),
        split_bf16(np.block([[c, s], [-s, c]])),
        split_bf16(np.block([[c, -s], [s, c]])),
        split_bf16(np.concatenate([np.cos(first).T, np.sin(first).T], axis=1) * scale),
    )


def split_value(value):
    high = value.astype(jnp.bfloat16)
    return high, (value - high.astype(jnp.float32)).astype(jnp.bfloat16)


def dot3(left, right):
    dot = functools.partial(jnp.dot, preferred_element_type=jnp.float32)
    return dot(left[0], right[0]) + (dot(left[0], right[1]) + dot(left[1], right[0]))


def forward(signal_ref, first, turn, second):
    seqs, channels = signal_ref.shape[:2]
    rows = seqs * signal_ref.shape[2]
    signal = jnp.concatenate(
        [signal_ref[:, c].reshape(rows, BLOCK) for c in range(channels)], axis=1
    )
    part = dot3(first, split_value(signal))
    turned = []
    for c in range(channels):
        real = part[:rows, c * BLOCK : (c + 1) * BLOCK]
        imag = part[rows:, c * BLOCK : (c + 1) * BLOCK]
        turned.append(
            jnp.concatenate(
                [real * turn[0] - imag * turn[1], real * turn[1] + imag * turn[0]], axis=1
            )
        )
    return dot3(split_value(jnp.concatenate(turned, axis=0)), second)


def taps_kernel(taps_ref, f_hi, f_lo, t_re, t_im, s_hi, s_lo, out_ref):
    out_ref[...] = forward(
        taps_ref, (f_hi[...], f_lo[...]), (t_re[...], t_im[...]), (s_hi[...], s_lo[...])
    )


def conv_kernel(
    kv_ref, spec_ref, f_hi, f_lo, t_re, t_im, s_hi, s_lo, b_hi, b_lo, i_hi, i_lo, out_ref
):
    seqs, channels, blocks, _ = kv_ref.shape
    rows = seqs * blocks
    turn = (t_re[...], t_im[...])
    spectrum = forward(kv_ref, (f_hi[...], f_lo[...]), turn, (s_hi[...], s_lo[...]))
    real, imag = spectrum[:, :BLOCK], spectrum[:, BLOCK:]
    taps_real, taps_imag = spec_ref[:, :BLOCK], spec_ref[:, BLOCK:]
    product = jnp.concatenate(
        [real * taps_real - imag * taps_imag, real * taps_imag + imag * taps_real], axis=1
    )
    back = dot3(split_value(product), (b_hi[...], b_lo[...]))
    columns = []
    for c in range(channels):
        real = back[c * rows : (c + 1) * rows, :BLOCK]
        imag = back[c * rows : (c + 1) * rows, BLOCK:]
        columns.append(
            jnp.concatenate(
                [real * turn[0] + imag * turn[1], imag * turn[0] - real * turn[1]], axis=0
            )
        )
    result = dot3((i_hi[...], i_lo[...]), split_value(jnp.concatenate(columns, axis=1)))
    for c in range(channels):
        out_ref[:, c] = result[:, c * BLOCK : (c + 1) * BLOCK].reshape(seqs, blocks, BLOCK)


def turn_blocks(value_ref, out_ref):
    for b in range(out_ref.shape[1]):
        out_ref[:, b, :] = value_ref[b * BLOCK : (b + 1) * BLOCK, :].T


def taps_turn_kernel(taps_ref, out_ref):
    turn_blocks(taps_ref, out_ref)


def kv_kernel(*refs):
    parts, out_ref, kv_ref = refs[:-2], refs[-2], refs[-1]
    z_key, z_value, x_key, x_value = summed(*parts)
    rows = z_key.shape[0]
    kv_ref[:rows] = z_key * z_value
    kv_ref[rows:] = x_key * x_value
    turn_blocks(kv_ref, out_ref)


def query_kernel(*refs):
    parts, out_ref = refs[:-1], refs[-1]
    for i, query in enumerate(summed(*parts)):
        rows = query.shape[0]
        out_ref[i * rows : (i + 1) * rows] = query


def gate_kernel(conv_ref, query_ref, out_ref):
    for b in range(conv_ref.shape[1]):
        rows = slice(b * BLOCK, (b + 1) * BLOCK)
        out_ref[rows] = conv_ref[:, b, :].T * query_ref[rows]


def call(kernel, out_shape, *operands, after=(), scratch=(), tables=(), to_hbm=False):
    def body(*refs):
        count = len(operands) + len(tables)
        kernel(*refs[:count], *refs[count + len(after) :])

    def whole(shape):
        return pl.BlockSpec(shape, lambda i: (0,) * len(shape))

    return pl.pallas_call(
        body,
        grid=(1,),
        in_specs=[pl.BlockSpec(memory_space=pltpu.VMEM)] * len(operands)
        + [whole(table.shape) for table in tables]
        + [pl.BlockSpec(memory_space=pl.ANY)] * len(after),
        out_specs=whole(out_shape) if to_hbm else pl.BlockSpec(memory_space=pltpu.VMEM),
        out_shape=pltpu.HBM(out_shape, jnp.float32)
        if to_hbm
        else jax.ShapeDtypeStruct(out_shape, jnp.float32),
        scratch_shapes=scratch,
        compiler_params=params(24),
        name=kernel.__name__,
    )(*operands, *[in_hbm(jnp.asarray(table)) for table in tables], *after)


def exchange(value):
    return lax.all_to_all(value, "seq", split_axis=0, concat_axis=0, tiled=True)


def on_device(activations, proj_weight, filter_taps):
    tokens, channels = filter_taps.shape
    seqs = lax.axis_size("seq")
    length = tokens * seqs
    blocks = tokens // BLOCK
    owned = channels // seqs
    turned_shape = (channels, blocks, BLOCK)
    moved_shape = (seqs, owned, blocks, BLOCK)
    first, turn, second, back, inverse = tables(length)

    chan = lax.axis_index("chan")
    x_at, z_at = chan // 2, chan % 2
    owners = [(x_at + dx) % X_SIZE for dx in (2, 1, 3, 0)]
    place = jnp.stack(owners + [z_at]).astype(jnp.int32)
    weight = in_hbm(jnp.transpose(proj_weight, (1, 0, 2)))
    activations = in_hbm(activations)

    hold = {}
    kv_halves, q_halves = Halves(tokens, (1, 2)), Halves(tokens, (0,))

    def prepare(ready):
        taps = call(taps_turn_kernel, turned_shape, filter_taps, after=(ready,), to_hbm=True)
        hold["taps"] = exchange(taps.reshape(moved_shape))
        hold["query"] = project_query(q_halves, place, activations, weight, ready)
        return hold["taps"], hold["query"][0]

    kv_parts, kv_part = reduce_kv(kv_halves, place, activations, weight, prepare)
    spectrum = call(
        taps_kernel,
        (owned * length // BLOCK, 2 * BLOCK),
        hold["taps"],
        tables=first + turn + second,
        after=(kv_part,),
        to_hbm=True,
    )
    kv = call(
        kv_kernel,
        turned_shape,
        *kv_parts,
        after=(spectrum,),
        scratch=[pltpu.VMEM((tokens, channels), jnp.float32)],
        to_hbm=True,
    )
    q_parts = reduce_query(q_halves, hold["query"], spectrum)
    moved = exchange(kv.reshape(moved_shape))
    convolved = call(
        conv_kernel,
        moved_shape,
        moved,
        tables=(spectrum,) + first + turn + second + back + inverse,
        to_hbm=True,
    )
    query = call(query_kernel, (tokens, channels), *q_parts)
    home = exchange(convolved).reshape(turned_shape)
    return call(gate_kernel, (tokens, channels), home, query)


def solution(mesh):
    return jax.shard_map(
        on_device,
        mesh=mesh,
        in_specs=(P("seq", "chan"), P("chan", None, None), P("seq", "chan")),
        out_specs=P("seq", "chan"),
        check_vma=False,
    )
```

```python
import functools

import jax
import jax.numpy as jnp
import ml_dtypes
import numpy as np
from jax import lax
from jax.experimental import pallas as pl
from jax.experimental.pallas import tpu as pltpu
from jax.sharding import PartitionSpec as P

BLOCK = 128
X_SIZE = 4
CHUNK = 512


def params(mebibytes):
    return pltpu.CompilerParams(vmem_limit_bytes=mebibytes * 1024 * 1024)


def in_hbm(value):
    return pltpu.with_memory_space_constraint(value, pltpu.HBM)


def shift_x(value, step):
    return lax.ppermute(value, "chan", [(i, (i + 2 * step) % 8) for i in range(8)])


def swap_z(value):
    return lax.ppermute(value, "chan", [(i, i ^ 1) for i in range(8)])


def parts_of(rows, weight, z_at):
    product = jnp.dot(rows, weight, preferred_element_type=jnp.float32)
    low, high = product[:, :BLOCK], product[:, BLOCK:]
    return jnp.where(z_at == 0, high, low), jnp.where(z_at == 0, low, high)


class Halves:
    def __init__(self, tokens, columns):
        self.columns = columns
        parts = 2 // len(columns)
        self.rows = tokens // 2 // parts
        self.z_start = [h % parts * self.rows for h in range(2)]
        self.x_start = [tokens // 2 + start for start in self.z_start]

    def shape(self, count):
        return (count, self.rows, BLOCK)

    def fill(self, place, act, weight, half, x_outs, z_outs):
        for begin, outs in ((self.x_start[half], x_outs), (self.z_start[half], z_outs)):
            if outs == (None, None):
                continue
            for start in range(0, self.rows, CHUNK):
                rows = act[begin + start : begin + start + CHUNK]
                for out, part in zip(outs, parts_of(rows, weight[0], place[4])):
                    if out is not None:
                        out[0][out[1], start : start + CHUNK] = part


def first_kernel(halves, place, act, weight, outs):
    send_r, send_l, z_other, z_mine = outs

    def put(other, mine):
        other[0][other[1]], mine[0][mine[1]] = parts_of(act[...], weight[0], place[4])

    for half, send in enumerate((send_r, send_l)):
        step = pl.program_id(0) - 2 * half
        pl.when(step == 0)(functools.partial(put, (send, 0), (send, 1)))
        pl.when(step == 1)(functools.partial(put, (z_other, half), (z_mine, half)))


def second_kernel(halves, place, act, weight, outs):
    next_r, next_l, z_send = outs
    x_outs = (
        ((next_r, 2), (next_r, 3)),
        ((next_r, 0), (next_r, 1)),
        ((next_l, 0), (next_l, 1)),
        ((next_l, 2), (next_l, 3)),
        (None, None),
    )
    for i, outs in enumerate(x_outs):
        pl.when(pl.program_id(0) == i)(
            functools.partial(
                halves.fill, place, act, weight, i % 2, outs, ((z_send, i), None)
            )
        )


def third_kernel(halves, place, act, weight, outs):
    (mine,) = outs
    for i in range(6):
        x_outs = (None, None) if i < 4 else ((mine, i + 3), (mine, i + 5))
        z_other = (mine, 6) if i == 5 else None
        pl.when(pl.program_id(0) == i)(
            functools.partial(
                halves.fill, place, act, weight, i % 2, x_outs, (z_other, (mine, i))
            )
        )


def project(kernel, halves, place, activations, weight, owner, steps, outs, after=(), split=1):
    first, last = halves.columns[0], halves.columns[-1]

    def weight_block(i, at):
        i = i // split
        return (first + (last - first) * (i % 2), 0, at[owner + i // 2])

    def body(at, act, weight_ref, *refs):
        kernel(halves, at, act, weight_ref, refs[len(after) :])

    specs, results = [], []
    for count, where in outs:
        if where == "vmem":
            specs.append(pl.BlockSpec(memory_space=pltpu.VMEM))
            results.append(jax.ShapeDtypeStruct(halves.shape(count), jnp.float32))
            continue
        results.append(pltpu.HBM(halves.shape(count), jnp.float32))
        if where == "hbm":
            specs.append(pl.BlockSpec(halves.shape(count), lambda i, at: (0, 0, 0)))
        else:
            specs.append(
                pl.BlockSpec(
                    halves.shape(1),
                    lambda i, at, start=where, end=count - 1: (
                        jnp.clip(i - start, 0, end),
                        0,
                        0,
                    ),
                )
            )
    return pl.pallas_call(
        body,
        grid_spec=pltpu.PrefetchScalarGridSpec(
            num_scalar_prefetch=1,
            grid=(steps,),
            in_specs=[
                pl.BlockSpec(
                    (activations.shape[0] // split, activations.shape[1]),
                    lambda i, at: (split - 1 - i % split, 0),
                ),
                pl.BlockSpec((1, weight.shape[1], 2 * BLOCK), weight_block),
            ]
            + [pl.BlockSpec(memory_space=pl.ANY)] * len(after),
            out_specs=specs,
        ),
        out_shape=results,
        compiler_params=params(24),
        name=kernel.__name__,
    )(place, activations, weight, *after)


def sum_call(kernel, halves, counts, near, far, after=()):
    tile = min(BLOCK, halves.rows)

    def body(*refs):
        rows = pl.ds(pl.multiple_of(pl.program_id(0) * tile, tile), tile)
        ins = [ref.at[:, rows] for ref in refs[: len(near)]]
        ins += refs[len(near) : len(near) + len(far)]
        kernel(*ins, *[ref.at[:, rows] for ref in refs[len(near) + len(far) + len(after) :]])

    return pl.pallas_call(
        body,
        grid=(halves.rows // tile,),
        in_specs=[pl.BlockSpec(memory_space=pltpu.VMEM)] * len(near)
        + [pl.BlockSpec((value.shape[0], tile, BLOCK), lambda i: (0, i, 0)) for value in far]
        + [pl.BlockSpec(memory_space=pl.ANY)] * len(after),
        out_specs=[pl.BlockSpec(memory_space=pltpu.VMEM)] * len(counts),
        out_shape=[jax.ShapeDtypeStruct(halves.shape(count), jnp.float32) for count in counts],
        compiler_params=params(8),
        name=kernel.__name__,
    )(*near, *[in_hbm(value) for value in far], *after)


def first_sum_kernel(got_r, got_l, z_got, keep_r, keep_l, z_mine, out_r, out_l):
    for half, (keep, got, out) in enumerate(((keep_r, got_r, out_r), (keep_l, got_l, out_l))):
        out[0] = keep[0] + got[0]
        out[1] = keep[1] + got[1]
        out[2] = z_mine[half] + z_got[half]


def kv_first_sum_kernel(got_r, got_l, z_got, next_r, next_l, z_mine, out_r, out_l):
    for half, (mine, got, out) in enumerate(((next_r, got_r, out_r), (next_l, got_l, out_l))):
        out[0] = mine[0]
        out[1] = mine[1]
        out[2] = mine[2] + got[0]
        out[3] = mine[3] + got[1]
        out[4] = z_mine[half] + z_got[half]


def piece_call(kernel, halves, counts, pieces, after=()):
    tile = min(2 * BLOCK, halves.rows)

    def body(*refs):
        kernel(*refs[: len(pieces)], *refs[len(pieces) + len(after) :])

    def spec(index):
        return pl.BlockSpec((1, tile, BLOCK), lambda i: (index, i, 0))

    return pl.pallas_call(
        body,
        grid=(halves.rows // tile,),
        in_specs=[spec(index) for _, index in pieces]
        + [pl.BlockSpec(memory_space=pl.ANY)] * len(after),
        out_specs=[pl.BlockSpec((n, tile, BLOCK), lambda i: (0, i, 0)) for n in counts],
        out_shape=[jax.ShapeDtypeStruct(halves.shape(count), jnp.float32) for count in counts],
        compiler_params=params(12),
        name=kernel.__name__,
    )(*[value for value, _ in pieces], *after)


def kv_other_kernel(own_k, own_v, r_k, r_v, l_k, l_v, late, out):
    out[0:1] = own_k[...] + (r_k[...] + l_k[...])
    out[1:2] = own_v[...] + (r_v[...] + l_v[...])
    out[2:3] = late[...]


def kv_last_kernel(m0, m1, m2, m3, g0, g1, g2, g3, next_r, next_l, out_r, out_l):
    out_r[0:1] = m0[...] + g0[...] + next_r[...]
    out_r[1:2] = m1[...] + g1[...]
    out_l[0:1] = m2[...] + g2[...]
    out_l[1:2] = m3[...] + g3[...] + next_l[...]


def kv_beside_kernel(m4, m5, g4, own_k, own_v, r_k, r_v, l_k, l_v, out):
    out[0:1] = m4[...] + g4[...]
    out[1:2] = m5[...]
    out[2:3] = own_k[...] + (r_k[...] + l_k[...])
    out[3:4] = own_v[...] + (r_v[...] + l_v[...])


def release(values, after):
    def body(*refs):
        pass

    count = len(values)
    return pl.pallas_call(
        body,
        in_specs=[pl.BlockSpec(memory_space=pl.ANY)] * (count + 1),
        out_specs=[pl.BlockSpec(memory_space=pl.ANY)] * count,
        out_shape=[pltpu.HBM(value.shape, value.dtype) for value in values],
        input_output_aliases={i: i for i in range(count)},
        name="release",
    )(*values, after)


def query_project_kernel(place, act, weight, *refs):
    send_r, send_l, keep_r, keep_l, z_send, z_next, z_mine, x_other, x_mine, product = refs[-10:]
    product[...] = jnp.dot(act[...], weight[0], preferred_element_type=jnp.float32)

    def put(owner, other, mine):
        start = pl.multiple_of(place[owner] * 2 * BLOCK, 2 * BLOCK)
        columns = product[:, pl.ds(start, 2 * BLOCK)]
        low, high = columns[:, :BLOCK], columns[:, BLOCK:]
        other[0][other[1]] = jnp.where(place[4] == 0, high, low)
        mine[0][mine[1]] = jnp.where(place[4] == 0, low, high)

    def z_step(half):
        for owner in range(4):
            piece = 2 * owner + half
            other = (z_send, piece) if piece < 3 else (z_next, piece - 3)
            put(owner, other, (z_mine, piece))

    def x_step(half):
        far, right, left = (
            ((send_r, 0), (keep_r, 0), (send_l, 2)),
            ((send_l, 0), (send_r, 2), (keep_l, 0)),
        )[half]
        for owner, (ref, piece) in enumerate((far, right, left)):
            put(owner, (ref, piece), (ref, piece + 1))
        put(3, (x_other, half), (x_mine, half))

    for i in range(4):
        pl.when(pl.program_id(0) == i)(
            functools.partial(z_step if i < 2 else x_step, i % 2)
        )


def query_second_sum_kernel(
    dep_r, dep_l, got_r, got_l, z_got, z_next, z_mine, x_other, out_r, out_l, out_x
):
    out_r[0] = z_mine[2] + z_got[2] + dep_r[2]
    out_r[1] = z_mine[3] + z_next[0]
    out_l[0] = z_mine[4] + z_next[1]
    out_l[1] = z_mine[5] + z_next[2] + dep_l[2]
    out_x[0] = x_other[0] + (dep_r[0] + got_l[2])
    out_x[1] = x_other[1] + (got_r[2] + dep_l[0])


def query_beside_kernel(dep_r, dep_l, got_r, got_l, z_next, z_mine, x_mine, out):
    out[0] = z_mine[6] + z_next[3]
    out[1] = z_mine[7] + z_next[4]
    out[2] = x_mine[0] + (dep_r[1] + got_l[3])
    out[3] = x_mine[1] + (got_r[3] + dep_l[1])


def reduce_kv(halves, place, activations, weight, beside):
    make = functools.partial(
        project, halves=halves, place=place, activations=activations, weight=weight
    )
    send_r, send_l, z_send, z_mine = make(
        first_kernel, owner=0, steps=4, outs=[(2, "vmem")] * 4, split=2
    )
    got_r, got_l, z_got = shift_x(send_r, 1), shift_x(send_l, -1), swap_z(z_send)
    next_r, next_l, z_send = make(
        second_kernel, owner=1, steps=5, outs=[(5, "vmem")] * 3, after=(z_mine,)
    )
    next_r, next_l = sum_call(
        kv_first_sum_kernel, halves, [5, 5], [got_r, got_l, z_got, next_r, next_l, z_mine], []
    )
    ready = beside(next_r)
    (mine,) = make(
        third_kernel,
        owner=1,
        steps=6,
        outs=[(11, "vmem")],
        after=(next_r,) + ready[1:],
    )
    next_r, next_l, z_five = shift_x(next_r, 1), shift_x(next_l, -1), swap_z(z_send)
    (last_xz,) = piece_call(
        kv_other_kernel,
        halves,
        [3],
        [(mine, 7), (mine, 8), (next_r, 2), (next_r, 0), (next_l, 0), (next_l, 2), (mine, 6)],
        after=(z_five,) + ready,
    )
    last_r, last_l = piece_call(
        kv_last_kernel,
        halves,
        [2, 2],
        [(mine, i) for i in range(4)]
        + [(z_five, i) for i in range(4)]
        + [(next_r, 4), (next_l, 4)],
        after=(last_xz,),
    )
    (part,) = piece_call(
        kv_beside_kernel,
        halves,
        [4],
        [(mine, 4), (mine, 5), (z_five, 4), (mine, 9), (mine, 10)]
        + [(next_r, 3), (next_r, 1), (next_l, 1), (next_l, 3)],
        after=(last_r,),
    )
    last_r, last_l, last_xz = shift_x(last_r, 1), shift_x(last_l, -1), swap_z(last_xz)
    return (part, last_r, last_l, last_xz), part


def project_query(halves, place, activations, weight, after):
    features, columns = weight.shape[1:]
    shapes = [halves.shape(count) for count in (4, 4, 2, 2, 3, 5, 8, 2, 2)]
    return pl.pallas_call(
        query_project_kernel,
        grid_spec=pltpu.PrefetchScalarGridSpec(
            num_scalar_prefetch=1,
            grid=(4,),
            in_specs=[
                pl.BlockSpec((halves.rows, features), lambda i, at: (i, 0)),
                pl.BlockSpec((1, features, columns), lambda i, at: (0, 0, 0)),
                pl.BlockSpec(memory_space=pl.ANY),
            ],
            out_specs=[pl.BlockSpec(shape, lambda i, at: (0, 0, 0)) for shape in shapes],
            scratch_shapes=[pltpu.VMEM((halves.rows, columns), jnp.float32)],
        ),
        out_shape=[pltpu.HBM(shape, jnp.float32) for shape in shapes],
        compiler_params=params(24),
        name="query_project_kernel",
    )(place, activations, weight, after)


def reduce_query(halves, projected, after):
    send_r, send_l, keep_r, keep_l, z_send, z_next, z_mine, x_other, x_mine = projected
    send_r, send_l, z_send, z_next = release((send_r, send_l, z_send, z_next), after)
    got_r, got_l, z_got = shift_x(send_r, 1), shift_x(send_l, -1), swap_z(z_send)
    z_next = swap_z(z_next)
    dep_r, dep_l = sum_call(
        first_sum_kernel,
        halves,
        [3, 3],
        [got_r, got_l, z_got],
        [keep_r, keep_l, z_mine],
    )
    dep_r, dep_l = shift_x(dep_r, 1), shift_x(dep_l, -1)
    last_r, last_l, x_sum = sum_call(
        query_second_sum_kernel,
        halves,
        [2, 2, 2],
        [dep_r, dep_l, got_r, got_l, z_got, z_next],
        [z_mine, x_other],
    )
    (part,) = sum_call(
        query_beside_kernel,
        halves,
        [4],
        [dep_r, dep_l, got_r, got_l, z_next],
        [z_mine, x_mine],
        after=(last_r,),
    )
    last_r, last_l, x_sum = shift_x(last_r, 1), shift_x(last_l, -1), swap_z(x_sum)
    return part, last_r, last_l, x_sum


def summed(part, last_r, last_l, last_x):
    z_total = [part[h] + (last_r[h] + last_l[h]) for h in range(2)]
    if last_x.shape[0] == 3:
        z_total[1] = z_total[1] + last_x[2]
    return z_total + [part[2 + h] + last_x[h] for h in range(2)]


def split_bf16(table):
    high = table.astype(np.float32).astype(ml_dtypes.bfloat16)
    low = (table - high.astype(np.float64)).astype(ml_dtypes.bfloat16)
    return high, low


@functools.lru_cache(None)
def tables(length):
    rows = length // BLOCK
    period = 2 * length
    odd = np.arange(rows) + 0.5
    first = -2 * np.pi * np.outer(odd, np.arange(rows)) / (2 * rows)
    turn = -2 * np.pi * np.outer(odd, np.arange(BLOCK)) / period
    second = -2 * np.pi * (np.outer(np.arange(BLOCK), np.arange(BLOCK)) % BLOCK) / BLOCK
    c, s = np.cos(second), np.sin(second)
    scale = 1.0 / length
    return (
        split_bf16(np.concatenate([np.cos(first), np.sin(first)], axis=0)),
        (np.cos(turn).astype(np.float32), np.sin(turn).astype(np.float32)),
        split_bf16(np.block([[c, s], [-s, c]])),
        split_bf16(np.block([[c, -s], [s, c]])),
        split_bf16(np.concatenate([np.cos(first).T, np.sin(first).T], axis=1) * scale),
    )


def split_value(value):
    high = value.astype(jnp.bfloat16)
    return high, (value - high.astype(jnp.float32)).astype(jnp.bfloat16)


def dot3(left, right):
    dot = functools.partial(jnp.dot, preferred_element_type=jnp.float32)
    return dot(left[0], right[0]) + (dot(left[0], right[1]) + dot(left[1], right[0]))


def forward(signal_ref, first, turn, second):
    seqs, channels = signal_ref.shape[:2]
    rows = seqs * signal_ref.shape[2]
    signal = jnp.concatenate(
        [signal_ref[:, c].reshape(rows, BLOCK) for c in range(channels)], axis=1
    )
    part = dot3(first, split_value(signal))
    turned = []
    for c in range(channels):
        real = part[:rows, c * BLOCK : (c + 1) * BLOCK]
        imag = part[rows:, c * BLOCK : (c + 1) * BLOCK]
        turned.append(
            jnp.concatenate(
                [real * turn[0] - imag * turn[1], real * turn[1] + imag * turn[0]], axis=1
            )
        )
    return dot3(split_value(jnp.concatenate(turned, axis=0)), second)


def taps_kernel(taps_ref, f_hi, f_lo, t_re, t_im, s_hi, s_lo, out_ref):
    out_ref[...] = forward(
        taps_ref, (f_hi[...], f_lo[...]), (t_re[...], t_im[...]), (s_hi[...], s_lo[...])
    )


def conv_kernel(
    kv_ref, spec_ref, f_hi, f_lo, t_re, t_im, s_hi, s_lo, b_hi, b_lo, i_hi, i_lo, out_ref
):
    seqs, channels, blocks, _ = kv_ref.shape
    rows = seqs * blocks
    turn = (t_re[...], t_im[...])
    spectrum = forward(kv_ref, (f_hi[...], f_lo[...]), turn, (s_hi[...], s_lo[...]))
    real, imag = spectrum[:, :BLOCK], spectrum[:, BLOCK:]
    taps_real, taps_imag = spec_ref[:, :BLOCK], spec_ref[:, BLOCK:]
    product = jnp.concatenate(
        [real * taps_real - imag * taps_imag, real * taps_imag + imag * taps_real], axis=1
    )
    back = dot3(split_value(product), (b_hi[...], b_lo[...]))
    columns = []
    for c in range(channels):
        real = back[c * rows : (c + 1) * rows, :BLOCK]
        imag = back[c * rows : (c + 1) * rows, BLOCK:]
        columns.append(
            jnp.concatenate(
                [real * turn[0] + imag * turn[1], imag * turn[0] - real * turn[1]], axis=0
            )
        )
    result = dot3((i_hi[...], i_lo[...]), split_value(jnp.concatenate(columns, axis=1)))
    for c in range(channels):
        out_ref[:, c] = result[:, c * BLOCK : (c + 1) * BLOCK].reshape(seqs, blocks, BLOCK)


def turn_blocks(value_ref, out_ref):
    for b in range(out_ref.shape[1]):
        out_ref[:, b, :] = value_ref[b * BLOCK : (b + 1) * BLOCK, :].T


def taps_turn_kernel(taps_ref, out_ref):
    turn_blocks(taps_ref, out_ref)


def kv_kernel(part, last_r, last_l, last_x, out_ref):
    key, value, x_key, x_value = summed(part, last_r, last_l, last_x)
    first, second = (key * value).T, (x_key * x_value).T
    steps = out_ref.shape[1] // 2

    def put(step):
        out_ref[:, step, :] = first
        out_ref[:, steps + step, :] = second

    for step in range(steps):
        pl.when(pl.program_id(0) == step)(functools.partial(put, step))


def multiply_kv(parts, out_shape):
    def spec(value):
        return pl.BlockSpec((value.shape[0], BLOCK, BLOCK), lambda i: (0, i, 0))

    return pl.pallas_call(
        kv_kernel,
        grid=(parts[0].shape[1] // BLOCK,),
        in_specs=[spec(value) for value in parts],
        out_specs=pl.BlockSpec(out_shape, lambda i: (0, 0, 0)),
        out_shape=pltpu.HBM(out_shape, jnp.float32),
        compiler_params=params(8),
        name="kv_kernel",
    )(*parts)


def query_kernel(*refs):
    parts, out_ref = refs[:-1], refs[-1]
    for i, query in enumerate(summed(*parts)):
        rows = query.shape[0]
        out_ref[i * rows : (i + 1) * rows] = query


def gate_kernel(conv_ref, query_ref, out_ref):
    for b in range(conv_ref.shape[1]):
        rows = slice(b * BLOCK, (b + 1) * BLOCK)
        out_ref[rows] = conv_ref[:, b, :].T * query_ref[rows]


def call(kernel, out_shape, *operands, after=(), scratch=(), tables=(), to_hbm=False):
    def body(*refs):
        count = len(operands) + len(tables)
        kernel(*refs[:count], *refs[count + len(after) :])

    def whole(shape):
        return pl.BlockSpec(shape, lambda i: (0,) * len(shape))

    return pl.pallas_call(
        body,
        grid=(1,),
        in_specs=[pl.BlockSpec(memory_space=pltpu.VMEM)] * len(operands)
        + [whole(table.shape) for table in tables]
        + [pl.BlockSpec(memory_space=pl.ANY)] * len(after),
        out_specs=whole(out_shape) if to_hbm else pl.BlockSpec(memory_space=pltpu.VMEM),
        out_shape=pltpu.HBM(out_shape, jnp.float32)
        if to_hbm
        else jax.ShapeDtypeStruct(out_shape, jnp.float32),
        scratch_shapes=scratch,
        compiler_params=params(24),
        name=kernel.__name__,
    )(*operands, *[in_hbm(jnp.asarray(table)) for table in tables], *after)


def exchange(value):
    return lax.all_to_all(value, "seq", split_axis=0, concat_axis=0, tiled=True)


def on_device(activations, proj_weight, filter_taps):
    tokens, channels = filter_taps.shape
    seqs = lax.axis_size("seq")
    length = tokens * seqs
    blocks = tokens // BLOCK
    owned = channels // seqs
    turned_shape = (channels, blocks, BLOCK)
    moved_shape = (seqs, owned, blocks, BLOCK)
    first, turn, second, back, inverse = tables(length)

    chan = lax.axis_index("chan")
    x_at, z_at = chan // 2, chan % 2
    owners = [(x_at + dx) % X_SIZE for dx in (2, 1, 3, 0)]
    place = jnp.stack(owners + [z_at]).astype(jnp.int32)
    weight = in_hbm(jnp.transpose(proj_weight, (1, 0, 2)))
    activations = in_hbm(activations)

    hold = {}
    kv_halves, q_halves = Halves(tokens, (1, 2)), Halves(tokens, (0,))

    def prepare(ready):
        taps = call(taps_turn_kernel, turned_shape, filter_taps, after=(ready,), to_hbm=True)
        hold["taps"] = exchange(taps.reshape(moved_shape))
        hold["query"] = project_query(q_halves, place, activations, weight, ready)
        return hold["taps"], hold["query"][0]

    kv_parts, kv_part = reduce_kv(kv_halves, place, activations, weight, prepare)
    spectrum = call(
        taps_kernel,
        (owned * length // BLOCK, 2 * BLOCK),
        hold["taps"],
        tables=first + turn + second,
        after=(kv_part,),
        to_hbm=True,
    )
    kv = multiply_kv(kv_parts, turned_shape)
    q_parts = reduce_query(q_halves, hold["query"], spectrum)
    moved = exchange(kv.reshape(moved_shape))
    convolved = call(
        conv_kernel,
        moved_shape,
        moved,
        tables=(spectrum,) + first + turn + second + back + inverse,
        to_hbm=True,
    )
    query = call(query_kernel, (tokens, channels), *q_parts)
    home = exchange(convolved).reshape(turned_shape)
    return call(gate_kernel, (tokens, channels), home, query)


def solution(mesh):
    return jax.shard_map(
        on_device,
        mesh=mesh,
        in_specs=(P("seq", "chan"), P("chan", None, None), P("seq", "chan")),
        out_specs=P("seq", "chan"),
        check_vma=False,
    )
```

```python
import functools

import jax
import jax.numpy as jnp
import ml_dtypes
import numpy as np
from jax import lax
from jax.experimental import pallas as pl
from jax.experimental.pallas import tpu as pltpu
from jax.sharding import PartitionSpec as P

BLOCK = 128
X_SIZE = 4
CHUNK = 512


def params(mebibytes):
    return pltpu.CompilerParams(vmem_limit_bytes=mebibytes * 1024 * 1024)


def in_hbm(value):
    return pltpu.with_memory_space_constraint(value, pltpu.HBM)


def shift_x(value, step):
    return lax.ppermute(value, "chan", [(i, (i + 2 * step) % 8) for i in range(8)])


def swap_z(value):
    return lax.ppermute(value, "chan", [(i, i ^ 1) for i in range(8)])


def parts_of(rows, weight, z_at):
    product = jnp.dot(rows, weight, preferred_element_type=jnp.float32)
    low, high = product[:, :BLOCK], product[:, BLOCK:]
    return jnp.where(z_at == 0, high, low), jnp.where(z_at == 0, low, high)


class Halves:
    def __init__(self, tokens, columns):
        self.columns = columns
        parts = 2 // len(columns)
        self.rows = tokens // 2 // parts
        self.z_start = [h % parts * self.rows for h in range(2)]
        self.x_start = [tokens // 2 + start for start in self.z_start]

    def shape(self, count):
        return (count, self.rows, BLOCK)

    def fill(self, place, act, weight, half, x_outs, z_outs):
        for begin, outs in ((self.x_start[half], x_outs), (self.z_start[half], z_outs)):
            if outs == (None, None):
                continue
            for start in range(0, self.rows, CHUNK):
                rows = act[begin + start : begin + start + CHUNK]
                for out, part in zip(outs, parts_of(rows, weight[0], place[4])):
                    if out is not None:
                        out[0][out[1], start : start + CHUNK] = part


def first_kernel(halves, place, act, weight, outs):
    send_r, send_l, z_other, z_mine = outs
    for half, send in enumerate((send_r, send_l)):
        pl.when(pl.program_id(0) == half)(
            functools.partial(
                halves.fill,
                place,
                act,
                weight,
                half,
                ((send, 0), (send, 1)),
                ((z_other, half), (z_mine, half)),
            )
        )


def second_kernel(halves, place, act, weight, outs):
    next_r, next_l, z_send = outs
    x_outs = (
        ((next_r, 2), (next_r, 3)),
        ((next_r, 0), (next_r, 1)),
        ((next_l, 0), (next_l, 1)),
        ((next_l, 2), (next_l, 3)),
        (None, None),
    )
    for i, outs in enumerate(x_outs):
        pl.when(pl.program_id(0) == i)(
            functools.partial(
                halves.fill, place, act, weight, i % 2, outs, ((z_send, i), None)
            )
        )


def third_kernel(halves, place, act, weight, outs):
    (mine,) = outs
    for i in range(6):
        x_outs = (None, None) if i < 4 else ((mine, i + 3), (mine, i + 5))
        z_other = (mine, 6) if i == 5 else None
        pl.when(pl.program_id(0) == i)(
            functools.partial(
                halves.fill, place, act, weight, i % 2, x_outs, (z_other, (mine, i))
            )
        )


def project(kernel, halves, place, activations, weight, owner, steps, outs, after=()):
    first, last = halves.columns[0], halves.columns[-1]

    def weight_block(i, at):
        return (first + (last - first) * (i % 2), 0, at[owner + i // 2])

    def body(at, act, weight_ref, *refs):
        kernel(halves, at, act, weight_ref, refs[len(after) :])

    specs, results = [], []
    for count, where in outs:
        if where == "vmem":
            specs.append(pl.BlockSpec(memory_space=pltpu.VMEM))
            results.append(jax.ShapeDtypeStruct(halves.shape(count), jnp.float32))
            continue
        results.append(pltpu.HBM(halves.shape(count), jnp.float32))
        if where == "hbm":
            specs.append(pl.BlockSpec(halves.shape(count), lambda i, at: (0, 0, 0)))
        else:
            specs.append(
                pl.BlockSpec(
                    halves.shape(1),
                    lambda i, at, start=where, end=count - 1: (
                        jnp.clip(i - start, 0, end),
                        0,
                        0,
                    ),
                )
            )
    return pl.pallas_call(
        body,
        grid_spec=pltpu.PrefetchScalarGridSpec(
            num_scalar_prefetch=1,
            grid=(steps,),
            in_specs=[
                pl.BlockSpec(activations.shape, lambda i, at: (0, 0)),
                pl.BlockSpec((1, weight.shape[1], 2 * BLOCK), weight_block),
            ]
            + [pl.BlockSpec(memory_space=pl.ANY)] * len(after),
            out_specs=specs,
        ),
        out_shape=results,
        compiler_params=params(24),
        name=kernel.__name__,
    )(place, activations, weight, *after)


def sum_call(kernel, halves, counts, near, far, after=()):
    tile = halves.rows

    def body(*refs):
        rows = pl.ds(pl.multiple_of(pl.program_id(0) * tile, tile), tile)
        ins = [ref.at[:, rows] for ref in refs[: len(near)]]
        ins += refs[len(near) : len(near) + len(far)]
        kernel(*ins, *[ref.at[:, rows] for ref in refs[len(near) + len(far) + len(after) :]])

    return pl.pallas_call(
        body,
        grid=(halves.rows // tile,),
        in_specs=[pl.BlockSpec(memory_space=pltpu.VMEM)] * len(near)
        + [pl.BlockSpec((value.shape[0], tile, BLOCK), lambda i: (0, i, 0)) for value in far]
        + [pl.BlockSpec(memory_space=pl.ANY)] * len(after),
        out_specs=[pl.BlockSpec(memory_space=pltpu.VMEM)] * len(counts),
        out_shape=[jax.ShapeDtypeStruct(halves.shape(count), jnp.float32) for count in counts],
        compiler_params=params(8),
        name=kernel.__name__,
    )(*near, *[in_hbm(value) for value in far], *after)


def first_sum_kernel(got_r, got_l, z_got, keep_r, keep_l, z_mine, out_r, out_l):
    for half, (keep, got, out) in enumerate(((keep_r, got_r, out_r), (keep_l, got_l, out_l))):
        out[0] = keep[0] + got[0]
        out[1] = keep[1] + got[1]
        out[2] = z_mine[half] + z_got[half]


def kv_first_sum_kernel(got_r, got_l, z_got, next_r, next_l, z_mine, out_r, out_l):
    for half, (mine, got, out) in enumerate(((next_r, got_r, out_r), (next_l, got_l, out_l))):
        out[0] = mine[0]
        out[1] = mine[1]
        out[2] = mine[2] + got[0]
        out[3] = mine[3] + got[1]
        out[4] = z_mine[half] + z_got[half]


def piece_call(kernel, halves, counts, pieces, after=()):
    tile = halves.rows

    def body(*refs):
        kernel(*refs[: len(pieces)], *refs[len(pieces) + len(after) :])

    def spec(index):
        return pl.BlockSpec((1, tile, BLOCK), lambda i: (index, i, 0))

    return pl.pallas_call(
        body,
        grid=(halves.rows // tile,),
        in_specs=[spec(index) for _, index in pieces]
        + [pl.BlockSpec(memory_space=pl.ANY)] * len(after),
        out_specs=[pl.BlockSpec((n, tile, BLOCK), lambda i: (0, i, 0)) for n in counts],
        out_shape=[jax.ShapeDtypeStruct(halves.shape(count), jnp.float32) for count in counts],
        compiler_params=params(12),
        name=kernel.__name__,
    )(*[value for value, _ in pieces], *after)


def kv_other_kernel(own_k, own_v, r_k, r_v, l_k, l_v, late, out):
    out[0:1] = own_k[...] + (r_k[...] + l_k[...])
    out[1:2] = own_v[...] + (r_v[...] + l_v[...])
    out[2:3] = late[...]


def kv_last_kernel(m0, m1, m2, m3, g0, g1, g2, g3, next_r, next_l, out_r, out_l):
    out_r[0:1] = m0[...] + g0[...] + next_r[...]
    out_r[1:2] = m1[...] + g1[...]
    out_l[0:1] = m2[...] + g2[...]
    out_l[1:2] = m3[...] + g3[...] + next_l[...]


def kv_beside_kernel(m4, m5, g4, own_k, own_v, r_k, r_v, l_k, l_v, out):
    out[0:1] = m4[...] + g4[...]
    out[1:2] = m5[...]
    out[2:3] = own_k[...] + (r_k[...] + l_k[...])
    out[3:4] = own_v[...] + (r_v[...] + l_v[...])


def release(values, after):
    def body(*refs):
        pass

    count = len(values)
    return pl.pallas_call(
        body,
        in_specs=[pl.BlockSpec(memory_space=pl.ANY)] * (count + 1),
        out_specs=[pl.BlockSpec(memory_space=pl.ANY)] * count,
        out_shape=[pltpu.HBM(value.shape, value.dtype) for value in values],
        input_output_aliases={i: i for i in range(count)},
        name="release",
    )(*values, after)


def query_project_kernel(place, act, weight, *refs):
    send_r, send_l, keep_r, keep_l, z_send, z_next, z_mine, x_other, x_mine, product = refs[-10:]
    product[...] = jnp.dot(act[...], weight[0], preferred_element_type=jnp.float32)

    def put(owner, other, mine):
        start = pl.multiple_of(place[owner] * 2 * BLOCK, 2 * BLOCK)
        columns = product[:, pl.ds(start, 2 * BLOCK)]
        low, high = columns[:, :BLOCK], columns[:, BLOCK:]
        other[0][other[1]] = jnp.where(place[4] == 0, high, low)
        mine[0][mine[1]] = jnp.where(place[4] == 0, low, high)

    def z_step(half):
        for owner in range(4):
            piece = 2 * owner + half
            other = (z_send, piece) if piece < 3 else (z_next, piece - 3)
            put(owner, other, (z_mine, piece))

    def x_step(half):
        far, right, left = (
            ((send_r, 0), (keep_r, 0), (send_l, 2)),
            ((send_l, 0), (send_r, 2), (keep_l, 0)),
        )[half]
        for owner, (ref, piece) in enumerate((far, right, left)):
            put(owner, (ref, piece), (ref, piece + 1))
        put(3, (x_other, half), (x_mine, half))

    for i in range(4):
        pl.when(pl.program_id(0) == i)(
            functools.partial(z_step if i < 2 else x_step, i % 2)
        )


def query_second_sum_kernel(
    dep_r, dep_l, got_r, got_l, z_got, z_next, z_mine, x_other, out_r, out_l, out_x
):
    out_r[0] = z_mine[2] + z_got[2] + dep_r[2]
    out_r[1] = z_mine[3] + z_next[0]
    out_l[0] = z_mine[4] + z_next[1]
    out_l[1] = z_mine[5] + z_next[2] + dep_l[2]
    out_x[0] = x_other[0] + (dep_r[0] + got_l[2])
    out_x[1] = x_other[1] + (got_r[2] + dep_l[0])


def query_beside_kernel(dep_r, dep_l, got_r, got_l, z_next, z_mine, x_mine, out):
    out[0] = z_mine[6] + z_next[3]
    out[1] = z_mine[7] + z_next[4]
    out[2] = x_mine[0] + (dep_r[1] + got_l[3])
    out[3] = x_mine[1] + (got_r[3] + dep_l[1])


def reduce_kv(halves, place, activations, weight, beside):
    make = functools.partial(
        project, halves=halves, place=place, activations=activations, weight=weight
    )
    send_r, send_l, z_send, z_mine = make(
        first_kernel, owner=0, steps=2, outs=[(2, "vmem")] * 4
    )
    got_r, got_l, z_got = shift_x(send_r, 1), shift_x(send_l, -1), swap_z(z_send)
    next_r, next_l, z_send = make(
        second_kernel, owner=1, steps=5, outs=[(5, "vmem")] * 3, after=(z_mine,)
    )
    next_r, next_l = sum_call(
        kv_first_sum_kernel, halves, [5, 5], [got_r, got_l, z_got, next_r, next_l, z_mine], []
    )
    ready = beside(next_r)
    (mine,) = make(
        third_kernel,
        owner=1,
        steps=6,
        outs=[(11, "vmem")],
        after=(next_r,) + ready[1:],
    )
    next_r, next_l, z_five = shift_x(next_r, 1), shift_x(next_l, -1), swap_z(z_send)
    (last_xz,) = piece_call(
        kv_other_kernel,
        halves,
        [3],
        [(mine, 7), (mine, 8), (next_r, 2), (next_r, 0), (next_l, 0), (next_l, 2), (mine, 6)],
        after=(z_five,) + ready,
    )
    last_r, last_l = piece_call(
        kv_last_kernel,
        halves,
        [2, 2],
        [(mine, i) for i in range(4)]
        + [(z_five, i) for i in range(4)]
        + [(next_r, 4), (next_l, 4)],
        after=(last_xz,),
    )
    (part,) = piece_call(
        kv_beside_kernel,
        halves,
        [4],
        [(mine, 4), (mine, 5), (z_five, 4), (mine, 9), (mine, 10)]
        + [(next_r, 3), (next_r, 1), (next_l, 1), (next_l, 3)],
        after=(last_r,),
    )
    last_r, last_l, last_xz = shift_x(last_r, 1), shift_x(last_l, -1), swap_z(last_xz)
    return (part, last_r, last_l, last_xz), part


def project_query(halves, place, activations, weight, after):
    features, columns = weight.shape[1:]
    shapes = [halves.shape(count) for count in (4, 4, 2, 2, 3, 5, 8, 2, 2)]
    return pl.pallas_call(
        query_project_kernel,
        grid_spec=pltpu.PrefetchScalarGridSpec(
            num_scalar_prefetch=1,
            grid=(4,),
            in_specs=[
                pl.BlockSpec((halves.rows, features), lambda i, at: (i, 0)),
                pl.BlockSpec((1, features, columns), lambda i, at: (0, 0, 0)),
                pl.BlockSpec(memory_space=pl.ANY),
            ],
            out_specs=[pl.BlockSpec(shape, lambda i, at: (0, 0, 0)) for shape in shapes],
            scratch_shapes=[pltpu.VMEM((halves.rows, columns), jnp.float32)],
        ),
        out_shape=[pltpu.HBM(shape, jnp.float32) for shape in shapes],
        compiler_params=params(24),
        name="query_project_kernel",
    )(place, activations, weight, after)


def reduce_query(halves, projected, after):
    send_r, send_l, keep_r, keep_l, z_send, z_next, z_mine, x_other, x_mine = projected
    send_r, send_l, z_send, z_next = release((send_r, send_l, z_send, z_next), after)
    got_r, got_l, z_got = shift_x(send_r, 1), shift_x(send_l, -1), swap_z(z_send)
    z_next = swap_z(z_next)
    dep_r, dep_l = sum_call(
        first_sum_kernel,
        halves,
        [3, 3],
        [got_r, got_l, z_got],
        [keep_r, keep_l, z_mine],
    )
    dep_r, dep_l = shift_x(dep_r, 1), shift_x(dep_l, -1)
    last_r, last_l, x_sum = sum_call(
        query_second_sum_kernel,
        halves,
        [2, 2, 2],
        [dep_r, dep_l, got_r, got_l, z_got, z_next],
        [z_mine, x_other],
    )
    (part,) = sum_call(
        query_beside_kernel,
        halves,
        [4],
        [dep_r, dep_l, got_r, got_l, z_next],
        [z_mine, x_mine],
        after=(last_r,),
    )
    last_r, last_l, x_sum = shift_x(last_r, 1), shift_x(last_l, -1), swap_z(x_sum)
    return part, last_r, last_l, x_sum


def summed(part, last_r, last_l, last_x):
    z_total = [part[h] + (last_r[h] + last_l[h]) for h in range(2)]
    if last_x.shape[0] == 3:
        z_total[1] = z_total[1] + last_x[2]
    return z_total + [part[2 + h] + last_x[h] for h in range(2)]


def split_bf16(table):
    high = table.astype(np.float32).astype(ml_dtypes.bfloat16)
    low = (table - high.astype(np.float64)).astype(ml_dtypes.bfloat16)
    return high, low


@functools.lru_cache(None)
def tables(length):
    rows = length // BLOCK
    period = 2 * length
    odd = np.arange(rows) + 0.5
    first = -2 * np.pi * np.outer(odd, np.arange(rows)) / (2 * rows)
    turn = -2 * np.pi * np.outer(odd, np.arange(BLOCK)) / period
    second = -2 * np.pi * (np.outer(np.arange(BLOCK), np.arange(BLOCK)) % BLOCK) / BLOCK
    c, s = np.cos(second), np.sin(second)
    scale = 1.0 / length
    return (
        split_bf16(np.concatenate([np.cos(first), np.sin(first)], axis=0)),
        (np.cos(turn).astype(np.float32), np.sin(turn).astype(np.float32)),
        split_bf16(np.block([[c, s], [-s, c]])),
        split_bf16(np.block([[c, -s], [s, c]])),
        split_bf16(np.concatenate([np.cos(first).T, np.sin(first).T], axis=1) * scale),
    )


def split_value(value):
    high = value.astype(jnp.bfloat16)
    return high, (value - high.astype(jnp.float32)).astype(jnp.bfloat16)


def dot3(left, right):
    dot = functools.partial(jnp.dot, preferred_element_type=jnp.float32)
    return dot(left[0], right[0]) + (dot(left[0], right[1]) + dot(left[1], right[0]))


def forward(signal_ref, first, turn, second):
    seqs, channels = signal_ref.shape[:2]
    rows = seqs * signal_ref.shape[2]
    signal = jnp.concatenate(
        [signal_ref[:, c].reshape(rows, BLOCK) for c in range(channels)], axis=1
    )
    part = dot3(first, split_value(signal))
    turned = []
    for c in range(channels):
        real = part[:rows, c * BLOCK : (c + 1) * BLOCK]
        imag = part[rows:, c * BLOCK : (c + 1) * BLOCK]
        turned.append(
            jnp.concatenate(
                [real * turn[0] - imag * turn[1], real * turn[1] + imag * turn[0]], axis=1
            )
        )
    return dot3(split_value(jnp.concatenate(turned, axis=0)), second)


def taps_kernel(taps_ref, f_hi, f_lo, t_re, t_im, s_hi, s_lo, out_ref):
    out_ref[...] = forward(
        taps_ref, (f_hi[...], f_lo[...]), (t_re[...], t_im[...]), (s_hi[...], s_lo[...])
    )


def conv_kernel(
    kv_ref, spec_ref, f_hi, f_lo, t_re, t_im, s_hi, s_lo, b_hi, b_lo, i_hi, i_lo, out_ref
):
    seqs, channels, blocks, _ = kv_ref.shape
    rows = seqs * blocks
    turn = (t_re[...], t_im[...])
    spectrum = forward(kv_ref, (f_hi[...], f_lo[...]), turn, (s_hi[...], s_lo[...]))
    real, imag = spectrum[:, :BLOCK], spectrum[:, BLOCK:]
    taps_real, taps_imag = spec_ref[:, :BLOCK], spec_ref[:, BLOCK:]
    product = jnp.concatenate(
        [real * taps_real - imag * taps_imag, real * taps_imag + imag * taps_real], axis=1
    )
    back = dot3(split_value(product), (b_hi[...], b_lo[...]))
    columns = []
    for c in range(channels):
        real = back[c * rows : (c + 1) * rows, :BLOCK]
        imag = back[c * rows : (c + 1) * rows, BLOCK:]
        columns.append(
            jnp.concatenate(
                [real * turn[0] + imag * turn[1], imag * turn[0] - real * turn[1]], axis=0
            )
        )
    result = dot3((i_hi[...], i_lo[...]), split_value(jnp.concatenate(columns, axis=1)))
    for c in range(channels):
        out_ref[:, c] = result[:, c * BLOCK : (c + 1) * BLOCK].reshape(seqs, blocks, BLOCK)


def turn_blocks(value_ref, out_ref):
    for b in range(out_ref.shape[1]):
        out_ref[:, b, :] = value_ref[b * BLOCK : (b + 1) * BLOCK, :].T


def taps_turn_kernel(taps_ref, out_ref):
    turn_blocks(taps_ref, out_ref)


def kv_kernel(*refs):
    parts, out_ref, kv_ref = refs[:-2], refs[-2], refs[-1]
    z_key, z_value, x_key, x_value = summed(*parts)
    rows = z_key.shape[0]
    kv_ref[:rows] = z_key * z_value
    kv_ref[rows:] = x_key * x_value
    turn_blocks(kv_ref, out_ref)


def query_kernel(*refs):
    parts, out_ref = refs[:-1], refs[-1]
    for i, query in enumerate(summed(*parts)):
        rows = query.shape[0]
        out_ref[i * rows : (i + 1) * rows] = query


def gate_kernel(conv_ref, query_ref, out_ref):
    for b in range(conv_ref.shape[1]):
        rows = slice(b * BLOCK, (b + 1) * BLOCK)
        out_ref[rows] = conv_ref[:, b, :].T * query_ref[rows]


def call(kernel, out_shape, *operands, after=(), scratch=(), tables=(), to_hbm=False):
    def body(*refs):
        count = len(operands) + len(tables)
        kernel(*refs[:count], *refs[count + len(after) :])

    def whole(shape):
        return pl.BlockSpec(shape, lambda i: (0,) * len(shape))

    return pl.pallas_call(
        body,
        grid=(1,),
        in_specs=[pl.BlockSpec(memory_space=pltpu.VMEM)] * len(operands)
        + [whole(table.shape) for table in tables]
        + [pl.BlockSpec(memory_space=pl.ANY)] * len(after),
        out_specs=whole(out_shape) if to_hbm else pl.BlockSpec(memory_space=pltpu.VMEM),
        out_shape=pltpu.HBM(out_shape, jnp.float32)
        if to_hbm
        else jax.ShapeDtypeStruct(out_shape, jnp.float32),
        scratch_shapes=scratch,
        compiler_params=params(24),
        name=kernel.__name__,
    )(*operands, *[in_hbm(jnp.asarray(table)) for table in tables], *after)


def exchange(value):
    return lax.all_to_all(value, "seq", split_axis=0, concat_axis=0, tiled=True)


def on_device(activations, proj_weight, filter_taps):
    tokens, channels = filter_taps.shape
    seqs = lax.axis_size("seq")
    length = tokens * seqs
    blocks = tokens // BLOCK
    owned = channels // seqs
    turned_shape = (channels, blocks, BLOCK)
    moved_shape = (seqs, owned, blocks, BLOCK)
    first, turn, second, back, inverse = tables(length)

    chan = lax.axis_index("chan")
    x_at, z_at = chan // 2, chan % 2
    owners = [(x_at + dx) % X_SIZE for dx in (2, 1, 3, 0)]
    place = jnp.stack(owners + [z_at]).astype(jnp.int32)
    weight = in_hbm(jnp.transpose(proj_weight, (1, 0, 2)))
    activations = in_hbm(activations)

    hold = {}
    kv_halves, q_halves = Halves(tokens, (1, 2)), Halves(tokens, (0,))

    def prepare(ready):
        taps = call(taps_turn_kernel, turned_shape, filter_taps, after=(ready,), to_hbm=True)
        hold["taps"] = exchange(taps.reshape(moved_shape))
        hold["query"] = project_query(q_halves, place, activations, weight, ready)
        return hold["taps"], hold["query"][0]

    kv_parts, kv_part = reduce_kv(kv_halves, place, activations, weight, prepare)
    spectrum = call(
        taps_kernel,
        (owned * length // BLOCK, 2 * BLOCK),
        hold["taps"],
        tables=first + turn + second,
        after=(kv_part,),
        to_hbm=True,
    )
    kv = call(
        kv_kernel,
        turned_shape,
        *kv_parts,
        after=(spectrum,),
        scratch=[pltpu.VMEM((tokens, channels), jnp.float32)],
        to_hbm=True,
    )
    q_parts = reduce_query(q_halves, hold["query"], spectrum)
    moved = exchange(kv.reshape(moved_shape))
    convolved = call(
        conv_kernel,
        moved_shape,
        moved,
        tables=(spectrum,) + first + turn + second + back + inverse,
        to_hbm=True,
    )
    query = call(query_kernel, (tokens, channels), *q_parts)
    home = exchange(convolved).reshape(turned_shape)
    return call(gate_kernel, (tokens, channels), home, query)


def solution(mesh):
    return jax.shard_map(
        on_device,
        mesh=mesh,
        in_specs=(P("seq", "chan"), P("chan", None, None), P("seq", "chan")),
        out_specs=P("seq", "chan"),
        check_vma=False,
    )
```

```python
import functools

import jax
import jax.numpy as jnp
import ml_dtypes
import numpy as np
from jax import lax
from jax.experimental import pallas as pl
from jax.experimental.pallas import tpu as pltpu
from jax.sharding import PartitionSpec as P

BLOCK = 128
X_SIZE = 4
CHUNK = 512


def params(mebibytes):
    return pltpu.CompilerParams(vmem_limit_bytes=mebibytes * 1024 * 1024)


def in_hbm(value):
    return pltpu.with_memory_space_constraint(value, pltpu.HBM)


def shift_x(value, step):
    return lax.ppermute(value, "chan", [(i, (i + 2 * step) % 8) for i in range(8)])


def swap_z(value):
    return lax.ppermute(value, "chan", [(i, i ^ 1) for i in range(8)])


def parts_of(rows, weight, z_at):
    product = jnp.dot(rows, weight, preferred_element_type=jnp.float32)
    low, high = product[:, :BLOCK], product[:, BLOCK:]
    return jnp.where(z_at == 0, high, low), jnp.where(z_at == 0, low, high)


class Halves:
    def __init__(self, tokens, columns):
        self.columns = columns
        parts = 2 // len(columns)
        self.rows = tokens // 2 // parts
        self.z_start = [h % parts * self.rows for h in range(2)]
        self.x_start = [tokens // 2 + start for start in self.z_start]

    def shape(self, count):
        return (count, self.rows, BLOCK)

    def fill(self, place, act, weight, half, x_outs, z_outs):
        for begin, outs in ((self.x_start[half], x_outs), (self.z_start[half], z_outs)):
            if outs == (None, None):
                continue
            for start in range(0, self.rows, CHUNK):
                rows = act[begin + start : begin + start + CHUNK]
                for out, part in zip(outs, parts_of(rows, weight[0], place[4])):
                    if out is not None:
                        out[0][out[1], start : start + CHUNK] = part


def first_kernel(halves, place, act, weight, outs):
    send_r, send_l, z_other, z_mine = outs
    for half, send in enumerate((send_r, send_l)):
        pl.when(pl.program_id(0) == half)(
            functools.partial(
                halves.fill,
                place,
                act,
                weight,
                half,
                ((send, 0), (send, 1)),
                ((z_other, half), (z_mine, half)),
            )
        )


def second_kernel(halves, place, act, weight, outs):
    next_r, next_l, z_send = outs
    x_outs = (
        ((next_r, 2), (next_r, 3)),
        ((next_r, 0), (next_r, 1)),
        ((next_l, 0), (next_l, 1)),
        ((next_l, 2), (next_l, 3)),
        (None, None),
    )
    for i, outs in enumerate(x_outs):
        pl.when(pl.program_id(0) == i)(
            functools.partial(
                halves.fill, place, act, weight, i % 2, outs, ((z_send, i), None)
            )
        )


def third_kernel(halves, place, act, weight, outs):
    (mine,) = outs
    for i in range(6):
        x_outs = (None, None) if i < 4 else ((mine, i + 3), (mine, i + 5))
        z_other = (mine, 6) if i == 5 else None
        pl.when(pl.program_id(0) == i)(
            functools.partial(
                halves.fill, place, act, weight, i % 2, x_outs, (z_other, (mine, i))
            )
        )


def project(kernel, halves, place, activations, weight, owner, steps, outs, after=()):
    first, last = halves.columns[0], halves.columns[-1]

    def weight_block(i, at):
        return (first + (last - first) * (i % 2), 0, at[owner + i // 2])

    def body(at, act, weight_ref, *refs):
        kernel(halves, at, act, weight_ref, refs[len(after) :])

    specs, results = [], []
    for count, where in outs:
        if where == "vmem":
            specs.append(pl.BlockSpec(memory_space=pltpu.VMEM))
            results.append(jax.ShapeDtypeStruct(halves.shape(count), jnp.float32))
            continue
        results.append(pltpu.HBM(halves.shape(count), jnp.float32))
        if where == "hbm":
            specs.append(pl.BlockSpec(halves.shape(count), lambda i, at: (0, 0, 0)))
        else:
            specs.append(
                pl.BlockSpec(
                    halves.shape(1),
                    lambda i, at, start=where, end=count - 1: (
                        jnp.clip(i - start, 0, end),
                        0,
                        0,
                    ),
                )
            )
    return pl.pallas_call(
        body,
        grid_spec=pltpu.PrefetchScalarGridSpec(
            num_scalar_prefetch=1,
            grid=(steps,),
            in_specs=[
                pl.BlockSpec(activations.shape, lambda i, at: (0, 0)),
                pl.BlockSpec((1, weight.shape[1], 2 * BLOCK), weight_block),
            ]
            + [pl.BlockSpec(memory_space=pl.ANY)] * len(after),
            out_specs=specs,
        ),
        out_shape=results,
        compiler_params=params(24),
        name=kernel.__name__,
    )(place, activations, weight, *after)


def sum_call(kernel, halves, counts, near, far, after=()):
    tile = halves.rows

    def body(*refs):
        rows = pl.ds(pl.multiple_of(pl.program_id(0) * tile, tile), tile)
        ins = [ref.at[:, rows] for ref in refs[: len(near)]]
        ins += refs[len(near) : len(near) + len(far)]
        kernel(*ins, *[ref.at[:, rows] for ref in refs[len(near) + len(far) + len(after) :]])

    return pl.pallas_call(
        body,
        grid=(halves.rows // tile,),
        in_specs=[pl.BlockSpec(memory_space=pltpu.VMEM)] * len(near)
        + [pl.BlockSpec((value.shape[0], tile, BLOCK), lambda i: (0, i, 0)) for value in far]
        + [pl.BlockSpec(memory_space=pl.ANY)] * len(after),
        out_specs=[pl.BlockSpec(memory_space=pltpu.VMEM)] * len(counts),
        out_shape=[jax.ShapeDtypeStruct(halves.shape(count), jnp.float32) for count in counts],
        compiler_params=params(8),
        name=kernel.__name__,
    )(*near, *[in_hbm(value) for value in far], *after)


def first_sum_kernel(got_r, got_l, z_got, keep_r, keep_l, z_mine, out_r, out_l):
    for half, (keep, got, out) in enumerate(((keep_r, got_r, out_r), (keep_l, got_l, out_l))):
        out[0] = keep[0] + got[0]
        out[1] = keep[1] + got[1]
        out[2] = z_mine[half] + z_got[half]


def kv_first_sum_kernel(got_r, got_l, z_got, next_r, next_l, z_mine, out_r, out_l):
    for half, (mine, got, out) in enumerate(((next_r, got_r, out_r), (next_l, got_l, out_l))):
        out[0] = mine[0]
        out[1] = mine[1]
        out[2] = mine[2] + got[0]
        out[3] = mine[3] + got[1]
        out[4] = z_mine[half] + z_got[half]


def piece_call(kernel, halves, counts, pieces, after=()):
    tile = halves.rows

    def body(*refs):
        kernel(*refs[: len(pieces)], *refs[len(pieces) + len(after) :])

    def spec(index):
        return pl.BlockSpec((1, tile, BLOCK), lambda i: (index, i, 0))

    return pl.pallas_call(
        body,
        grid=(halves.rows // tile,),
        in_specs=[spec(index) for _, index in pieces]
        + [pl.BlockSpec(memory_space=pl.ANY)] * len(after),
        out_specs=[pl.BlockSpec((n, tile, BLOCK), lambda i: (0, i, 0)) for n in counts],
        out_shape=[jax.ShapeDtypeStruct(halves.shape(count), jnp.float32) for count in counts],
        compiler_params=params(12),
        name=kernel.__name__,
    )(*[value for value, _ in pieces], *after)


def kv_other_kernel(own_k, own_v, r_k, r_v, l_k, l_v, late, out):
    out[0:1] = own_k[...] + (r_k[...] + l_k[...])
    out[1:2] = own_v[...] + (r_v[...] + l_v[...])
    out[2:3] = late[...]


def kv_last_kernel(m0, m1, m2, m3, g0, g1, g2, g3, next_r, next_l, out_r, out_l):
    out_r[0:1] = m0[...] + g0[...] + next_r[...]
    out_r[1:2] = m1[...] + g1[...]
    out_l[0:1] = m2[...] + g2[...]
    out_l[1:2] = m3[...] + g3[...] + next_l[...]


def kv_beside_kernel(m4, m5, g4, own_k, own_v, r_k, r_v, l_k, l_v, out):
    out[0:1] = m4[...] + g4[...]
    out[1:2] = m5[...]
    out[2:3] = own_k[...] + (r_k[...] + l_k[...])
    out[3:4] = own_v[...] + (r_v[...] + l_v[...])


def release(values, after):
    def body(*refs):
        pass

    count = len(values)
    return pl.pallas_call(
        body,
        in_specs=[pl.BlockSpec(memory_space=pl.ANY)] * (count + 1),
        out_specs=[pl.BlockSpec(memory_space=pl.ANY)] * count,
        out_shape=[pltpu.HBM(value.shape, value.dtype) for value in values],
        input_output_aliases={i: i for i in range(count)},
        name="release",
    )(*values, after)


def query_project_kernel(place, act, weight, *refs):
    send_r, send_l, keep_r, keep_l, z_send, z_next, z_mine, x_other, x_mine, product = refs[-10:]
    product[...] = jnp.dot(act[...], weight[0], preferred_element_type=jnp.float32)

    def put(owner, other, mine):
        start = pl.multiple_of(place[owner] * 2 * BLOCK, 2 * BLOCK)
        columns = product[:, pl.ds(start, 2 * BLOCK)]
        low, high = columns[:, :BLOCK], columns[:, BLOCK:]
        other[0][other[1]] = jnp.where(place[4] == 0, high, low)
        mine[0][mine[1]] = jnp.where(place[4] == 0, low, high)

    def z_step(half):
        for owner in range(4):
            piece = 2 * owner + half
            other = (z_send, piece) if piece < 3 else (z_next, piece - 3)
            put(owner, other, (z_mine, piece))

    def x_step(half):
        far, right, left = (
            ((send_r, 0), (keep_r, 0), (send_l, 2)),
            ((send_l, 0), (send_r, 2), (keep_l, 0)),
        )[half]
        for owner, (ref, piece) in enumerate((far, right, left)):
            put(owner, (ref, piece), (ref, piece + 1))
        put(3, (x_other, half), (x_mine, half))

    for i in range(4):
        pl.when(pl.program_id(0) == i)(
            functools.partial(z_step if i < 2 else x_step, i % 2)
        )


def query_second_sum_kernel(
    dep_r, dep_l, got_r, got_l, z_got, z_next, z_mine, x_other, out_r, out_l, out_x
):
    out_r[0] = z_mine[2] + z_got[2] + dep_r[2]
    out_r[1] = z_mine[3] + z_next[0]
    out_l[0] = z_mine[4] + z_next[1]
    out_l[1] = z_mine[5] + z_next[2] + dep_l[2]
    out_x[0] = x_other[0] + (dep_r[0] + got_l[2])
    out_x[1] = x_other[1] + (got_r[2] + dep_l[0])


def query_beside_kernel(dep_r, dep_l, got_r, got_l, z_next, z_mine, x_mine, out):
    out[0] = z_mine[6] + z_next[3]
    out[1] = z_mine[7] + z_next[4]
    out[2] = x_mine[0] + (dep_r[1] + got_l[3])
    out[3] = x_mine[1] + (got_r[3] + dep_l[1])


def reduce_kv(halves, place, activations, weight, beside):
    make = functools.partial(
        project, halves=halves, place=place, activations=activations, weight=weight
    )
    send_r, send_l, z_send, z_mine = make(
        first_kernel, owner=0, steps=2, outs=[(2, "vmem")] * 4
    )
    got_r, got_l, z_got = shift_x(send_r, 1), shift_x(send_l, -1), swap_z(z_send)
    next_r, next_l, z_send = make(
        second_kernel, owner=1, steps=5, outs=[(5, "vmem")] * 3, after=(z_mine,)
    )
    next_r, next_l = sum_call(
        kv_first_sum_kernel, halves, [5, 5], [got_r, got_l, z_got, next_r, next_l, z_mine], []
    )
    ready = beside(next_r)
    (mine,) = make(
        third_kernel,
        owner=1,
        steps=6,
        outs=[(11, "vmem")],
        after=(next_r,) + ready[1:],
    )
    next_r, next_l, z_five = shift_x(next_r, 1), shift_x(next_l, -1), swap_z(z_send)
    (last_xz,) = piece_call(
        kv_other_kernel,
        halves,
        [3],
        [(mine, 7), (mine, 8), (next_r, 2), (next_r, 0), (next_l, 0), (next_l, 2), (mine, 6)],
        after=(z_five,) + ready,
    )
    last_r, last_l = piece_call(
        kv_last_kernel,
        halves,
        [2, 2],
        [(mine, i) for i in range(4)]
        + [(z_five, i) for i in range(4)]
        + [(next_r, 4), (next_l, 4)],
        after=(last_xz,),
    )
    (part,) = piece_call(
        kv_beside_kernel,
        halves,
        [4],
        [(mine, 4), (mine, 5), (z_five, 4), (mine, 9), (mine, 10)]
        + [(next_r, 3), (next_r, 1), (next_l, 1), (next_l, 3)],
        after=(last_r,),
    )
    last_r, last_l, last_xz = shift_x(last_r, 1), shift_x(last_l, -1), swap_z(last_xz)
    return (part, last_r, last_l, last_xz), part


def project_query(halves, place, activations, weight, after):
    features, columns = weight.shape[1:]
    shapes = [halves.shape(count) for count in (4, 4, 2, 2, 3, 5, 8, 2, 2)]
    return pl.pallas_call(
        query_project_kernel,
        grid_spec=pltpu.PrefetchScalarGridSpec(
            num_scalar_prefetch=1,
            grid=(4,),
            in_specs=[
                pl.BlockSpec((halves.rows, features), lambda i, at: (i, 0)),
                pl.BlockSpec((1, features, columns), lambda i, at: (0, 0, 0)),
                pl.BlockSpec(memory_space=pl.ANY),
            ],
            out_specs=[pl.BlockSpec(shape, lambda i, at: (0, 0, 0)) for shape in shapes],
            scratch_shapes=[pltpu.VMEM((halves.rows, columns), jnp.float32)],
        ),
        out_shape=[pltpu.HBM(shape, jnp.float32) for shape in shapes],
        compiler_params=params(24),
        name="query_project_kernel",
    )(place, activations, weight, after)


def reduce_query(halves, projected, after):
    send_r, send_l, keep_r, keep_l, z_send, z_next, z_mine, x_other, x_mine = projected
    send_r, send_l, z_send, z_next = release((send_r, send_l, z_send, z_next), after)
    got_r, got_l, z_got = shift_x(send_r, 1), shift_x(send_l, -1), swap_z(z_send)
    z_next = swap_z(z_next)
    dep_r, dep_l = sum_call(
        first_sum_kernel,
        halves,
        [3, 3],
        [got_r, got_l, z_got],
        [keep_r, keep_l, z_mine],
    )
    dep_r, dep_l = shift_x(dep_r, 1), shift_x(dep_l, -1)
    last_r, last_l, x_sum = sum_call(
        query_second_sum_kernel,
        halves,
        [2, 2, 2],
        [dep_r, dep_l, got_r, got_l, z_got, z_next],
        [z_mine, x_other],
    )
    (part,) = sum_call(
        query_beside_kernel,
        halves,
        [4],
        [dep_r, dep_l, got_r, got_l, z_next],
        [z_mine, x_mine],
        after=(last_r,),
    )
    last_r, last_l, x_sum = shift_x(last_r, 1), shift_x(last_l, -1), swap_z(x_sum)
    return part, last_r, last_l, x_sum


def summed(part, last_r, last_l, last_x):
    z_total = [part[h] + (last_r[h] + last_l[h]) for h in range(2)]
    if last_x.shape[0] == 3:
        z_total[1] = z_total[1] + last_x[2]
    return z_total + [part[2 + h] + last_x[h] for h in range(2)]


def split_bf16(table):
    high = table.astype(np.float32).astype(ml_dtypes.bfloat16)
    low = (table - high.astype(np.float64)).astype(ml_dtypes.bfloat16)
    return high, low


@functools.lru_cache(None)
def tables(length):
    rows = length // BLOCK
    period = 2 * length
    odd = np.arange(rows) + 0.5
    first = -2 * np.pi * np.outer(odd, np.arange(rows)) / (2 * rows)
    turn = -2 * np.pi * np.outer(odd, np.arange(BLOCK)) / period
    second = -2 * np.pi * (np.outer(np.arange(BLOCK), np.arange(BLOCK)) % BLOCK) / BLOCK
    c, s = np.cos(second), np.sin(second)
    scale = 1.0 / length
    return (
        split_bf16(np.concatenate([np.cos(first), np.sin(first)], axis=0)),
        (np.cos(turn).astype(np.float32), np.sin(turn).astype(np.float32)),
        split_bf16(np.block([[c, s], [-s, c]])),
        split_bf16(np.block([[c, -s], [s, c]])),
        split_bf16(np.concatenate([np.cos(first).T, np.sin(first).T], axis=1) * scale),
    )


def split_value(value):
    high = value.astype(jnp.bfloat16)
    return high, (value - high.astype(jnp.float32)).astype(jnp.bfloat16)


def dot3(left, right):
    dot = functools.partial(jnp.dot, preferred_element_type=jnp.float32)
    return dot(left[0], right[0]) + (dot(left[0], right[1]) + dot(left[1], right[0]))


def forward(signal_ref, first, turn, second):
    seqs, channels = signal_ref.shape[:2]
    rows = seqs * signal_ref.shape[2]
    signal = jnp.concatenate(
        [signal_ref[:, c].reshape(rows, BLOCK) for c in range(channels)], axis=1
    )
    part = dot3(first, split_value(signal))
    turned = []
    for c in range(channels):
        real = part[:rows, c * BLOCK : (c + 1) * BLOCK]
        imag = part[rows:, c * BLOCK : (c + 1) * BLOCK]
        turned.append(
            jnp.concatenate(
                [real * turn[0] - imag * turn[1], real * turn[1] + imag * turn[0]], axis=1
            )
        )
    return dot3(split_value(jnp.concatenate(turned, axis=0)), second)


def taps_kernel(taps_ref, f_hi, f_lo, t_re, t_im, s_hi, s_lo, out_ref):
    out_ref[...] = forward(
        taps_ref, (f_hi[...], f_lo[...]), (t_re[...], t_im[...]), (s_hi[...], s_lo[...])
    )


def conv_kernel(
    kv_ref, spec_ref, f_hi, f_lo, t_re, t_im, s_hi, s_lo, b_hi, b_lo, i_hi, i_lo, out_ref
):
    seqs, channels, blocks, _ = kv_ref.shape
    rows = seqs * blocks
    turn = (t_re[...], t_im[...])
    spectrum = forward(kv_ref, (f_hi[...], f_lo[...]), turn, (s_hi[...], s_lo[...]))
    real, imag = spectrum[:, :BLOCK], spectrum[:, BLOCK:]
    taps_real, taps_imag = spec_ref[:, :BLOCK], spec_ref[:, BLOCK:]
    product = jnp.concatenate(
        [real * taps_real - imag * taps_imag, real * taps_imag + imag * taps_real], axis=1
    )
    back = dot3(split_value(product), (b_hi[...], b_lo[...]))
    columns = []
    for c in range(channels):
        real = back[c * rows : (c + 1) * rows, :BLOCK]
        imag = back[c * rows : (c + 1) * rows, BLOCK:]
        columns.append(
            jnp.concatenate(
                [real * turn[0] + imag * turn[1], imag * turn[0] - real * turn[1]], axis=0
            )
        )
    result = dot3((i_hi[...], i_lo[...]), split_value(jnp.concatenate(columns, axis=1)))
    for c in range(channels):
        out_ref[:, c] = result[:, c * BLOCK : (c + 1) * BLOCK].reshape(seqs, blocks, BLOCK)


def turn_blocks(value_ref, out_ref):
    for b in range(out_ref.shape[1]):
        out_ref[:, b, :] = value_ref[b * BLOCK : (b + 1) * BLOCK, :].T


def taps_turn_kernel(taps_ref, out_ref):
    turn_blocks(taps_ref, out_ref)


def kv_kernel(*refs):
    parts, out_ref, kv_ref = refs[:-2], refs[-2], refs[-1]
    z_key, z_value, x_key, x_value = summed(*parts)
    rows = z_key.shape[0]
    kv_ref[:rows] = z_key * z_value
    kv_ref[rows:] = x_key * x_value
    turn_blocks(kv_ref, out_ref)


def query_kernel(*refs):
    parts, out_ref = refs[:-1], refs[-1]
    for i, query in enumerate(summed(*parts)):
        rows = query.shape[0]
        out_ref[i * rows : (i + 1) * rows] = query


def gate_kernel(conv_ref, query_ref, out_ref):
    for b in range(conv_ref.shape[1]):
        rows = slice(b * BLOCK, (b + 1) * BLOCK)
        out_ref[rows] = conv_ref[:, b, :].T * query_ref[rows]


def call(kernel, out_shape, *operands, after=(), scratch=(), tables=(), to_hbm=False):
    def body(*refs):
        count = len(operands) + len(tables)
        kernel(*refs[:count], *refs[count + len(after) :])

    def whole(shape):
        return pl.BlockSpec(shape, lambda i: (0,) * len(shape))

    return pl.pallas_call(
        body,
        grid=(1,),
        in_specs=[pl.BlockSpec(memory_space=pltpu.VMEM)] * len(operands)
        + [whole(table.shape) for table in tables]
        + [pl.BlockSpec(memory_space=pl.ANY)] * len(after),
        out_specs=whole(out_shape) if to_hbm else pl.BlockSpec(memory_space=pltpu.VMEM),
        out_shape=pltpu.HBM(out_shape, jnp.float32)
        if to_hbm
        else jax.ShapeDtypeStruct(out_shape, jnp.float32),
        scratch_shapes=scratch,
        compiler_params=params(24),
        name=kernel.__name__,
    )(*operands, *[in_hbm(jnp.asarray(table)) for table in tables], *after)


def exchange(value):
    return lax.all_to_all(value, "seq", split_axis=0, concat_axis=0, tiled=True)


def on_device(activations, proj_weight, filter_taps):
    tokens, channels = filter_taps.shape
    seqs = lax.axis_size("seq")
    length = tokens * seqs
    blocks = tokens // BLOCK
    owned = channels // seqs
    turned_shape = (channels, blocks, BLOCK)
    moved_shape = (seqs, owned, blocks, BLOCK)
    first, turn, second, back, inverse = tables(length)

    chan = lax.axis_index("chan")
    x_at, z_at = chan // 2, chan % 2
    owners = [(x_at + dx) % X_SIZE for dx in (2, 1, 3, 0)]
    place = jnp.stack(owners + [z_at]).astype(jnp.int32)
    weight = in_hbm(jnp.transpose(proj_weight, (1, 0, 2)))
    activations = in_hbm(activations)

    hold = {}
    kv_halves, q_halves = Halves(tokens, (1, 2)), Halves(tokens, (0,))

    def prepare(ready):
        taps = call(taps_turn_kernel, turned_shape, filter_taps, after=(ready,), to_hbm=True)
        hold["taps"] = exchange(taps.reshape(moved_shape))
        hold["query"] = project_query(q_halves, place, activations, weight, ready)
        return hold["taps"], hold["query"][0]

    kv_parts, kv_part = reduce_kv(kv_halves, place, activations, weight, prepare)
    kv = call(
        kv_kernel,
        turned_shape,
        *kv_parts,
        scratch=[pltpu.VMEM((tokens, channels), jnp.float32)],
        to_hbm=True,
    )
    spectrum = call(
        taps_kernel,
        (owned * length // BLOCK, 2 * BLOCK),
        hold["taps"],
        tables=first + turn + second,
        after=(kv,),
        to_hbm=True,
    )
    q_parts = reduce_query(q_halves, hold["query"], kv_part)
    moved = exchange(kv.reshape(moved_shape))
    convolved = call(
        conv_kernel,
        moved_shape,
        moved,
        tables=(spectrum,) + first + turn + second + back + inverse,
        to_hbm=True,
    )
    query = call(query_kernel, (tokens, channels), *q_parts)
    home = exchange(convolved).reshape(turned_shape)
    return call(gate_kernel, (tokens, channels), home, query)


def solution(mesh):
    return jax.shard_map(
        on_device,
        mesh=mesh,
        in_specs=(P("seq", "chan"), P("chan", None, None), P("seq", "chan")),
        out_specs=P("seq", "chan"),
        check_vma=False,
    )
```

```python
import functools

import jax
import jax.numpy as jnp
import ml_dtypes
import numpy as np
from jax import lax
from jax.experimental import pallas as pl
from jax.experimental.pallas import tpu as pltpu
from jax.sharding import PartitionSpec as P

BLOCK = 128
X_SIZE = 4
CHUNK = 512


def params(mebibytes):
    return pltpu.CompilerParams(vmem_limit_bytes=mebibytes * 1024 * 1024)


def in_hbm(value):
    return pltpu.with_memory_space_constraint(value, pltpu.HBM)


def shift_x(value, step):
    return lax.ppermute(value, "chan", [(i, (i + 2 * step) % 8) for i in range(8)])


def swap_z(value):
    return lax.ppermute(value, "chan", [(i, i ^ 1) for i in range(8)])


def parts_of(rows, weight, z_at):
    product = jnp.dot(rows, weight, preferred_element_type=jnp.float32)
    low, high = product[:, :BLOCK], product[:, BLOCK:]
    return jnp.where(z_at == 0, high, low), jnp.where(z_at == 0, low, high)


class Halves:
    def __init__(self, tokens, columns):
        self.columns = columns
        parts = 2 // len(columns)
        self.rows = tokens // 2 // parts
        self.z_start = [h % parts * self.rows for h in range(2)]
        self.x_start = [tokens // 2 + start for start in self.z_start]

    def shape(self, count):
        return (count, self.rows, BLOCK)

    def fill(self, place, act, weight, half, x_outs, z_outs):
        for begin, outs in ((self.x_start[half], x_outs), (self.z_start[half], z_outs)):
            if outs == (None, None):
                continue
            for start in range(0, self.rows, CHUNK):
                rows = act[begin + start : begin + start + CHUNK]
                for out, part in zip(outs, parts_of(rows, weight[0], place[4])):
                    if out is not None:
                        out[0][out[1], start : start + CHUNK] = part


def first_kernel(halves, place, act, weight, outs):
    send_r, send_l, z_other, z_mine = outs
    for half, send in enumerate((send_r, send_l)):
        pl.when(pl.program_id(0) == half)(
            functools.partial(
                halves.fill,
                place,
                act,
                weight,
                half,
                ((send, 0), (send, 1)),
                ((z_other, half), (z_mine, half)),
            )
        )


def second_kernel(halves, place, act, weight, outs):
    next_r, next_l, z_send = outs
    x_outs = (
        ((next_r, 2), (next_r, 3)),
        ((next_r, 0), (next_r, 1)),
        ((next_l, 0), (next_l, 1)),
        ((next_l, 2), (next_l, 3)),
        (None, None),
    )
    for i, outs in enumerate(x_outs):
        pl.when(pl.program_id(0) == i)(
            functools.partial(
                halves.fill, place, act, weight, i % 2, outs, ((z_send, i), None)
            )
        )


def third_kernel(halves, place, act, weight, outs):
    (mine,) = outs
    for i in range(6):
        x_outs = (None, None) if i < 4 else ((mine, i + 3), (mine, i + 5))
        z_other = (mine, 6) if i == 5 else None
        pl.when(pl.program_id(0) == i)(
            functools.partial(
                halves.fill, place, act, weight, i % 2, x_outs, (z_other, (mine, i))
            )
        )


def project(kernel, halves, place, activations, weight, owner, steps, outs, after=()):
    first, last = halves.columns[0], halves.columns[-1]

    def weight_block(i, at):
        return (first + (last - first) * (i % 2), 0, at[owner + i // 2])

    def body(at, act, weight_ref, *refs):
        kernel(halves, at, act, weight_ref, refs[len(after) :])

    specs, results = [], []
    for count, where in outs:
        if where == "vmem":
            specs.append(pl.BlockSpec(memory_space=pltpu.VMEM))
            results.append(jax.ShapeDtypeStruct(halves.shape(count), jnp.float32))
            continue
        results.append(pltpu.HBM(halves.shape(count), jnp.float32))
        if where == "hbm":
            specs.append(pl.BlockSpec(halves.shape(count), lambda i, at: (0, 0, 0)))
        else:
            specs.append(
                pl.BlockSpec(
                    halves.shape(1),
                    lambda i, at, start=where, end=count - 1: (
                        jnp.clip(i - start, 0, end),
                        0,
                        0,
                    ),
                )
            )
    return pl.pallas_call(
        body,
        grid_spec=pltpu.PrefetchScalarGridSpec(
            num_scalar_prefetch=1,
            grid=(steps,),
            in_specs=[
                pl.BlockSpec(activations.shape, lambda i, at: (0, 0)),
                pl.BlockSpec((1, weight.shape[1], 2 * BLOCK), weight_block),
            ]
            + [pl.BlockSpec(memory_space=pl.ANY)] * len(after),
            out_specs=specs,
        ),
        out_shape=results,
        compiler_params=params(24),
        name=kernel.__name__,
    )(place, activations, weight, *after)


def sum_call(kernel, halves, counts, near, far, after=()):
    tile = halves.rows

    def body(*refs):
        rows = pl.ds(pl.multiple_of(pl.program_id(0) * tile, tile), tile)
        ins = [ref.at[:, rows] for ref in refs[: len(near)]]
        ins += refs[len(near) : len(near) + len(far)]
        kernel(*ins, *[ref.at[:, rows] for ref in refs[len(near) + len(far) + len(after) :]])

    return pl.pallas_call(
        body,
        grid=(halves.rows // tile,),
        in_specs=[pl.BlockSpec(memory_space=pltpu.VMEM)] * len(near)
        + [pl.BlockSpec((value.shape[0], tile, BLOCK), lambda i: (0, i, 0)) for value in far]
        + [pl.BlockSpec(memory_space=pl.ANY)] * len(after),
        out_specs=[pl.BlockSpec(memory_space=pltpu.VMEM)] * len(counts),
        out_shape=[jax.ShapeDtypeStruct(halves.shape(count), jnp.float32) for count in counts],
        compiler_params=params(8),
        name=kernel.__name__,
    )(*near, *[in_hbm(value) for value in far], *after)


def first_sum_kernel(got_r, got_l, z_got, keep_r, keep_l, z_mine, out_r, out_l):
    for half, (keep, got, out) in enumerate(((keep_r, got_r, out_r), (keep_l, got_l, out_l))):
        out[0] = keep[0] + got[0]
        out[1] = keep[1] + got[1]
        out[2] = z_mine[half] + z_got[half]


def kv_first_sum_kernel(got_r, got_l, z_got, next_r, next_l, z_mine, out_r, out_l):
    for half, (mine, got, out) in enumerate(((next_r, got_r, out_r), (next_l, got_l, out_l))):
        out[0] = mine[0]
        out[1] = mine[1]
        out[2] = mine[2] + got[0]
        out[3] = mine[3] + got[1]
        out[4] = z_mine[half] + z_got[half]


def piece_call(kernel, halves, counts, pieces, after=()):
    tile = halves.rows

    def body(*refs):
        kernel(*refs[: len(pieces)], *refs[len(pieces) + len(after) :])

    def spec(index):
        return pl.BlockSpec((1, tile, BLOCK), lambda i: (index, i, 0))

    return pl.pallas_call(
        body,
        grid=(halves.rows // tile,),
        in_specs=[spec(index) for _, index in pieces]
        + [pl.BlockSpec(memory_space=pl.ANY)] * len(after),
        out_specs=[pl.BlockSpec((n, tile, BLOCK), lambda i: (0, i, 0)) for n in counts],
        out_shape=[jax.ShapeDtypeStruct(halves.shape(count), jnp.float32) for count in counts],
        compiler_params=params(12),
        name=kernel.__name__,
    )(*[value for value, _ in pieces], *after)


def kv_other_kernel(own_k, own_v, r_k, r_v, l_k, l_v, late, out):
    out[0:1] = own_k[...] + (r_k[...] + l_k[...])
    out[1:2] = own_v[...] + (r_v[...] + l_v[...])
    out[2:3] = late[...]


def kv_last_kernel(m0, m1, m2, m3, g0, g1, g2, g3, next_r, next_l, out_r, out_l):
    out_r[0:1] = m0[...] + g0[...] + next_r[...]
    out_r[1:2] = m1[...] + g1[...]
    out_l[0:1] = m2[...] + g2[...]
    out_l[1:2] = m3[...] + g3[...] + next_l[...]


def kv_beside_kernel(m4, m5, g4, own_k, own_v, r_k, r_v, l_k, l_v, out):
    out[0:1] = m4[...] + g4[...]
    out[1:2] = m5[...]
    out[2:3] = own_k[...] + (r_k[...] + l_k[...])
    out[3:4] = own_v[...] + (r_v[...] + l_v[...])


def release(values, after):
    def body(*refs):
        pass

    count = len(values)
    return pl.pallas_call(
        body,
        in_specs=[pl.BlockSpec(memory_space=pl.ANY)] * (count + 1),
        out_specs=[pl.BlockSpec(memory_space=pl.ANY)] * count,
        out_shape=[pltpu.HBM(value.shape, value.dtype) for value in values],
        input_output_aliases={i: i for i in range(count)},
        name="release",
    )(*values, after)


def query_project_kernel(place, act, weight, *refs):
    send_r, send_l, keep_r, keep_l, z_send, z_next, z_mine, x_other, x_mine, product = refs[-10:]
    product[...] = jnp.dot(act[...], weight[0], preferred_element_type=jnp.float32)

    def put(owner, other, mine):
        start = pl.multiple_of(place[owner] * 2 * BLOCK, 2 * BLOCK)
        columns = product[:, pl.ds(start, 2 * BLOCK)]
        low, high = columns[:, :BLOCK], columns[:, BLOCK:]
        other[0][other[1]] = jnp.where(place[4] == 0, high, low)
        mine[0][mine[1]] = jnp.where(place[4] == 0, low, high)

    def z_step(half):
        for owner in range(4):
            piece = 2 * owner + half
            other = (z_send, piece) if piece < 2 else (z_next, piece - 2)
            put(owner, other, (z_mine, piece))

    def x_step(half):
        far, right, left = (
            ((send_r, 0), (keep_r, 0), (send_l, 2)),
            ((send_l, 0), (send_r, 2), (keep_l, 0)),
        )[half]
        for owner, (ref, piece) in enumerate((far, right, left)):
            put(owner, (ref, piece), (ref, piece + 1))
        put(3, (x_other, half), (x_mine, half))

    for i in range(4):
        pl.when(pl.program_id(0) == i)(
            functools.partial(z_step if i < 2 else x_step, i % 2)
        )


def query_second_sum_kernel(
    dep_r, dep_l, got_r, got_l, z_got, z_next, z_mine, x_other, out_r, out_l, out_x
):
    out_r[0] = z_mine[2] + z_next[0] + dep_r[2]
    out_r[1] = z_mine[3] + z_next[1]
    out_l[0] = z_mine[4] + z_next[2]
    out_l[1] = z_mine[5] + z_next[3] + dep_l[2]
    out_x[0] = x_other[0] + (dep_r[0] + got_l[2])
    out_x[1] = x_other[1] + (got_r[2] + dep_l[0])


def query_beside_kernel(dep_r, dep_l, got_r, got_l, z_next, z_mine, x_mine, out):
    out[0] = z_mine[6] + z_next[4]
    out[1] = z_mine[7] + z_next[5]
    out[2] = x_mine[0] + (dep_r[1] + got_l[3])
    out[3] = x_mine[1] + (got_r[3] + dep_l[1])


def reduce_kv(halves, place, activations, weight, beside):
    make = functools.partial(
        project, halves=halves, place=place, activations=activations, weight=weight
    )
    send_r, send_l, z_send, z_mine = make(
        first_kernel, owner=0, steps=2, outs=[(2, "vmem")] * 4
    )
    got_r, got_l, z_got = shift_x(send_r, 1), shift_x(send_l, -1), swap_z(z_send)
    next_r, next_l, z_send = make(
        second_kernel, owner=1, steps=5, outs=[(5, "vmem")] * 3, after=(z_mine,)
    )
    next_r, next_l = sum_call(
        kv_first_sum_kernel, halves, [5, 5], [got_r, got_l, z_got, next_r, next_l, z_mine], []
    )
    ready = beside(next_r)
    (mine,) = make(
        third_kernel,
        owner=1,
        steps=6,
        outs=[(11, "vmem")],
        after=(next_r,) + ready[1:],
    )
    next_r, next_l, z_five = shift_x(next_r, 1), shift_x(next_l, -1), swap_z(z_send)
    (last_xz,) = piece_call(
        kv_other_kernel,
        halves,
        [3],
        [(mine, 7), (mine, 8), (next_r, 2), (next_r, 0), (next_l, 0), (next_l, 2), (mine, 6)],
        after=(z_five,) + ready,
    )
    last_r, last_l = piece_call(
        kv_last_kernel,
        halves,
        [2, 2],
        [(mine, i) for i in range(4)]
        + [(z_five, i) for i in range(4)]
        + [(next_r, 4), (next_l, 4)],
        after=(last_xz,),
    )
    (part,) = piece_call(
        kv_beside_kernel,
        halves,
        [4],
        [(mine, 4), (mine, 5), (z_five, 4), (mine, 9), (mine, 10)]
        + [(next_r, 3), (next_r, 1), (next_l, 1), (next_l, 3)],
        after=(last_r,),
    )
    last_r, last_l, last_xz = shift_x(last_r, 1), shift_x(last_l, -1), swap_z(last_xz)
    return (part, last_r, last_l, last_xz), part


def project_query(halves, place, activations, weight, after):
    features, columns = weight.shape[1:]
    shapes = [halves.shape(count) for count in (4, 4, 2, 2, 2, 6, 8, 2, 2)]
    return pl.pallas_call(
        query_project_kernel,
        grid_spec=pltpu.PrefetchScalarGridSpec(
            num_scalar_prefetch=1,
            grid=(4,),
            in_specs=[
                pl.BlockSpec((halves.rows, features), lambda i, at: (i, 0)),
                pl.BlockSpec((1, features, columns), lambda i, at: (0, 0, 0)),
                pl.BlockSpec(memory_space=pl.ANY),
            ],
            out_specs=[pl.BlockSpec(shape, lambda i, at: (0, 0, 0)) for shape in shapes],
            scratch_shapes=[pltpu.VMEM((halves.rows, columns), jnp.float32)],
        ),
        out_shape=[pltpu.HBM(shape, jnp.float32) for shape in shapes],
        compiler_params=params(24),
        name="query_project_kernel",
    )(place, activations, weight, after)


def reduce_query(halves, projected, after):
    send_r, send_l, keep_r, keep_l, z_send, z_next, z_mine, x_other, x_mine = projected
    send_r, send_l, z_send, z_next = release((send_r, send_l, z_send, z_next), after)
    got_r, got_l, z_got = shift_x(send_r, 1), shift_x(send_l, -1), swap_z(z_send)
    z_next = swap_z(z_next)
    dep_r, dep_l = sum_call(
        first_sum_kernel,
        halves,
        [3, 3],
        [got_r, got_l, z_got],
        [keep_r, keep_l, z_mine],
    )
    dep_r, dep_l = shift_x(dep_r, 1), shift_x(dep_l, -1)
    last_r, last_l, x_sum = sum_call(
        query_second_sum_kernel,
        halves,
        [2, 2, 2],
        [dep_r, dep_l, got_r, got_l, z_got, z_next],
        [z_mine, x_other],
    )
    (part,) = sum_call(
        query_beside_kernel,
        halves,
        [4],
        [dep_r, dep_l, got_r, got_l, z_next],
        [z_mine, x_mine],
        after=(last_r,),
    )
    last_r, last_l, x_sum = shift_x(last_r, 1), shift_x(last_l, -1), swap_z(x_sum)
    return part, last_r, last_l, x_sum


def summed(part, last_r, last_l, last_x):
    z_total = [part[h] + (last_r[h] + last_l[h]) for h in range(2)]
    if last_x.shape[0] == 3:
        z_total[1] = z_total[1] + last_x[2]
    return z_total + [part[2 + h] + last_x[h] for h in range(2)]


def split_bf16(table):
    high = table.astype(np.float32).astype(ml_dtypes.bfloat16)
    low = (table - high.astype(np.float64)).astype(ml_dtypes.bfloat16)
    return high, low


@functools.lru_cache(None)
def tables(length):
    rows = length // BLOCK
    period = 2 * length
    odd = np.arange(rows) + 0.5
    first = -2 * np.pi * np.outer(odd, np.arange(rows)) / (2 * rows)
    turn = -2 * np.pi * np.outer(odd, np.arange(BLOCK)) / period
    second = -2 * np.pi * (np.outer(np.arange(BLOCK), np.arange(BLOCK)) % BLOCK) / BLOCK
    c, s = np.cos(second), np.sin(second)
    scale = 1.0 / length
    return (
        split_bf16(np.concatenate([np.cos(first), np.sin(first)], axis=0)),
        (np.cos(turn).astype(np.float32), np.sin(turn).astype(np.float32)),
        split_bf16(np.block([[c, s], [-s, c]])),
        split_bf16(np.block([[c, -s], [s, c]])),
        split_bf16(np.concatenate([np.cos(first).T, np.sin(first).T], axis=1) * scale),
    )


def split_value(value):
    high = value.astype(jnp.bfloat16)
    return high, (value - high.astype(jnp.float32)).astype(jnp.bfloat16)


def dot3(left, right):
    dot = functools.partial(jnp.dot, preferred_element_type=jnp.float32)
    return dot(left[0], right[0]) + (dot(left[0], right[1]) + dot(left[1], right[0]))


def forward(signal_ref, first, turn, second):
    seqs, channels = signal_ref.shape[:2]
    rows = seqs * signal_ref.shape[2]
    signal = jnp.concatenate(
        [signal_ref[:, c].reshape(rows, BLOCK) for c in range(channels)], axis=1
    )
    part = dot3(first, split_value(signal))
    turned = []
    for c in range(channels):
        real = part[:rows, c * BLOCK : (c + 1) * BLOCK]
        imag = part[rows:, c * BLOCK : (c + 1) * BLOCK]
        turned.append(
            jnp.concatenate(
                [real * turn[0] - imag * turn[1], real * turn[1] + imag * turn[0]], axis=1
            )
        )
    return dot3(split_value(jnp.concatenate(turned, axis=0)), second)


def taps_kernel(taps_ref, f_hi, f_lo, t_re, t_im, s_hi, s_lo, out_ref):
    out_ref[...] = forward(
        taps_ref, (f_hi[...], f_lo[...]), (t_re[...], t_im[...]), (s_hi[...], s_lo[...])
    )


def conv_kernel(
    kv_ref, spec_ref, f_hi, f_lo, t_re, t_im, s_hi, s_lo, b_hi, b_lo, i_hi, i_lo, out_ref
):
    seqs, channels, blocks, _ = kv_ref.shape
    rows = seqs * blocks
    turn = (t_re[...], t_im[...])
    spectrum = forward(kv_ref, (f_hi[...], f_lo[...]), turn, (s_hi[...], s_lo[...]))
    real, imag = spectrum[:, :BLOCK], spectrum[:, BLOCK:]
    taps_real, taps_imag = spec_ref[:, :BLOCK], spec_ref[:, BLOCK:]
    product = jnp.concatenate(
        [real * taps_real - imag * taps_imag, real * taps_imag + imag * taps_real], axis=1
    )
    back = dot3(split_value(product), (b_hi[...], b_lo[...]))
    columns = []
    for c in range(channels):
        real = back[c * rows : (c + 1) * rows, :BLOCK]
        imag = back[c * rows : (c + 1) * rows, BLOCK:]
        columns.append(
            jnp.concatenate(
                [real * turn[0] + imag * turn[1], imag * turn[0] - real * turn[1]], axis=0
            )
        )
    result = dot3((i_hi[...], i_lo[...]), split_value(jnp.concatenate(columns, axis=1)))
    for c in range(channels):
        out_ref[:, c] = result[:, c * BLOCK : (c + 1) * BLOCK].reshape(seqs, blocks, BLOCK)


def turn_blocks(value_ref, out_ref):
    for b in range(out_ref.shape[1]):
        out_ref[:, b, :] = value_ref[b * BLOCK : (b + 1) * BLOCK, :].T


def taps_turn_kernel(taps_ref, out_ref):
    turn_blocks(taps_ref, out_ref)


def kv_kernel(*refs):
    parts, out_ref, kv_ref = refs[:-2], refs[-2], refs[-1]
    z_key, z_value, x_key, x_value = summed(*parts)
    rows = z_key.shape[0]
    kv_ref[:rows] = z_key * z_value
    kv_ref[rows:] = x_key * x_value
    turn_blocks(kv_ref, out_ref)


def query_kernel(*refs):
    parts, out_ref = refs[:-1], refs[-1]
    for i, query in enumerate(summed(*parts)):
        rows = query.shape[0]
        out_ref[i * rows : (i + 1) * rows] = query


def gate_kernel(conv_ref, query_ref, out_ref):
    for b in range(conv_ref.shape[1]):
        rows = slice(b * BLOCK, (b + 1) * BLOCK)
        out_ref[rows] = conv_ref[:, b, :].T * query_ref[rows]


def call(kernel, out_shape, *operands, after=(), scratch=(), tables=(), to_hbm=False):
    def body(*refs):
        count = len(operands) + len(tables)
        kernel(*refs[:count], *refs[count + len(after) :])

    def whole(shape):
        return pl.BlockSpec(shape, lambda i: (0,) * len(shape))

    return pl.pallas_call(
        body,
        grid=(1,),
        in_specs=[pl.BlockSpec(memory_space=pltpu.VMEM)] * len(operands)
        + [whole(table.shape) for table in tables]
        + [pl.BlockSpec(memory_space=pl.ANY)] * len(after),
        out_specs=whole(out_shape) if to_hbm else pl.BlockSpec(memory_space=pltpu.VMEM),
        out_shape=pltpu.HBM(out_shape, jnp.float32)
        if to_hbm
        else jax.ShapeDtypeStruct(out_shape, jnp.float32),
        scratch_shapes=scratch,
        compiler_params=params(24),
        name=kernel.__name__,
    )(*operands, *[in_hbm(jnp.asarray(table)) for table in tables], *after)


def exchange(value):
    return lax.all_to_all(value, "seq", split_axis=0, concat_axis=0, tiled=True)


def on_device(activations, proj_weight, filter_taps):
    tokens, channels = filter_taps.shape
    seqs = lax.axis_size("seq")
    length = tokens * seqs
    blocks = tokens // BLOCK
    owned = channels // seqs
    turned_shape = (channels, blocks, BLOCK)
    moved_shape = (seqs, owned, blocks, BLOCK)
    first, turn, second, back, inverse = tables(length)

    chan = lax.axis_index("chan")
    x_at, z_at = chan // 2, chan % 2
    owners = [(x_at + dx) % X_SIZE for dx in (2, 1, 3, 0)]
    place = jnp.stack(owners + [z_at]).astype(jnp.int32)
    weight = in_hbm(jnp.transpose(proj_weight, (1, 0, 2)))
    activations = in_hbm(activations)

    hold = {}
    kv_halves, q_halves = Halves(tokens, (1, 2)), Halves(tokens, (0,))

    def prepare(ready):
        taps = call(taps_turn_kernel, turned_shape, filter_taps, after=(ready,), to_hbm=True)
        hold["taps"] = exchange(taps.reshape(moved_shape))
        hold["query"] = project_query(q_halves, place, activations, weight, ready)
        return hold["taps"], hold["query"][0]

    kv_parts, kv_part = reduce_kv(kv_halves, place, activations, weight, prepare)
    spectrum = call(
        taps_kernel,
        (owned * length // BLOCK, 2 * BLOCK),
        hold["taps"],
        tables=first + turn + second,
        after=(kv_part,),
        to_hbm=True,
    )
    kv = call(
        kv_kernel,
        turned_shape,
        *kv_parts,
        after=(spectrum,),
        scratch=[pltpu.VMEM((tokens, channels), jnp.float32)],
        to_hbm=True,
    )
    q_parts = reduce_query(q_halves, hold["query"], spectrum)
    moved = exchange(kv.reshape(moved_shape))
    convolved = call(
        conv_kernel,
        moved_shape,
        moved,
        tables=(spectrum,) + first + turn + second + back + inverse,
        to_hbm=True,
    )
    query = call(query_kernel, (tokens, channels), *q_parts)
    home = exchange(convolved).reshape(turned_shape)
    return call(gate_kernel, (tokens, channels), home, query)


def solution(mesh):
    return jax.shard_map(
        on_device,
        mesh=mesh,
        in_specs=(P("seq", "chan"), P("chan", None, None), P("seq", "chan")),
        out_specs=P("seq", "chan"),
        check_vma=False,
    )
```

```python
import functools

import jax
import jax.numpy as jnp
import ml_dtypes
import numpy as np
from jax import lax
from jax.experimental import pallas as pl
from jax.experimental.pallas import tpu as pltpu
from jax.sharding import PartitionSpec as P

BLOCK = 128
X_SIZE = 4
CHUNK = 512


def params(mebibytes):
    return pltpu.CompilerParams(vmem_limit_bytes=mebibytes * 1024 * 1024)


def in_hbm(value):
    return pltpu.with_memory_space_constraint(value, pltpu.HBM)


def shift_x(value, step):
    return lax.ppermute(value, "chan", [(i, (i + 2 * step) % 8) for i in range(8)])


def swap_z(value):
    return lax.ppermute(value, "chan", [(i, i ^ 1) for i in range(8)])


def parts_of(rows, weight, z_at):
    product = jnp.dot(rows, weight, preferred_element_type=jnp.float32)
    low, high = product[:, :BLOCK], product[:, BLOCK:]
    return jnp.where(z_at == 0, high, low), jnp.where(z_at == 0, low, high)


class Halves:
    def __init__(self, tokens, columns):
        self.columns = columns
        parts = 2 // len(columns)
        self.rows = tokens // 2 // parts
        self.z_start = [h % parts * self.rows for h in range(2)]
        self.x_start = [tokens // 2 + start for start in self.z_start]

    def shape(self, count):
        return (count, self.rows, BLOCK)

    def fill(self, place, act, weight, half, x_outs, z_outs):
        for begin, outs in ((self.x_start[half], x_outs), (self.z_start[half], z_outs)):
            if outs == (None, None):
                continue
            for start in range(0, self.rows, CHUNK):
                rows = act[begin + start : begin + start + CHUNK]
                for out, part in zip(outs, parts_of(rows, weight[0], place[4])):
                    if out is not None:
                        out[0][out[1], start : start + CHUNK] = part


def first_kernel(halves, place, act, weight, outs):
    send_r, send_l, z_other, z_mine = outs
    for half, send in enumerate((send_r, send_l)):
        pl.when(pl.program_id(0) == half)(
            functools.partial(
                halves.fill,
                place,
                act,
                weight,
                half,
                ((send, 0), (send, 1)),
                ((z_other, half), (z_mine, half)),
            )
        )


def second_kernel(halves, place, act, weight, outs):
    next_r, next_l, z_send = outs
    x_outs = (
        ((next_r, 2), (next_r, 3)),
        ((next_r, 0), (next_r, 1)),
        ((next_l, 0), (next_l, 1)),
        ((next_l, 2), (next_l, 3)),
        (None, None),
    )
    for i, outs in enumerate(x_outs):
        pl.when(pl.program_id(0) == i)(
            functools.partial(
                halves.fill, place, act, weight, i % 2, outs, ((z_send, i), None)
            )
        )


def third_kernel(halves, place, act, weight, outs):
    (mine,) = outs
    for i in range(6):
        x_outs = (None, None) if i < 4 else ((mine, i + 3), (mine, i + 5))
        z_other = (mine, 6) if i == 5 else None
        pl.when(pl.program_id(0) == i)(
            functools.partial(
                halves.fill, place, act, weight, i % 2, x_outs, (z_other, (mine, i))
            )
        )


def project(kernel, halves, place, activations, weight, owner, steps, outs, after=()):
    first, last = halves.columns[0], halves.columns[-1]

    def weight_block(i, at):
        return (first + (last - first) * (i % 2), 0, at[owner + i // 2])

    def body(at, act, weight_ref, *refs):
        kernel(halves, at, act, weight_ref, refs[len(after) :])

    specs, results = [], []
    for count, where in outs:
        if where == "vmem":
            specs.append(pl.BlockSpec(memory_space=pltpu.VMEM))
            results.append(jax.ShapeDtypeStruct(halves.shape(count), jnp.float32))
            continue
        results.append(pltpu.HBM(halves.shape(count), jnp.float32))
        if where == "hbm":
            specs.append(pl.BlockSpec(halves.shape(count), lambda i, at: (0, 0, 0)))
        else:
            specs.append(
                pl.BlockSpec(
                    halves.shape(1),
                    lambda i, at, start=where, end=count - 1: (
                        jnp.clip(i - start, 0, end),
                        0,
                        0,
                    ),
                )
            )
    return pl.pallas_call(
        body,
        grid_spec=pltpu.PrefetchScalarGridSpec(
            num_scalar_prefetch=1,
            grid=(steps,),
            in_specs=[
                pl.BlockSpec(activations.shape, lambda i, at: (0, 0)),
                pl.BlockSpec((1, weight.shape[1], 2 * BLOCK), weight_block),
            ]
            + [pl.BlockSpec(memory_space=pl.ANY)] * len(after),
            out_specs=specs,
        ),
        out_shape=results,
        compiler_params=params(24),
        name=kernel.__name__,
    )(place, activations, weight, *after)


def sum_call(kernel, halves, counts, near, far, after=()):
    tile = halves.rows

    def body(*refs):
        rows = pl.ds(pl.multiple_of(pl.program_id(0) * tile, tile), tile)
        ins = [ref.at[:, rows] for ref in refs[: len(near)]]
        ins += refs[len(near) : len(near) + len(far)]
        kernel(*ins, *[ref.at[:, rows] for ref in refs[len(near) + len(far) + len(after) :]])

    return pl.pallas_call(
        body,
        grid=(halves.rows // tile,),
        in_specs=[pl.BlockSpec(memory_space=pltpu.VMEM)] * len(near)
        + [pl.BlockSpec((value.shape[0], tile, BLOCK), lambda i: (0, i, 0)) for value in far]
        + [pl.BlockSpec(memory_space=pl.ANY)] * len(after),
        out_specs=[pl.BlockSpec(memory_space=pltpu.VMEM)] * len(counts),
        out_shape=[jax.ShapeDtypeStruct(halves.shape(count), jnp.float32) for count in counts],
        compiler_params=params(8),
        name=kernel.__name__,
    )(*near, *[in_hbm(value) for value in far], *after)


def first_sum_kernel(got_r, got_l, z_got, keep_r, keep_l, z_mine, out_r, out_l):
    for half, (keep, got, out) in enumerate(((keep_r, got_r, out_r), (keep_l, got_l, out_l))):
        out[0] = keep[0] + got[0]
        out[1] = keep[1] + got[1]
        out[2] = z_mine[half] + z_got[half]


def kv_first_sum_kernel(got_r, got_l, z_got, next_r, next_l, z_mine, out_r, out_l):
    for half, (mine, got, out) in enumerate(((next_r, got_r, out_r), (next_l, got_l, out_l))):
        out[0] = mine[0]
        out[1] = mine[1]
        out[2] = mine[2] + got[0]
        out[3] = mine[3] + got[1]
        out[4] = z_mine[half] + z_got[half]


def piece_call(kernel, halves, counts, pieces, after=()):
    tile = halves.rows

    def body(*refs):
        kernel(*refs[: len(pieces)], *refs[len(pieces) + len(after) :])

    def spec(index):
        return pl.BlockSpec((1, tile, BLOCK), lambda i: (index, i, 0))

    return pl.pallas_call(
        body,
        grid=(halves.rows // tile,),
        in_specs=[spec(index) for _, index in pieces]
        + [pl.BlockSpec(memory_space=pl.ANY)] * len(after),
        out_specs=[pl.BlockSpec((n, tile, BLOCK), lambda i: (0, i, 0)) for n in counts],
        out_shape=[jax.ShapeDtypeStruct(halves.shape(count), jnp.float32) for count in counts],
        compiler_params=params(12),
        name=kernel.__name__,
    )(*[value for value, _ in pieces], *after)


def kv_other_kernel(own_k, own_v, r_k, r_v, l_k, l_v, late, out):
    out[0:1] = own_k[...] + (r_k[...] + l_k[...])
    out[1:2] = own_v[...] + (r_v[...] + l_v[...])
    out[2:3] = late[...]


def kv_last_kernel(m0, m1, m2, m3, g0, g1, g2, g3, next_r, next_l, out_r, out_l):
    out_r[0:1] = m0[...] + g0[...] + next_r[...]
    out_r[1:2] = m1[...] + g1[...]
    out_l[0:1] = m2[...] + g2[...]
    out_l[1:2] = m3[...] + g3[...] + next_l[...]


def kv_beside_kernel(m4, m5, g4, own_k, own_v, r_k, r_v, l_k, l_v, out):
    out[0:1] = m4[...] + g4[...]
    out[1:2] = m5[...]
    out[2:3] = own_k[...] + (r_k[...] + l_k[...])
    out[3:4] = own_v[...] + (r_v[...] + l_v[...])


def release(values, after):
    def body(*refs):
        pass

    count = len(values)
    return pl.pallas_call(
        body,
        in_specs=[pl.BlockSpec(memory_space=pl.ANY)] * (count + 1),
        out_specs=[pl.BlockSpec(memory_space=pl.ANY)] * count,
        out_shape=[pltpu.HBM(value.shape, value.dtype) for value in values],
        input_output_aliases={i: i for i in range(count)},
        name="release",
    )(*values, after)


def query_project_kernel(place, act, weight, *refs):
    send_r, send_l, keep_r, keep_l, z_send, z_next, z_mine, x_other, x_mine, product = refs[-10:]
    product[...] = jnp.dot(act[...], weight[0], preferred_element_type=jnp.float32)

    def put(owner, other, mine):
        start = pl.multiple_of(place[owner] * 2 * BLOCK, 2 * BLOCK)
        columns = product[:, pl.ds(start, 2 * BLOCK)]
        low, high = columns[:, :BLOCK], columns[:, BLOCK:]
        other[0][other[1]] = jnp.where(place[4] == 0, high, low)
        mine[0][mine[1]] = jnp.where(place[4] == 0, low, high)

    def z_step(half):
        for owner in range(4):
            piece = 2 * owner + half
            other = (z_send, piece) if piece < 4 else (z_next, piece - 4)
            put(owner, other, (z_mine, piece))

    def x_step(half):
        far, right, left = (
            ((send_r, 0), (keep_r, 0), (send_l, 2)),
            ((send_l, 0), (send_r, 2), (keep_l, 0)),
        )[half]
        for owner, (ref, piece) in enumerate((far, right, left)):
            put(owner, (ref, piece), (ref, piece + 1))
        put(3, (x_other, half), (x_mine, half))

    for i in range(4):
        pl.when(pl.program_id(0) == i)(
            functools.partial(z_step if i < 2 else x_step, i % 2)
        )


def query_second_sum_kernel(
    dep_r, dep_l, got_r, got_l, z_got, z_next, z_mine, x_other, out_r, out_l, out_x
):
    out_r[0] = z_mine[2] + z_got[2] + dep_r[2]
    out_r[1] = z_mine[3] + z_got[3]
    out_l[0] = z_mine[4] + z_next[0]
    out_l[1] = z_mine[5] + z_next[1] + dep_l[2]
    out_x[0] = x_other[0] + (dep_r[0] + got_l[2])
    out_x[1] = x_other[1] + (got_r[2] + dep_l[0])


def query_beside_kernel(dep_r, dep_l, got_r, got_l, z_next, z_mine, x_mine, out):
    out[0] = z_mine[6] + z_next[2]
    out[1] = z_mine[7] + z_next[3]
    out[2] = x_mine[0] + (dep_r[1] + got_l[3])
    out[3] = x_mine[1] + (got_r[3] + dep_l[1])


def reduce_kv(halves, place, activations, weight, beside):
    make = functools.partial(
        project, halves=halves, place=place, activations=activations, weight=weight
    )
    send_r, send_l, z_send, z_mine = make(
        first_kernel, owner=0, steps=2, outs=[(2, "vmem")] * 4
    )
    got_r, got_l, z_got = shift_x(send_r, 1), shift_x(send_l, -1), swap_z(z_send)
    next_r, next_l, z_send = make(
        second_kernel, owner=1, steps=5, outs=[(5, "vmem")] * 3, after=(z_mine,)
    )
    next_r, next_l = sum_call(
        kv_first_sum_kernel, halves, [5, 5], [got_r, got_l, z_got, next_r, next_l, z_mine], []
    )
    ready = beside(next_r)
    (mine,) = make(
        third_kernel,
        owner=1,
        steps=6,
        outs=[(11, "vmem")],
        after=(next_r,) + ready[1:],
    )
    next_r, next_l, z_five = shift_x(next_r, 1), shift_x(next_l, -1), swap_z(z_send)
    (last_xz,) = piece_call(
        kv_other_kernel,
        halves,
        [3],
        [(mine, 7), (mine, 8), (next_r, 2), (next_r, 0), (next_l, 0), (next_l, 2), (mine, 6)],
        after=(z_five,) + ready,
    )
    last_r, last_l = piece_call(
        kv_last_kernel,
        halves,
        [2, 2],
        [(mine, i) for i in range(4)]
        + [(z_five, i) for i in range(4)]
        + [(next_r, 4), (next_l, 4)],
        after=(last_xz,),
    )
    (part,) = piece_call(
        kv_beside_kernel,
        halves,
        [4],
        [(mine, 4), (mine, 5), (z_five, 4), (mine, 9), (mine, 10)]
        + [(next_r, 3), (next_r, 1), (next_l, 1), (next_l, 3)],
        after=(last_r,),
    )
    last_r, last_l, last_xz = shift_x(last_r, 1), shift_x(last_l, -1), swap_z(last_xz)
    return (part, last_r, last_l, last_xz), part


def project_query(halves, place, activations, weight, after):
    features, columns = weight.shape[1:]
    shapes = [halves.shape(count) for count in (4, 4, 2, 2, 4, 4, 8, 2, 2)]
    return pl.pallas_call(
        query_project_kernel,
        grid_spec=pltpu.PrefetchScalarGridSpec(
            num_scalar_prefetch=1,
            grid=(4,),
            in_specs=[
                pl.BlockSpec((halves.rows, features), lambda i, at: (i, 0)),
                pl.BlockSpec((1, features, columns), lambda i, at: (0, 0, 0)),
                pl.BlockSpec(memory_space=pl.ANY),
            ],
            out_specs=[pl.BlockSpec(shape, lambda i, at: (0, 0, 0)) for shape in shapes],
            scratch_shapes=[pltpu.VMEM((halves.rows, columns), jnp.float32)],
        ),
        out_shape=[pltpu.HBM(shape, jnp.float32) for shape in shapes],
        compiler_params=params(24),
        name="query_project_kernel",
    )(place, activations, weight, after)


def reduce_query(halves, projected, after):
    send_r, send_l, keep_r, keep_l, z_send, z_next, z_mine, x_other, x_mine = projected
    send_r, send_l, z_send, z_next = release((send_r, send_l, z_send, z_next), after)
    got_r, got_l, z_got = shift_x(send_r, 1), shift_x(send_l, -1), swap_z(z_send)
    z_next = swap_z(z_next)
    dep_r, dep_l = sum_call(
        first_sum_kernel,
        halves,
        [3, 3],
        [got_r, got_l, z_got],
        [keep_r, keep_l, z_mine],
    )
    dep_r, dep_l = shift_x(dep_r, 1), shift_x(dep_l, -1)
    last_r, last_l, x_sum = sum_call(
        query_second_sum_kernel,
        halves,
        [2, 2, 2],
        [dep_r, dep_l, got_r, got_l, z_got, z_next],
        [z_mine, x_other],
    )
    (part,) = sum_call(
        query_beside_kernel,
        halves,
        [4],
        [dep_r, dep_l, got_r, got_l, z_next],
        [z_mine, x_mine],
        after=(last_r,),
    )
    last_r, last_l, x_sum = shift_x(last_r, 1), shift_x(last_l, -1), swap_z(x_sum)
    return part, last_r, last_l, x_sum


def summed(part, last_r, last_l, last_x):
    z_total = [part[h] + (last_r[h] + last_l[h]) for h in range(2)]
    if last_x.shape[0] == 3:
        z_total[1] = z_total[1] + last_x[2]
    return z_total + [part[2 + h] + last_x[h] for h in range(2)]


def split_bf16(table):
    high = table.astype(np.float32).astype(ml_dtypes.bfloat16)
    low = (table - high.astype(np.float64)).astype(ml_dtypes.bfloat16)
    return high, low


@functools.lru_cache(None)
def tables(length):
    rows = length // BLOCK
    period = 2 * length
    odd = np.arange(rows) + 0.5
    first = -2 * np.pi * np.outer(odd, np.arange(rows)) / (2 * rows)
    turn = -2 * np.pi * np.outer(odd, np.arange(BLOCK)) / period
    second = -2 * np.pi * (np.outer(np.arange(BLOCK), np.arange(BLOCK)) % BLOCK) / BLOCK
    c, s = np.cos(second), np.sin(second)
    scale = 1.0 / length
    return (
        split_bf16(np.concatenate([np.cos(first), np.sin(first)], axis=0)),
        (np.cos(turn).astype(np.float32), np.sin(turn).astype(np.float32)),
        split_bf16(np.block([[c, s], [-s, c]])),
        split_bf16(np.block([[c, -s], [s, c]])),
        split_bf16(np.concatenate([np.cos(first).T, np.sin(first).T], axis=1) * scale),
    )


def split_value(value):
    high = value.astype(jnp.bfloat16)
    return high, (value - high.astype(jnp.float32)).astype(jnp.bfloat16)


def dot3(left, right):
    dot = functools.partial(jnp.dot, preferred_element_type=jnp.float32)
    return dot(left[0], right[0]) + (dot(left[0], right[1]) + dot(left[1], right[0]))


def forward(signal_ref, first, turn, second):
    seqs, channels = signal_ref.shape[:2]
    rows = seqs * signal_ref.shape[2]
    signal = jnp.concatenate(
        [signal_ref[:, c].reshape(rows, BLOCK) for c in range(channels)], axis=1
    )
    part = dot3(first, split_value(signal))
    turned = []
    for c in range(channels):
        real = part[:rows, c * BLOCK : (c + 1) * BLOCK]
        imag = part[rows:, c * BLOCK : (c + 1) * BLOCK]
        turned.append(
            jnp.concatenate(
                [real * turn[0] - imag * turn[1], real * turn[1] + imag * turn[0]], axis=1
            )
        )
    return dot3(split_value(jnp.concatenate(turned, axis=0)), second)


def taps_kernel(taps_ref, f_hi, f_lo, t_re, t_im, s_hi, s_lo, out_ref):
    out_ref[...] = forward(
        taps_ref, (f_hi[...], f_lo[...]), (t_re[...], t_im[...]), (s_hi[...], s_lo[...])
    )


def conv_kernel(
    kv_ref, spec_ref, f_hi, f_lo, t_re, t_im, s_hi, s_lo, b_hi, b_lo, i_hi, i_lo, out_ref
):
    seqs, channels, blocks, _ = kv_ref.shape
    rows = seqs * blocks
    turn = (t_re[...], t_im[...])
    spectrum = forward(kv_ref, (f_hi[...], f_lo[...]), turn, (s_hi[...], s_lo[...]))
    real, imag = spectrum[:, :BLOCK], spectrum[:, BLOCK:]
    taps_real, taps_imag = spec_ref[:, :BLOCK], spec_ref[:, BLOCK:]
    product = jnp.concatenate(
        [real * taps_real - imag * taps_imag, real * taps_imag + imag * taps_real], axis=1
    )
    back = dot3(split_value(product), (b_hi[...], b_lo[...]))
    columns = []
    for c in range(channels):
        real = back[c * rows : (c + 1) * rows, :BLOCK]
        imag = back[c * rows : (c + 1) * rows, BLOCK:]
        columns.append(
            jnp.concatenate(
                [real * turn[0] + imag * turn[1], imag * turn[0] - real * turn[1]], axis=0
            )
        )
    result = dot3((i_hi[...], i_lo[...]), split_value(jnp.concatenate(columns, axis=1)))
    for c in range(channels):
        out_ref[:, c] = result[:, c * BLOCK : (c + 1) * BLOCK].reshape(seqs, blocks, BLOCK)


def turn_blocks(value_ref, out_ref):
    for b in range(out_ref.shape[1]):
        out_ref[:, b, :] = value_ref[b * BLOCK : (b + 1) * BLOCK, :].T


def taps_turn_kernel(taps_ref, out_ref):
    turn_blocks(taps_ref, out_ref)


def kv_kernel(*refs):
    parts, out_ref, kv_ref = refs[:-2], refs[-2], refs[-1]
    z_key, z_value, x_key, x_value = summed(*parts)
    rows = z_key.shape[0]
    kv_ref[:rows] = z_key * z_value
    kv_ref[rows:] = x_key * x_value
    turn_blocks(kv_ref, out_ref)


def query_kernel(*refs):
    parts, out_ref = refs[:-1], refs[-1]
    for i, query in enumerate(summed(*parts)):
        rows = query.shape[0]
        out_ref[i * rows : (i + 1) * rows] = query


def gate_kernel(conv_ref, query_ref, out_ref):
    for b in range(conv_ref.shape[1]):
        rows = slice(b * BLOCK, (b + 1) * BLOCK)
        out_ref[rows] = conv_ref[:, b, :].T * query_ref[rows]


def call(kernel, out_shape, *operands, after=(), scratch=(), tables=(), to_hbm=False):
    def body(*refs):
        count = len(operands) + len(tables)
        kernel(*refs[:count], *refs[count + len(after) :])

    def whole(shape):
        return pl.BlockSpec(shape, lambda i: (0,) * len(shape))

    return pl.pallas_call(
        body,
        grid=(1,),
        in_specs=[pl.BlockSpec(memory_space=pltpu.VMEM)] * len(operands)
        + [whole(table.shape) for table in tables]
        + [pl.BlockSpec(memory_space=pl.ANY)] * len(after),
        out_specs=whole(out_shape) if to_hbm else pl.BlockSpec(memory_space=pltpu.VMEM),
        out_shape=pltpu.HBM(out_shape, jnp.float32)
        if to_hbm
        else jax.ShapeDtypeStruct(out_shape, jnp.float32),
        scratch_shapes=scratch,
        compiler_params=params(24),
        name=kernel.__name__,
    )(*operands, *[in_hbm(jnp.asarray(table)) for table in tables], *after)


def exchange(value):
    return lax.all_to_all(value, "seq", split_axis=0, concat_axis=0, tiled=True)


def on_device(activations, proj_weight, filter_taps):
    tokens, channels = filter_taps.shape
    seqs = lax.axis_size("seq")
    length = tokens * seqs
    blocks = tokens // BLOCK
    owned = channels // seqs
    turned_shape = (channels, blocks, BLOCK)
    moved_shape = (seqs, owned, blocks, BLOCK)
    first, turn, second, back, inverse = tables(length)

    chan = lax.axis_index("chan")
    x_at, z_at = chan // 2, chan % 2
    owners = [(x_at + dx) % X_SIZE for dx in (2, 1, 3, 0)]
    place = jnp.stack(owners + [z_at]).astype(jnp.int32)
    weight = in_hbm(jnp.transpose(proj_weight, (1, 0, 2)))
    activations = in_hbm(activations)

    hold = {}
    kv_halves, q_halves = Halves(tokens, (1, 2)), Halves(tokens, (0,))

    def prepare(ready):
        taps = call(taps_turn_kernel, turned_shape, filter_taps, after=(ready,), to_hbm=True)
        hold["taps"] = exchange(taps.reshape(moved_shape))
        hold["query"] = project_query(q_halves, place, activations, weight, ready)
        return hold["taps"], hold["query"][0]

    kv_parts, kv_part = reduce_kv(kv_halves, place, activations, weight, prepare)
    spectrum = call(
        taps_kernel,
        (owned * length // BLOCK, 2 * BLOCK),
        hold["taps"],
        tables=first + turn + second,
        after=(kv_part,),
        to_hbm=True,
    )
    kv = call(
        kv_kernel,
        turned_shape,
        *kv_parts,
        after=(spectrum,),
        scratch=[pltpu.VMEM((tokens, channels), jnp.float32)],
        to_hbm=True,
    )
    q_parts = reduce_query(q_halves, hold["query"], spectrum)
    moved = exchange(kv.reshape(moved_shape))
    convolved = call(
        conv_kernel,
        moved_shape,
        moved,
        tables=(spectrum,) + first + turn + second + back + inverse,
        to_hbm=True,
    )
    query = call(query_kernel, (tokens, channels), *q_parts)
    home = exchange(convolved).reshape(turned_shape)
    return call(gate_kernel, (tokens, channels), home, query)


def solution(mesh):
    return jax.shard_map(
        on_device,
        mesh=mesh,
        in_specs=(P("seq", "chan"), P("chan", None, None), P("seq", "chan")),
        out_specs=P("seq", "chan"),
        check_vma=False,
    )
```
